256 devices in a mesh: row: 32 (over z, x), col: 8 (over y, core).
Axes of the slice: x: 4, y: 4, z: 8, core: 2. Of those that a mesh axis runs over, the one named last changes fastest.
Arguments:
- density: float32 [3, 4194304], P(None, ('row', 'col')), may hold values from -6 to 6
- interp_weight: float32 [27, 4194304], P(None, ('row', 'col')), may hold values from -1.2 to 1.2
- proj_weight: float32 [27, 4194304], P(None, ('row', 'col')), may hold values from -1.2 to 1.2
- stencil_corner: int32 [3, 32768], P(None, ('row', 'col')), may hold values from 0 to 253, as said below
- near_tiles: bfloat16 [3072, 3, 3, 128, 128], P(('row', 'col')), may hold values from -0.1875 to 0.1875
- pair_target: int32 [3072], P(('row', 'col')), may hold values from 0 to 127
- pair_landing: int32 [3072], P(('row', 'col')), may hold values from 0 to 127
- pair_count: int32 [256], P(('row', 'col')), may hold values from 4 to 12, as said below
Outputs:
- traction_adjoint: float32 [3, 4194304], P(None, ('row', 'col'))
The draws below stay inside these ranges and needn't reach their ends.
Inputs may be any that keep to these rules, and one draw needn't show every extreme that they name: `stencil_corner`: the stencil of a cluster held by the device with row index r and col index c lies in cells r * 8 to r * 8 + 7 of the first dimension and c * 32 to c * 32 + 31 of the second; every stencil lies inside the grid. `pair_count`: slots at or beyond a device's count are padding; the most is reached on some device in every draw.
All inputs are finite; a program needn't handle non-finite values.
Results may differ from the reference program's by a relative error of at most 0.0003.
Values sent between devices are 32-bit elements; how exact they have to be, the bound alone decides.
A program may use at most 128 MiB of HBM per device.

```python
import math
import jax
import jax.numpy as jnp
from jax import lax

G = 256
PC = 128
STENCIL = 27
CL_DEV = 128
PAIR_GROUP = 4
CLUSTERS = 32768
PANELS = 4194304
PAIRS = 3072
N_ROW = 32
N_COL = 8
DEVICES = 256


def pair_tables(key):
    base_key = jax.random.fold_in(key, 11)
    subkeys = jax.random.split(base_key, 4)
    slot_count = 3 * PAIR_GROUP
    target = jax.random.randint(subkeys[0], (DEVICES, slot_count), 0, CL_DEV)
    landing = jax.random.randint(subkeys[1], (DEVICES, slot_count), 0, CL_DEV)
    count_draws = jax.random.randint(subkeys[2], (2, DEVICES), 0, 2 * PAIR_GROUP + 1)
    counts = PAIR_GROUP + jnp.min(count_draws, axis=0)
    chosen = jax.random.randint(subkeys[3], (), 0, DEVICES)
    counts = counts.at[chosen].set(3 * PAIR_GROUP).astype(jnp.int32)
    return (target.reshape(-1).astype(jnp.int32), landing.reshape(-1).astype(jnp.int32), counts)


def draw_pair_target(key, part):
    return pair_tables(key)[0]


def draw_pair_landing(key, part):
    return pair_tables(key)[1]


def draw_pair_count(key, part):
    return pair_tables(key)[2]


def draw_stencil_corner(key, part):
    base_key = jax.random.fold_in(key, 5)
    key_first, key_second, key_third = jax.random.split(base_key, 3)
    holder = jnp.arange(CLUSTERS, dtype=jnp.int32) // CL_DEV
    row_of = holder // N_COL
    col_of = holder % N_COL
    slab_first = G // N_ROW
    slab_second = G // N_COL
    first_corner = row_of * slab_first + jax.random.randint(key_first, (CLUSTERS,), 0, slab_first - 2)
    second_corner = col_of * slab_second + jax.random.randint(key_second, (CLUSTERS,), 0, slab_second - 2)
    third_corner = jax.random.randint(key_third, (CLUSTERS,), 0, G - 2)
    return jnp.stack([first_corner, second_corner, third_corner]).astype(jnp.int32)


def levels(key, shape, cuts, smallest, high):
    def one(axis_at, blocks):
        steps = jax.random.uniform(jax.random.fold_in(jax.random.fold_in(key, 6), axis_at), (blocks,), jnp.float32, smallest / len(cuts), high / len(cuts))
        return jnp.repeat(jnp.exp(steps), shape[axis_at] // blocks).reshape((-1,) + (1,) * (len(shape) - axis_at - 1))

    gain = one(*cuts[0])
    for cut in cuts[1:]:
        gain = gain * one(*cut)
    return gain


def centred(stream_key, dims, scale, reach, cuts=(), held_as=jnp.bfloat16):
    values = scale * jax.random.normal(stream_key, dims, jnp.float32)
    if cuts:
        values = values * levels(stream_key, dims, cuts, -0.22, 0.18)
    return jnp.clip(values, -reach, reach).astype(held_as)


def setup_inputs(seed: int = 0) -> dict:
    seeds = jax.random.split(jax.random.key(seed), 9)
    return {
        "density": centred(seeds[0], (3, PANELS), 1.0, 6.0, ((1, 256),), jnp.float32),
        "interp_weight": centred(seeds[1], (STENCIL, PANELS), 0.19245, 1.2, ((1, 256),), jnp.float32),
        "proj_weight": centred(seeds[2], (STENCIL, PANELS), 0.19245, 1.2, ((1, 256),), jnp.float32),
        "stencil_corner": draw_stencil_corner(jax.random.fold_in(seeds[8], 71), 0),
        "near_tiles": centred(seeds[4], (PAIRS, 3, 3, PC, PC), (9 * PC) ** -0.5, 0.1875, ((0, 256),)),
        "pair_target": draw_pair_target(jax.random.fold_in(seeds[8], 71), 0),
        "pair_landing": draw_pair_landing(jax.random.fold_in(seeds[8], 71), 0),
        "pair_count": draw_pair_count(jax.random.fold_in(seeds[8], 71), 0),
    }


precise = lax.Precision.HIGHEST
screen_shift = 0.5

def wavenumbers(count, offset, length):
    indices = offset + jnp.arange(count, dtype=jnp.int32)
    wave_values = jnp.where(indices < length // 2, indices, indices - length).astype(jnp.float32)
    keep_mask = (indices != length // 2).astype(jnp.float32)
    return (wave_values, keep_mask)

def screen_project(spectra, first_pair, second_pair, third_pair, factor):
    kfirst, keep_first = first_pair
    ksecond, keep_second = second_pair
    kthird, keep_third = third_pair
    squared = kfirst * kfirst + ksecond * ksecond + kthird * kthird
    weighting = factor * keep_first * keep_second * keep_third / (squared + screen_shift)
    floor_sq = jnp.maximum(squared, 1.0)
    result = []
    for spectral in spectra:
        inner_sum = (kfirst * spectral[0] + ksecond * spectral[1] + kthird * spectral[2]) / floor_sq
        stacked = jnp.stack([spectral[0] - kfirst * inner_sum, spectral[1] - ksecond * inner_sum, spectral[2] - kthird * inner_sum])
        result.append(stacked * weighting)
    return result

def reference(density, interp_weight, proj_weight, stencil_corner, near_tiles, pair_target, pair_landing, pair_count):
    charges = density.reshape(3, CLUSTERS, PC)
    weights_in = interp_weight.reshape(STENCIL, CLUSTERS, PC)
    weights_out = proj_weight.reshape(STENCIL, CLUSTERS, PC)
    offsets = jnp.arange(STENCIL, dtype=jnp.int32)
    cell_index = ((stencil_corner[0][:, None] + offsets // 9) * G + stencil_corner[1][:, None] + offsets // 3 % 3) * G + stencil_corner[2][:, None] + offsets % 3
    cell_index = cell_index.astype(jnp.int32)
    spread = jnp.einsum('ckp,skp->cks', charges, weights_in, precision=precise)
    charge_grid = jnp.zeros((3, G * G * G), jnp.float32).at[:, cell_index.reshape(-1)].add(spread.reshape(3, -1)).reshape(3, G, G, G)
    spectrum = jnp.fft.fftn(charge_grid, axes=(1, 2, 3))
    wave_pair = wavenumbers(G, 0, G)
    first_pair = tuple((member[:, None, None] for member in wave_pair))
    second_pair = tuple((member[None, :, None] for member in wave_pair))
    third_pair = tuple((member[None, None, :] for member in wave_pair))
    factor = 1.0 / math.sqrt(PANELS)
    real_part, imag_part = screen_project((jnp.real(spectrum), jnp.imag(spectrum)), first_pair, second_pair, third_pair, factor)
    potential = jnp.real(jnp.fft.ifftn(lax.complex(real_part, imag_part), axes=(1, 2, 3))) * float(G ** 3)
    sampled = potential.reshape(3, -1)[:, cell_index]
    far_term = jnp.einsum('cks,skp->ckp', sampled, weights_out, precision=precise)
    rounded = charges.astype(jnp.bfloat16).astype(jnp.float32)
    per_device = 3 * PAIR_GROUP
    tiles_by_dev = near_tiles.reshape(DEVICES, per_device, 3, 3, PC, PC)
    target_by_dev = pair_target.reshape(DEVICES, per_device)
    landing_by_dev = pair_landing.reshape(DEVICES, per_device)
    position = jnp.arange(per_device, dtype=jnp.int32)
    shift_code = jnp.where(position < PAIR_GROUP, 0, jnp.where((position - PAIR_GROUP) % 2 == 0, -1, 1)).astype(jnp.int32)

    def visit_device(near_total, device):
        block_tiles = lax.dynamic_index_in_dim(tiles_by_dev, device, keepdims=False).astype(jnp.float32)
        targets = (device * CL_DEV + lax.dynamic_index_in_dim(target_by_dev, device, keepdims=False)).astype(jnp.int32)
        picked = rounded[:, targets, :]
        partial_value = jnp.einsum('qabij,aqi->qbj', block_tiles, picked, precision=precise)
        live_mask = position < pair_count[device]
        row_of = device // N_COL
        col_of = device % N_COL
        holder = ((row_of + shift_code) % N_ROW * N_COL + col_of).astype(jnp.int32)
        sources = (holder * CL_DEV + landing_by_dev[holder, position]).astype(jnp.int32)
        masked = jnp.where(live_mask[:, None, None], partial_value, jnp.zeros_like(partial_value))
        near_total = near_total.at[:, sources, :].add(jnp.transpose(masked, (1, 0, 2)))
        return (near_total, None)
    near_term, unused = lax.scan(visit_device, jnp.zeros((3, CLUSTERS, PC), jnp.float32), jnp.arange(DEVICES, dtype=jnp.int32))
    return (far_term + near_term).reshape(3, PANELS)
```

```python
import math

import jax
import jax.numpy as jnp
import ml_dtypes
import numpy as np
from jax import lax
from jax.experimental import pallas as pl
from jax.experimental.pallas import tpu as pltpu
from jax.sharding import PartitionSpec as P

G = 256
STENCIL = 27
ROWS = 32
COLS = 8
CLUSTERS = 128
PANELS = 128
SLOTS = 12
BF16 = jnp.bfloat16
F32 = jnp.float32
MESH = pl.DeviceIdType.MESH
FACTOR = 1.0 / math.sqrt(ROWS * COLS * CLUSTERS * PANELS)


def halves(table):
    table = np.asarray(table, np.float64)
    high = table.astype(np.float32).astype(ml_dtypes.bfloat16)
    low = (table - high.astype(np.float64)).astype(np.float32).astype(ml_dtypes.bfloat16)
    return np.stack([high, low])


def rotation(theta):
    cosine, sine = np.cos(theta), np.sin(theta)
    return np.array([[cosine, sine], [-sine, cosine]])


def make_tables():
    two_pi = 2 * np.pi
    bins, cells = np.arange(128), np.arange(G)
    theta = two_pi * (bins[:, None] * cells[None, :] % G) / G
    line = np.stack([np.cos(theta), -np.sin(theta)]).reshape(2, COLS, 16, G)
    line = line.transpose(1, 0, 2, 3).reshape(G, G)
    eight = np.arange(8)
    wide = np.arange(32)
    turn8 = rotation(two_pi * (eight[:, None] * eight[None, :] % 8) / 8)
    turn32 = rotation(two_pi * (wide[:, None] * wide[None, :] % 32) / 32)
    second = np.einsum("oipc,hg,lm->phol" "cigm", turn8, np.eye(4), np.eye(4)).reshape(G, G)
    first = np.einsum("oipr,lm->polrim", turn32, np.eye(4)).reshape(G, G)
    lane32 = [np.kron(np.eye(8), f(two_pi * (wide[:, None] * wide[None, :] % 32) / 32)) for f in (np.cos, np.sin)]
    lane8 = [np.kron(f(two_pi * (eight[:, None] * eight[None, :] % 8) / 8), np.eye(32)) for f in (np.cos, np.sin)]
    row = np.arange(G)
    lane = np.arange(G)
    part_sign = np.where(row // 4 % 2 == 0, 1.0, -1.0)[:, None]
    twist_y = two_pi * ((row // 32)[:, None] * (lane % 32)[None, :]) / G
    twist_x = two_pi * ((row // 8)[:, None] * (lane // 32)[None, :]) / G
    twiddle = np.stack(
        [np.cos(twist_y), part_sign * np.sin(twist_y), np.cos(twist_x), part_sign * np.sin(twist_x)]
    ).astype(np.float32)
    rows_table = np.stack([halves(t) for t in (second, first, first.T, second.T)])
    lanes_table = np.stack([halves(np.concatenate(t, axis=1)) for t in (lane32, lane8)])
    return halves(line), rows_table, lanes_table, twiddle


def split(values):
    high = values.astype(BF16)
    return high, (values - high.astype(F32)).astype(BF16)


def mm(a, b):
    return jnp.dot(a, b, preferred_element_type=F32)


def mm_nt(a, b):
    return lax.dot_general(a, b, (((1,), (1,)), ((), ())), preferred_element_type=F32)


def swap(values):
    grouped = values.reshape(32, 8, values.shape[1])
    return pltpu.roll(grouped, 4, 1).reshape(values.shape)


def on_rows(table_high, table_low, values):
    high, low = split(values)
    return mm(table_high, high) + (mm(table_low, high) + mm(table_high, low))


def on_lanes(values, table_high, table_low, sign):
    high, low = split(values)
    both = mm(high, table_high) + (mm(low, table_high) + mm(high, table_low))
    return both[:, :G] + sign * swap(both[:, G:])


def signs(direction):
    row = lax.broadcasted_iota(jnp.int32, (G, G), 0)
    return jnp.where((row & 4) == 0, direction, -direction).astype(F32)


def forward(values, rows_high, rows_low, lanes_high, lanes_low, cosines, sines):
    values = on_rows(rows_high, rows_low, values)
    values = values * cosines + swap(values) * sines
    return on_lanes(values, lanes_high, lanes_low, signs(1.0))


def backward(values, rows_high, rows_low, lanes_high, lanes_low, cosines, sines):
    values = on_lanes(values, lanes_high, lanes_low, signs(-1.0))
    values = values * cosines - swap(values) * sines
    return on_rows(rows_high, rows_low, values)


def wave(index):
    return jnp.where(index < G // 2, index, index - G).astype(F32)


def wavevector(row_index, col_index):
    row = lax.broadcasted_iota(jnp.int32, (G, G), 0)
    lane = lax.broadcasted_iota(jnp.int32, (G, G), 1)
    m1 = (row >> 3) + (lane & -32)
    m2 = row_index // 4 + 8 * (lane & 31)
    m3 = 16 * col_index + 4 * (row_index % 4) + (row & 3)
    return m1, m2, m3


def screen(row_index, col_index):
    m1, m2, m3 = wavevector(row_index, col_index)
    w1, w2, w3 = wave(m1), wave(m2), m3.astype(F32)
    squared = w1 * w1 + w2 * w2 + w3 * w3
    kept = jnp.where((m1 == G // 2) | (m2 == G // 2), 0.0, FACTOR).astype(F32)
    fold = jnp.where(m3 == 0, 1.0, 2.0).astype(F32)
    return w1, w2, w3, 1.0 / jnp.maximum(squared, 1.0), kept * fold / (squared + 0.5)


def spread_kernel(density, weight, corner, line, target, count, grid, phases, hot, picked, upper, lower):
    row_index, col_index = lax.axis_index("row"), lax.axis_index("col")
    lane = lax.broadcasted_iota(jnp.int32, (STENCIL, CLUSTERS), 1)
    group = 8

    def gather_sums(i, sums):
        start = pl.multiple_of(i * group * PANELS, group * PANELS)
        block = weight[:, pl.ds(start, group * PANELS)]
        charge = density[:, pl.ds(start, group * PANELS)]
        sums = list(sums)
        for c in range(3):
            product = block * charge[c : c + 1]
            for k in range(group):
                total = jnp.sum(product[:, k * PANELS : (k + 1) * PANELS], axis=1, keepdims=True)
                sums[c] = jnp.where(lane == i * group + k, total, sums[c])
        return tuple(sums)

    picked[...] = jnp.zeros_like(picked)
    live = count[0]
    for q in range(SLOTS):
        start = pl.multiple_of(target[q] * PANELS, PANELS)
        charge = density[:, pl.ds(start, PANELS)].astype(BF16).astype(F32)
        picked[q, 0:3] = jnp.where(q < live, charge, jnp.zeros_like(charge))

    zero = jnp.zeros((STENCIL, CLUSTERS), F32)
    sums = lax.fori_loop(0, CLUSTERS // group, gather_sums, (zero,) * 3)

    corners = corner[...]
    local = (corners[0:1] - row_index * 8) * 32 + (corners[1:2] - col_index * 32)
    cell = lax.broadcasted_iota(jnp.int32, (G, CLUSTERS), 0)
    for dz in range(3):
        at = jnp.where(cell == corners[2:3] + dz, 1.0, 0.0).astype(BF16)
        phases[dz] = mm(line[0], at) + mm(line[1], at)
    for d in range(9):
        here = jnp.where(cell == local + (d // 3 * 32 + d % 3), 1.0, 0.0).astype(BF16)
        hot[:, d * CLUSTERS : (d + 1) * CLUSTERS] = here
    for c in range(3):
        for d in range(9):
            value = phases[0] * sums[c][3 * d : 3 * d + 1]
            value += phases[1] * sums[c][3 * d + 1 : 3 * d + 2]
            value += phases[2] * sums[c][3 * d + 2 : 3 * d + 3]
            high, low = split(value)
            upper[:, d * CLUSTERS : (d + 1) * CLUSTERS] = high
            lower[:, d * CLUSTERS : (d + 1) * CLUSTERS] = low
        total = mm_nt(upper[...], hot[...]) + mm_nt(lower[...], hot[...])
        grid[c] = total.reshape(COLS, 32, G)


def exchange_kernel(
    sent1, rows_table, lanes_table, twiddle, picked, tiles,
    got4, near_here, near_got,
    got1, sent2, got2, modes, sent3, got3, sent4, near_sent, blocks,
    send_sem, recv_sem, near_sem, tile_sem,
):
    row_index, col_index = lax.axis_index("row"), lax.axis_index("col")
    tile_copy = pltpu.make_async_copy(tiles, blocks, tile_sem)
    tile_copy.start()

    barrier = pltpu.get_barrier_semaphore()

    def row_peer(j):
        return lax.rem(row_index + j, ROWS)

    def col_peer(j):
        return lax.rem(col_index + j, COLS)

    def greet_row(j, carry):
        pl.semaphore_signal(barrier, inc=1, device_id=(row_peer(j), col_index), device_id_type=MESH)
        return carry

    def greet_col(j, carry):
        pl.semaphore_signal(barrier, inc=1, device_id=(row_index, col_peer(j)), device_id_type=MESH)
        return carry

    lax.fori_loop(1, COLS, greet_col, 0)
    lax.fori_loop(1, ROWS, greet_row, 0)
    pl.semaphore_wait(barrier, COLS + ROWS - 2)

    def to_cols(stage, source, target_ref, c):
        def one(j, carry):
            peer = col_peer(j)
            pltpu.make_async_remote_copy(
                source.at[c, peer],
                target_ref.at[c, col_index],
                send_sem.at[stage, c],
                recv_sem.at[stage, c],
                device_id=(row_index, peer),
                device_id_type=MESH,
            ).start()
            return carry

        lax.fori_loop(1, COLS, one, 0)
        target_ref[c, col_index] = source[c, col_index]

    def to_rows(stage, source, target_ref, c):
        def one(j, carry):
            peer = row_peer(j)
            pltpu.make_async_remote_copy(
                source.at[c, peer],
                target_ref.at[c, row_index],
                send_sem.at[stage, c],
                recv_sem.at[stage, c],
                device_id=(peer, col_index),
                device_id_type=MESH,
            ).start()
            return carry

        lax.fori_loop(1, ROWS, one, 0)
        target_ref[c, row_index] = source[c, row_index]

    def whole(stage, source, target_ref, c):
        peers = source.shape[1] - 1
        return pltpu.make_async_remote_copy(
            source.at[c, pl.ds(0, peers)],
            target_ref.at[c, pl.ds(0, peers)],
            send_sem.at[stage, c],
            recv_sem.at[stage, c],
            device_id=(row_peer(1), col_index),
            device_id_type=MESH,
        )

    def rows_of(k):
        return rows_table[k, 0], rows_table[k, 1]

    def lanes_of(k):
        return lanes_table[k, 0], lanes_table[k, 1]

    def start1(c, carry):
        to_cols(0, sent1, got1, c)
        return carry

    lax.fori_loop(0, 3, start1, 0)

    def second_dimension(c, carry):
        whole(0, sent1, got1, c).wait_recv()
        values = forward(got1[c].reshape(G, G), *rows_of(0), *lanes_of(0), twiddle[0], twiddle[1])
        sent2[c] = values.reshape(ROWS, 8, G)
        to_rows(1, sent2, got2, c)
        return carry

    lax.fori_loop(0, 3, second_dimension, 0)

    tile_copy.wait()

    near_sent[...] = jnp.zeros_like(near_sent)

    def slot(q, carry):
        charge = picked[q].astype(BF16)
        for b in range(3):
            total = mm(charge[0:1], blocks[q, 0, b])
            total += mm(charge[1:2], blocks[q, 1, b])
            total += mm(charge[2:3], blocks[q, 2, b])
            near_sent[q, b : b + 1] = total
        return carry

    lax.fori_loop(0, SLOTS, slot, 0)
    near_here[...] = near_sent[0:4]
    near_copies = []
    for side, peer in ((0, row_peer(ROWS - 1)), (1, row_peer(1))):
        for k in range(4):
            near_copies.append(
                pltpu.make_async_remote_copy(
                    near_sent.at[4 + 2 * k + side],
                    near_got.at[2 * k + side],
                    near_sem.at[0, 2 * k + side],
                    near_sem.at[1, 2 * k + side],
                    device_id=(peer, col_index),
                    device_id_type=MESH,
                )
            )
    for copy in near_copies:
        copy.start()

    w1, w2, w3, inverse, weighting = screen(row_index, col_index)

    def first_dimension(c, carry):
        whole(1, sent2, got2, c).wait_recv()
        modes[c] = forward(got2[c].reshape(G, G), *rows_of(1), *lanes_of(1), twiddle[2], twiddle[3])
        return carry

    lax.fori_loop(0, 3, first_dimension, 0)

    inner = (w1 * modes[0] + w2 * modes[1] + w3 * modes[2]) * inverse
    for c, w in enumerate((w1, w2, w3)):
        modes[c] = (modes[c] - w * inner) * weighting

    def first_back(c, carry):
        values = backward(modes[c], *rows_of(2), *lanes_of(1), twiddle[2], twiddle[3])
        sent3[c] = values.reshape(ROWS, 8, G)
        to_rows(2, sent3, got3, c)
        return carry

    lax.fori_loop(0, 3, first_back, 0)

    def second_back(c, carry):
        whole(2, sent3, got3, c).wait_recv()
        values = backward(got3[c].reshape(G, G), *rows_of(3), *lanes_of(0), twiddle[0], twiddle[1])
        sent4[c] = values.reshape(COLS, 32, G)
        to_cols(3, sent4, got4, c)
        return carry

    lax.fori_loop(0, 3, second_back, 0)

    for copy in near_copies:
        copy.wait()

    def finish(c, carry):
        whole(3, sent4, got4, c).wait()
        whole(0, sent1, got1, c).wait_send()
        whole(1, sent2, got2, c).wait_send()
        whole(2, sent3, got3, c).wait_send()
        return carry

    lax.fori_loop(0, 3, finish, 0)


def project_kernel(got4, phases, hot, weight, near_here, near_got, landing, out, mixed, values):
    values[...] = jnp.zeros_like(values)
    for c in range(3):
        high, low = split(got4[c].reshape(G, G))
        mixed[...] = mm(high, hot[...]) + mm(low, hot[...])
        for d in range(9):
            part = mixed[:, d * CLUSTERS : (d + 1) * CLUSTERS]
            for dz in range(3):
                values[c, 3 * d + dz : 3 * d + dz + 1] = jnp.sum(part * phases[dz], axis=0, keepdims=True)
    group = 8

    def clusters(i, carry):
        start = pl.multiple_of(i * group * PANELS, group * PANELS)
        block = weight[:, pl.ds(start, group * PANELS)]
        shift = lax.rem(CLUSTERS - i * group, CLUSTERS)
        for c in range(3):
            turned = pltpu.roll(values[c], shift, 1)
            for k in range(group):
                product = block[:, k * PANELS : (k + 1) * PANELS] * turned[:STENCIL, k : k + 1]
                place = pl.multiple_of(start + k * PANELS, PANELS)
                out[c : c + 1, pl.ds(place, PANELS)] = jnp.sum(product, axis=0, keepdims=True)
        return carry

    lax.fori_loop(0, CLUSTERS // group, clusters, 0)
    for q in range(SLOTS):
        place = pl.multiple_of(landing[q] * PANELS, PANELS)
        arrived = near_here[q] if q < 4 else near_got[q - 4]
        out[:, pl.ds(place, PANELS)] += arrived[:3]


VMEM = pl.BlockSpec(memory_space=pltpu.VMEM)
SMEM = pl.BlockSpec(memory_space=pltpu.SMEM)
ANY = pl.BlockSpec(memory_space=pl.ANY)
LIMIT = 48 * 1024 * 1024


def shape(dims, dtype=F32):
    return jax.ShapeDtypeStruct(dims, dtype)


def per_device(
    density, interp_weight, proj_weight, stencil_corner, near_tiles, pair_target, pair_landing, pair_count
):
    line, rows_table, lanes_table, twiddle = (jnp.asarray(t) for t in make_tables())
    by_cols, by_rows = (3, COLS, 32, G), (3, ROWS, 8, G)
    grid, phases, hot, picked = pl.pallas_call(
        spread_kernel,
        out_shape=(shape(by_cols), shape((3, G, CLUSTERS)), shape((G, 9 * CLUSTERS), BF16), shape((SLOTS, 8, PANELS))),
        in_specs=[VMEM] * 4 + [SMEM] * 2,
        out_specs=(VMEM,) * 4,
        scratch_shapes=[pltpu.VMEM((G, 9 * CLUSTERS), BF16)] * 2,
        compiler_params=pltpu.CompilerParams(vmem_limit_bytes=LIMIT),
    )(density, interp_weight, stencil_corner, line, pair_target, pair_count)
    got4, near_here, near_got = pl.pallas_call(
        exchange_kernel,
        out_shape=(shape(by_cols), shape((4, 8, PANELS)), shape((8, 8, PANELS))),
        in_specs=[VMEM] * 5 + [ANY],
        out_specs=(VMEM, VMEM, VMEM),
        scratch_shapes=[
            pltpu.VMEM(by_cols, F32),
            pltpu.VMEM(by_rows, F32),
            pltpu.VMEM(by_rows, F32),
            pltpu.VMEM((3, G, G), F32),
            pltpu.VMEM(by_rows, F32),
            pltpu.VMEM(by_rows, F32),
            pltpu.VMEM(by_cols, F32),
            pltpu.VMEM((SLOTS, 8, PANELS), F32),
            pltpu.VMEM((SLOTS, 3, 3, PANELS, PANELS), BF16),
            pltpu.SemaphoreType.DMA((4, 3)),
            pltpu.SemaphoreType.DMA((4, 3)),
            pltpu.SemaphoreType.DMA((2, 8)),
            pltpu.SemaphoreType.DMA,
        ],
        compiler_params=pltpu.CompilerParams(
            vmem_limit_bytes=LIMIT, collective_id=0, has_side_effects=True
        ),
    )(grid, rows_table, lanes_table, twiddle, picked, near_tiles)
    return pl.pallas_call(
        project_kernel,
        out_shape=shape((3, CLUSTERS * PANELS)),
        in_specs=[VMEM] * 6 + [SMEM],
        out_specs=VMEM,
        scratch_shapes=[pltpu.VMEM((G, 9 * CLUSTERS), F32), pltpu.VMEM((3, 32, CLUSTERS), F32)],
        compiler_params=pltpu.CompilerParams(vmem_limit_bytes=LIMIT),
    )(got4, phases, hot, proj_weight, near_here, near_got, pair_landing)


def solution(mesh):
    flat = P(None, ("row", "col"))
    slots = P(("row", "col"))
    in_specs = (flat, flat, flat, flat, P(("row", "col"), None, None, None, None), slots, slots, slots)
    return jax.shard_map(
        per_device, mesh=mesh, in_specs=in_specs, out_specs=flat, check_vma=False
    )
```

```python
import math

import jax
import jax.numpy as jnp
import ml_dtypes
import numpy as np
from jax import lax
from jax.experimental import pallas as pl
from jax.experimental.pallas import tpu as pltpu
from jax.sharding import PartitionSpec as P

G = 256
STENCIL = 27
ROWS = 32
COLS = 8
DEPTH = 8
WIDTH = 4
PACKED = 88
CLUSTERS = 128
PANELS = 128
SLOTS = 12
BF16 = jnp.bfloat16
F32 = jnp.float32
MESH = pl.DeviceIdType.MESH
FACTOR = 1.0 / math.sqrt(ROWS * COLS * CLUSTERS * PANELS)


def halves(table):
    table = np.asarray(table, np.float64)
    high = table.astype(np.float32).astype(ml_dtypes.bfloat16)
    low = (table - high.astype(np.float64)).astype(np.float32).astype(ml_dtypes.bfloat16)
    return np.stack([high, low])


def rotation(theta):
    cosine, sine = np.cos(theta), np.sin(theta)
    return np.array([[cosine, sine], [-sine, cosine]])


def make_tables():
    two_pi = 2 * np.pi
    bins, cells = np.arange(128), np.arange(G)
    theta = two_pi * (bins[:, None] * cells[None, :] % G) / G
    line = np.stack([np.cos(theta), -np.sin(theta)]).reshape(2, DEPTH, WIDTH, 4, G)
    line = line.transpose(1, 2, 0, 3, 4).reshape(DEPTH, 32, G)
    line = halves(line).transpose(1, 0, 2, 3).reshape(DEPTH, 64, G)
    eight = np.arange(8)
    wide = np.arange(32)
    turn8 = rotation(two_pi * (eight[:, None] * eight[None, :] % 8) / 8)
    turn32 = rotation(two_pi * (wide[:, None] * wide[None, :] % 32) / 32)
    second = np.einsum("oipc,hg,lm->pholcgim", turn8, np.eye(4), np.eye(4)).reshape(G, G)
    by_block = turn32.reshape(2, 2, 32, DEPTH, WIDTH)
    first = np.einsum("oipzx,lm->polxzim", by_block, np.eye(4)).reshape(G, G)
    lane32 = [np.kron(np.eye(8), f(two_pi * (wide[:, None] * wide[None, :] % 32) / 32)) for f in (np.cos, np.sin)]
    lane8 = [np.kron(f(two_pi * (eight[:, None] * eight[None, :] % 8) / 8), np.eye(32)) for f in (np.cos, np.sin)]
    row = np.arange(G)
    lane = np.arange(G)
    part_sign = np.where(row // 4 % 2 == 0, 1.0, -1.0)[:, None]
    twist_y = two_pi * ((row // 32)[:, None] * (lane % 32)[None, :]) / G
    twist_x = two_pi * ((row // 8)[:, None] * (lane // 32)[None, :]) / G
    twiddle = np.stack(
        [np.cos(twist_y), part_sign * np.sin(twist_y), np.cos(twist_x), part_sign * np.sin(twist_x)]
    ).astype(np.float32)
    rows_table = np.stack([halves(t) for t in (second, first, first.T, second.T)])
    lanes_table = np.stack([halves(np.concatenate(t, axis=1)) for t in (lane32, lane8)])
    return line, rows_table, lanes_table, twiddle


def split(values):
    high = values.astype(BF16)
    return high, (values - high.astype(F32)).astype(BF16)


def mm(a, b):
    return jnp.dot(a, b, preferred_element_type=F32)


def mm_nt(a, b):
    return lax.dot_general(a, b, (((1,), (1,)), ((), ())), preferred_element_type=F32)


def swap(values):
    grouped = values.reshape(32, 8, values.shape[1])
    return pltpu.roll(grouped, 4, 1).reshape(values.shape)


def on_rows(table_high, table_low, values):
    high, low = split(values)
    return mm(table_high, high) + (mm(table_low, high) + mm(table_high, low))


def on_lanes(values, table_high, table_low, sign):
    high, low = split(values)
    both = mm(high, table_high) + (mm(low, table_high) + mm(high, table_low))
    return both[:, :G] + sign * swap(both[:, G:])


def signs(direction):
    row = lax.broadcasted_iota(jnp.int32, (G, G), 0)
    return jnp.where((row & 4) == 0, direction, -direction).astype(F32)


def forward(values, rows_high, rows_low, lanes_high, lanes_low, cosines, sines):
    values = on_rows(rows_high, rows_low, values)
    values = values * cosines + swap(values) * sines
    return on_lanes(values, lanes_high, lanes_low, signs(1.0))


def backward(values, rows_high, rows_low, lanes_high, lanes_low, cosines, sines):
    values = on_lanes(values, lanes_high, lanes_low, signs(-1.0))
    values = values * cosines - swap(values) * sines
    return on_rows(rows_high, rows_low, values)


def wave(index):
    return jnp.where(index < G // 2, index, index - G).astype(F32)


def wavevector(row_index, col_index):
    row = lax.broadcasted_iota(jnp.int32, (G, G), 0)
    lane = lax.broadcasted_iota(jnp.int32, (G, G), 1)
    m1 = 4 * col_index + ((row >> 3) & 3) + (lane & -32)
    m2 = (row >> 5) + 8 * (lane & 31)
    m3 = 4 * row_index + (row & 3)
    return m1, m2, m3


def screen(row_index, col_index):
    m1, m2, m3 = wavevector(row_index, col_index)
    w1, w2, w3 = wave(m1), wave(m2), m3.astype(F32)
    squared = w1 * w1 + w2 * w2 + w3 * w3
    kept = jnp.where((m1 == G // 2) | (m2 == G // 2), 0.0, FACTOR).astype(F32)
    fold = jnp.where(m3 == 0, 1.0, 2.0).astype(F32)
    return w1, w2, w3, 1.0 / jnp.maximum(squared, 1.0), kept * fold / (squared + 0.5)


def spread_kernel(density, weight, corner, target, count, packed, picked):
    row_index, col_index = lax.axis_index("row"), lax.axis_index("col")
    lane = lax.broadcasted_iota(jnp.int32, (STENCIL, CLUSTERS), 1)
    group = 8

    def gather_sums(i, sums):
        start = pl.multiple_of(i * group * PANELS, group * PANELS)
        block = weight[:, pl.ds(start, group * PANELS)]
        charge = density[:, pl.ds(start, group * PANELS)]
        sums = list(sums)
        for c in range(3):
            product = block * charge[c : c + 1]
            for k in range(group):
                total = jnp.sum(product[:, k * PANELS : (k + 1) * PANELS], axis=1, keepdims=True)
                sums[c] = jnp.where(lane == i * group + k, total, sums[c])
        return tuple(sums)

    picked[...] = jnp.zeros_like(picked)
    live = count[0]
    for q in range(SLOTS):
        start = pl.multiple_of(target[q] * PANELS, PANELS)
        charge = density[:, pl.ds(start, PANELS)].astype(BF16).astype(F32)
        picked[q, 0:3] = jnp.where(q < live, charge, jnp.zeros_like(charge))

    zero = jnp.zeros((STENCIL, CLUSTERS), F32)
    sums = lax.fori_loop(0, CLUSTERS // group, gather_sums, (zero,) * 3)

    corners = corner[...]
    local = (corners[0:1] - row_index * 8) * 32 + (corners[1:2] - col_index * 32)
    packed[80:PACKED] = jnp.zeros((PACKED - 80, CLUSTERS), F32)
    for c in range(3):
        packed[c * STENCIL : (c + 1) * STENCIL] = sums[c]
    packed[81:82] = local.astype(F32)
    packed[82:83] = corners[2:3].astype(F32)


def exchange_kernel(
    packed, line, rows_table, lanes_table, twiddle, picked, tiles,
    samples, near_here, near_got,
    gathered, hot, phases, upper, sent1, got1, sent2, got2, modes, sent3, got3, sent4, got4, sent5, got5, near_sent, blocks,
    slab_send, slab_recv, plane_sem, send_sem, recv_sem, near_sem, tile_sem,
):
    row_index, col_index = lax.axis_index("row"), lax.axis_index("col")
    z_index, x_index = row_index // WIDTH, lax.rem(row_index, WIDTH)
    tile_copy = pltpu.make_async_copy(tiles, blocks, tile_sem)
    tile_copy.start()

    def z_peer(j):
        return lax.rem(z_index + j, DEPTH)

    def x_peer(j):
        return lax.rem(x_index + j, WIDTH)

    def col_peer(j):
        return lax.rem(col_index + j, COLS)

    def at_z(peer):
        return (peer * WIDTH + x_index, col_index)

    def at_x(peer):
        return (z_index * WIDTH + peer, col_index)

    def at_col(peer):
        return (row_index, peer)

    def at_row(j):
        return (lax.rem(row_index + j, ROWS), col_index)

    barrier = pltpu.get_barrier_semaphore()

    def greet(device):
        pl.semaphore_signal(barrier, inc=1, device_id=device, device_id_type=MESH)

    def greet_z(j, carry):
        greet(at_z(z_peer(j)))
        return carry

    def greet_x(j, carry):
        greet(at_x(x_peer(j)))
        return carry

    def greet_col(j, carry):
        greet(at_col(col_peer(j)))
        return carry

    lax.fori_loop(1, DEPTH, greet_z, 0)
    lax.fori_loop(1, WIDTH, greet_x, 0)
    lax.fori_loop(1, COLS, greet_col, 0)
    greet(at_row(1))
    greet(at_row(ROWS - 1))
    pl.semaphore_wait(barrier, DEPTH + WIDTH + COLS - 3 + 2)

    def near_first(i):
        odd = lax.rem(i, 2)
        return odd * ((i + 1) // 2) + (1 - odd) * (DEPTH - i // 2)

    def slab_copy(j):
        return pltpu.make_async_remote_copy(
            packed,
            gathered.at[z_index],
            slab_send.at[j],
            slab_recv.at[j],
            device_id=at_z(z_peer(j)),
            device_id_type=MESH,
        )

    def send_slab(i, carry):
        slab_copy(near_first(i)).start()
        return carry

    lax.fori_loop(1, DEPTH, send_slab, 0)
    gathered[z_index] = packed[...]

    def plane_copy(source, target, device):
        return pltpu.make_async_remote_copy(
            source, target, plane_sem.at[0], plane_sem.at[1], device_id=device, device_id_type=MESH
        )

    cell = lax.broadcasted_iota(jnp.int32, (G, CLUSTERS), 0).astype(F32)

    def build(zs):
        local, depth = gathered[zs, 81:82], gathered[zs, 82:83]
        for dz in range(3):
            at = jnp.where(cell == depth + float(dz), 1.0, 0.0).astype(BF16)
            both = mm(line[z_index], at)
            phases[zs, dz] = both[:32] + both[32:]
        for d in range(9):
            here = jnp.where(cell == local + float(d // 3 * 32 + d % 3), 1.0, 0.0).astype(BF16)
            hot[zs, :, d * CLUSTERS : (d + 1) * CLUSTERS] = here
        for c in range(3):
            for d in range(9):
                at = c * STENCIL + 3 * d
                value = phases[zs, 0] * gathered[zs, at : at + 1]
                value += phases[zs, 1] * gathered[zs, at + 1 : at + 2]
                value += phases[zs, 2] * gathered[zs, at + 2 : at + 3]
                high, low = split(value)
                upper[c * 64 : c * 64 + 32, d * CLUSTERS : (d + 1) * CLUSTERS] = high
                upper[c * 64 + 32 : c * 64 + 64, d * CLUSTERS : (d + 1) * CLUSTERS] = low
        total = mm_nt(upper[...], hot[zs])
        for c in range(3):
            plane = total[c * 64 : c * 64 + 32] + total[c * 64 + 32 : c * 64 + 64]
            for peer in range(WIDTH):
                sent1[peer, zs, c] = plane[peer * 8 : peer * 8 + 8]

        def send(j, carry):
            peer = x_peer(j)
            plane_copy(sent1.at[peer, zs], got1.at[x_index, zs], at_x(peer)).start()
            return carry

        lax.fori_loop(1, WIDTH, send, 0)

    build(z_index)

    def next_slab(i, carry):
        j = near_first(i)
        slab_copy(j).wait_recv()
        build(z_peer(DEPTH - j))
        return carry

    lax.fori_loop(1, DEPTH, next_slab, 0)
    got1[x_index] = sent1[x_index]

    def copy(stage, c, source, target, device):
        return pltpu.make_async_remote_copy(
            source,
            target,
            send_sem.at[stage, c],
            recv_sem.at[stage, c],
            device_id=device,
            device_id_type=MESH,
        )

    def to_all(stage, c, source, target, count, mine, peer_of, device_of):
        def one(j, carry):
            peer = peer_of(j)
            copy(stage, c, source.at[c, peer], target.at[c, mine], device_of(peer)).start()
            return carry

        lax.fori_loop(1, count, one, 0)
        target[c, mine] = source[c, mine]

    def whole(stage, c, source, target):
        peers = source.shape[1] - 1
        return copy(stage, c, source.at[c, pl.ds(0, peers)], target.at[c, pl.ds(0, peers)], at_row(1))

    def rows_of(k):
        return rows_table[k, 0], rows_table[k, 1]

    def lanes_of(k):
        return lanes_table[k, 0], lanes_table[k, 1]

    planes = plane_copy(sent1.at[pl.ds(0, WIDTH - 1)], got1.at[pl.ds(0, WIDTH - 1)], at_x(x_peer(1)))
    planes.wait_recv()

    def first_dimension(c, carry):
        values = forward(got1[:, :, c].reshape(G, G), *rows_of(1), *lanes_of(1), twiddle[2], twiddle[3])
        sent2[c] = values.reshape(COLS, 32, G)
        to_all(0, c, sent2, got2, COLS, col_index, col_peer, at_col)
        return carry

    lax.fori_loop(0, 3, first_dimension, 0)

    tile_copy.wait()
    near_sent[...] = jnp.zeros_like(near_sent)

    def slot(q, carry):
        charge = picked[q].astype(BF16)
        for b in range(3):
            total = mm(charge[0:1], blocks[q, 0, b])
            total += mm(charge[1:2], blocks[q, 1, b])
            total += mm(charge[2:3], blocks[q, 2, b])
            near_sent[q, b : b + 1] = total
        return carry

    lax.fori_loop(0, SLOTS, slot, 0)
    near_here[...] = near_sent[0:4]
    near_copies = []
    for side, j in ((0, ROWS - 1), (1, 1)):
        for k in range(4):
            near_copies.append(
                pltpu.make_async_remote_copy(
                    near_sent.at[4 + 2 * k + side],
                    near_got.at[2 * k + side],
                    near_sem.at[0, 2 * k + side],
                    near_sem.at[1, 2 * k + side],
                    device_id=at_row(j),
                    device_id_type=MESH,
                )
            )
    for near_copy in near_copies:
        near_copy.start()

    w1, w2, w3, inverse, weighting = screen(row_index, col_index)

    def second_dimension(c, carry):
        whole(0, c, sent2, got2).wait_recv()
        modes[c] = forward(got2[c].reshape(G, G), *rows_of(0), *lanes_of(0), twiddle[0], twiddle[1])
        return carry

    lax.fori_loop(0, 3, second_dimension, 0)

    inner = (w1 * modes[0] + w2 * modes[1] + w3 * modes[2]) * inverse
    for c, w in enumerate((w1, w2, w3)):
        modes[c] = (modes[c] - w * inner) * weighting

    def second_back(c, carry):
        values = backward(modes[c], *rows_of(3), *lanes_of(0), twiddle[0], twiddle[1])
        sent3[c] = values.reshape(COLS, 32, G)
        to_all(1, c, sent3, got3, COLS, col_index, col_peer, at_col)
        return carry

    lax.fori_loop(0, 3, second_back, 0)

    def first_back(c, carry):
        whole(1, c, sent3, got3).wait_recv()
        values = backward(got3[c].reshape(G, G), *rows_of(2), *lanes_of(1), twiddle[2], twiddle[3])
        sent4[c] = values.reshape(WIDTH, DEPTH, 8, G)
        to_all(2, c, sent4, got4, WIDTH, x_index, x_peer, at_x)
        return carry

    lax.fori_loop(0, 3, first_back, 0)
    sent5[...] = jnp.zeros_like(sent5)

    def sample(c, carry):
        whole(2, c, sent4, got4).wait_recv()

        def slab(zs, carry):
            high, low = split(got4[c, :, zs].reshape(32, G))
            both = mm(jnp.concatenate([high, low], axis=0), hot[zs])
            both = both[:32] + both[32:]
            for d in range(9):
                part = both[:, d * CLUSTERS : (d + 1) * CLUSTERS]
                for dz in range(3):
                    total = jnp.sum(part * phases[zs, dz], axis=0, keepdims=True)
                    sent5[c, zs, 3 * d + dz : 3 * d + dz + 1] = total
            return carry

        lax.fori_loop(0, DEPTH, slab, 0)
        to_all(3, c, sent5, got5, DEPTH, z_index, z_peer, at_z)
        return carry

    lax.fori_loop(0, 3, sample, 0)

    for near_copy in near_copies:
        near_copy.wait()

    def send_done(j, carry):
        slab_copy(j).wait_send()
        return carry

    lax.fori_loop(1, DEPTH, send_done, 0)
    planes.wait_send()

    def finish(c, carry):
        whole(0, c, sent2, got2).wait_send()
        whole(1, c, sent3, got3).wait_send()
        whole(2, c, sent4, got4).wait_send()
        whole(3, c, sent5, got5).wait()
        samples[c] = jnp.sum(got5[c], axis=0)
        return carry

    lax.fori_loop(0, 3, finish, 0)


def project_kernel(values, weight, near_here, near_got, landing, out):
    group = 8

    def clusters(i, carry):
        start = pl.multiple_of(i * group * PANELS, group * PANELS)
        block = weight[:, pl.ds(start, group * PANELS)]
        shift = lax.rem(CLUSTERS - i * group, CLUSTERS)
        for c in range(3):
            turned = pltpu.roll(values[c], shift, 1)
            for k in range(group):
                product = block[:, k * PANELS : (k + 1) * PANELS] * turned[:STENCIL, k : k + 1]
                place = pl.multiple_of(start + k * PANELS, PANELS)
                out[c : c + 1, pl.ds(place, PANELS)] = jnp.sum(product, axis=0, keepdims=True)
        return carry

    lax.fori_loop(0, CLUSTERS // group, clusters, 0)
    for q in range(SLOTS):
        place = pl.multiple_of(landing[q] * PANELS, PANELS)
        arrived = near_here[q] if q < 4 else near_got[q - 4]
        out[:, pl.ds(place, PANELS)] += arrived[:3]


VMEM = pl.BlockSpec(memory_space=pltpu.VMEM)
SMEM = pl.BlockSpec(memory_space=pltpu.SMEM)
ANY = pl.BlockSpec(memory_space=pl.ANY)
LIMIT = 48 * 1024 * 1024


def shape(dims, dtype=F32):
    return jax.ShapeDtypeStruct(dims, dtype)


def per_device(
    density, interp_weight, proj_weight, stencil_corner, near_tiles, pair_target, pair_landing, pair_count
):
    line, rows_table, lanes_table, twiddle = (jnp.asarray(t) for t in make_tables())
    packed, picked = pl.pallas_call(
        spread_kernel,
        out_shape=(shape((PACKED, CLUSTERS)), shape((SLOTS, 8, PANELS))),
        in_specs=[VMEM] * 3 + [SMEM] * 2,
        out_specs=(VMEM, VMEM),
        compiler_params=pltpu.CompilerParams(vmem_limit_bytes=LIMIT),
    )(density, interp_weight, stencil_corner, pair_target, pair_count)
    planes, by_cols = (WIDTH, DEPTH, 3, 8, G), (3, COLS, 32, G)
    by_width, by_depth = (3, WIDTH, DEPTH, 8, G), (3, DEPTH, 32, CLUSTERS)
    samples, near_here, near_got = pl.pallas_call(
        exchange_kernel,
        out_shape=(shape((3, 32, CLUSTERS)), shape((4, 8, PANELS)), shape((8, 8, PANELS))),
        in_specs=[VMEM] * 6 + [ANY],
        out_specs=(VMEM, VMEM, VMEM),
        scratch_shapes=[
            pltpu.VMEM((DEPTH, PACKED, CLUSTERS), F32),
            pltpu.VMEM((DEPTH, G, 9 * CLUSTERS), BF16),
            pltpu.VMEM((DEPTH, 3, 32, CLUSTERS), F32),
            pltpu.VMEM((192, 9 * CLUSTERS), BF16),
            pltpu.VMEM(planes, F32),
            pltpu.VMEM(planes, F32),
            pltpu.VMEM(by_cols, F32),
            pltpu.VMEM(by_cols, F32),
            pltpu.VMEM((3, G, G), F32),
            pltpu.VMEM(by_cols, F32),
            pltpu.VMEM(by_cols, F32),
            pltpu.VMEM(by_width, F32),
            pltpu.VMEM(by_width, F32),
            pltpu.VMEM(by_depth, F32),
            pltpu.VMEM(by_depth, F32),
            pltpu.VMEM((SLOTS, 8, PANELS), F32),
            pltpu.VMEM((SLOTS, 3, 3, PANELS, PANELS), BF16),
            pltpu.SemaphoreType.DMA((DEPTH,)),
            pltpu.SemaphoreType.DMA((DEPTH,)),
            pltpu.SemaphoreType.DMA((2,)),
            pltpu.SemaphoreType.DMA((4, 3)),
            pltpu.SemaphoreType.DMA((4, 3)),
            pltpu.SemaphoreType.DMA((2, 8)),
            pltpu.SemaphoreType.DMA,
        ],
        compiler_params=pltpu.CompilerParams(
            vmem_limit_bytes=LIMIT, collective_id=0, has_side_effects=True
        ),
    )(packed, line, rows_table, lanes_table, twiddle, picked, near_tiles)
    return pl.pallas_call(
        project_kernel,
        out_shape=shape((3, CLUSTERS * PANELS)),
        in_specs=[VMEM] * 4 + [SMEM],
        out_specs=VMEM,
        compiler_params=pltpu.CompilerParams(vmem_limit_bytes=LIMIT),
    )(samples, proj_weight, near_here, near_got, pair_landing)


def solution(mesh):
    flat = P(None, ("row", "col"))
    slots = P(("row", "col"))
    in_specs = (flat, flat, flat, flat, P(("row", "col"), None, None, None, None), slots, slots, slots)
    return jax.shard_map(
        per_device, mesh=mesh, in_specs=in_specs, out_specs=flat, check_vma=False
    )
```

```python
import math

import jax
import jax.numpy as jnp
import ml_dtypes
import numpy as np
from jax import lax
from jax.experimental import pallas as pl
from jax.experimental.pallas import tpu as pltpu
from jax.sharding import PartitionSpec as P

G = 256
STENCIL = 27
ROWS = 32
COLS = 8
DEPTH = 8
WIDTH = 4
PACKED = 88
PIECES = 4
GROUP = 8
CLUSTERS = 128
PANELS = 128
SLOTS = 12
BF16 = jnp.bfloat16
F32 = jnp.float32
MESH = pl.DeviceIdType.MESH
FACTOR = 1.0 / math.sqrt(ROWS * COLS * CLUSTERS * PANELS)


def halves(table):
    table = np.asarray(table, np.float64)
    high = table.astype(np.float32).astype(ml_dtypes.bfloat16)
    low = (table - high.astype(np.float64)).astype(np.float32).astype(ml_dtypes.bfloat16)
    return np.stack([high, low])


def rotation(theta):
    cosine, sine = np.cos(theta), np.sin(theta)
    return np.array([[cosine, sine], [-sine, cosine]])


def make_tables():
    two_pi = 2 * np.pi
    bins, cells = np.arange(128), np.arange(G)
    theta = two_pi * (bins[:, None] * cells[None, :] % G) / G
    line = np.stack([np.cos(theta), -np.sin(theta)]).reshape(2, DEPTH, WIDTH, 4, G)
    line = line.transpose(1, 2, 0, 3, 4).reshape(DEPTH, 32, G)
    line = halves(line).transpose(1, 0, 2, 3).reshape(DEPTH, 64, G)
    eight = np.arange(8)
    wide = np.arange(32)
    turn8 = rotation(two_pi * (eight[:, None] * eight[None, :] % 8) / 8)
    turn32 = rotation(two_pi * (wide[:, None] * wide[None, :] % 32) / 32)
    second = np.einsum("oipc,hg,lm->pholcgim", turn8, np.eye(4), np.eye(4)).reshape(G, G)
    by_block = turn32.reshape(2, 2, 32, DEPTH, WIDTH)
    first = np.einsum("oipzx,lm->polxzim", by_block, np.eye(4)).reshape(G, G)
    lane32 = [np.kron(np.eye(8), f(two_pi * (wide[:, None] * wide[None, :] % 32) / 32)) for f in (np.cos, np.sin)]
    lane8 = [np.kron(f(two_pi * (eight[:, None] * eight[None, :] % 8) / 8), np.eye(32)) for f in (np.cos, np.sin)]
    row = np.arange(G)
    lane = np.arange(G)
    part_sign = np.where(row // 4 % 2 == 0, 1.0, -1.0)[:, None]
    twist_y = two_pi * ((row // 32)[:, None] * (lane % 32)[None, :]) / G
    twist_x = two_pi * ((row // 8)[:, None] * (lane // 32)[None, :]) / G
    twiddle = np.stack(
        [np.cos(twist_y), part_sign * np.sin(twist_y), np.cos(twist_x), part_sign * np.sin(twist_x)]
    ).astype(np.float32)
    rows_table = np.stack([halves(t) for t in (second, first, first.T, second.T)])
    lanes_table = np.stack([halves(np.concatenate(t, axis=1)) for t in (lane32, lane8)])
    return line, rows_table, lanes_table, twiddle


def split(values):
    high = values.astype(BF16)
    return high, (values - high.astype(F32)).astype(BF16)


def mm(a, b):
    return jnp.dot(a, b, preferred_element_type=F32)


def mm_nt(a, b):
    return lax.dot_general(a, b, (((1,), (1,)), ((), ())), preferred_element_type=F32)


def swap(values):
    grouped = values.reshape(32, 8, values.shape[1])
    return pltpu.roll(grouped, 4, 1).reshape(values.shape)


def on_rows(table_high, table_low, values):
    high, low = split(values)
    return mm(table_high, high) + (mm(table_low, high) + mm(table_high, low))


def on_lanes(values, table_high, table_low, sign):
    high, low = split(values)
    both = mm(high, table_high) + (mm(low, table_high) + mm(high, table_low))
    return both[:, :G] + sign * swap(both[:, G:])


def signs(direction):
    row = lax.broadcasted_iota(jnp.int32, (G, G), 0)
    return jnp.where((row & 4) == 0, direction, -direction).astype(F32)


def forward(values, rows_high, rows_low, lanes_high, lanes_low, cosines, sines):
    values = on_rows(rows_high, rows_low, values)
    values = values * cosines + swap(values) * sines
    return on_lanes(values, lanes_high, lanes_low, signs(1.0))


def backward(values, rows_high, rows_low, lanes_high, lanes_low, cosines, sines):
    values = on_lanes(values, lanes_high, lanes_low, signs(-1.0))
    values = values * cosines - swap(values) * sines
    return on_rows(rows_high, rows_low, values)


def wave(index):
    return jnp.where(index < G // 2, index, index - G).astype(F32)


def wavevector(row_index, col_index):
    row = lax.broadcasted_iota(jnp.int32, (G, G), 0)
    lane = lax.broadcasted_iota(jnp.int32, (G, G), 1)
    m1 = 4 * col_index + ((row >> 3) & 3) + (lane & -32)
    m2 = (row >> 5) + 8 * (lane & 31)
    m3 = 4 * row_index + (row & 3)
    return m1, m2, m3


def screen(row_index, col_index):
    m1, m2, m3 = wavevector(row_index, col_index)
    w1, w2, w3 = wave(m1), wave(m2), m3.astype(F32)
    squared = w1 * w1 + w2 * w2 + w3 * w3
    kept = jnp.where((m1 == G // 2) | (m2 == G // 2), 0.0, FACTOR).astype(F32)
    fold = jnp.where(m3 == 0, 1.0, 2.0).astype(F32)
    return w1, w2, w3, 1.0 / jnp.maximum(squared, 1.0), kept * fold / (squared + 0.5)


def spread(weight, density, first, sums):
    lane = lax.broadcasted_iota(jnp.int32, (STENCIL, CLUSTERS), 1)
    group = 8

    def some(i, sums):
        start = pl.multiple_of(i * group * PANELS, group * PANELS)
        block = weight[:, pl.ds(start, group * PANELS)]
        charge = density[:, pl.ds(start, group * PANELS)]
        sums = list(sums)
        for c in range(3):
            product = block * charge[c : c + 1]
            for k in range(group):
                total = jnp.sum(product[:, k * PANELS : (k + 1) * PANELS], axis=1, keepdims=True)
                sums[c] = jnp.where(lane == i * group + k, total, sums[c])
        return tuple(sums)

    groups = CLUSTERS // PIECES // group
    return lax.fori_loop(first * groups, (first + 1) * groups, some, sums)


def whole_kernel(
    corner, target, landing, count, density_in, interp_in, proj_in, line_in, rows_in, lanes_in, twiddle_in, tiles_in,
    out,
    density, interp, proj, line, rows_table, lanes_table, twiddle, blocks,
    packed, picked, gathered, hot, phases, upper, sent1, got1, sent2, got2, modes, sent3, got3, sent4, got4, sent5, got5,
    near_sent, near_got, near_rows, near_term, proj_high, proj_low, values,
    load_sem, slab_send, slab_recv, plane_sem, send_sem, recv_sem, near_sem,
):
    row_index, col_index = lax.axis_index("row"), lax.axis_index("col")
    z_index, x_index = row_index // WIDTH, lax.rem(row_index, WIDTH)
    width = CLUSTERS * PANELS // PIECES

    def piece(k):
        at = pl.ds(k * width, width)
        return pltpu.make_async_copy(interp_in.at[:, at], interp.at[:, at], load_sem.at[k])

    loads = [
        pltpu.make_async_copy(source, target_ref, load_sem.at[PIECES + k])
        for k, (source, target_ref) in enumerate(
            (
                (density_in, density),
                (line_in, line),
                (rows_in, rows_table),
                (lanes_in, lanes_table),
                (twiddle_in, twiddle),
                (tiles_in, blocks),
                (proj_in, proj),
            )
        )
    ]
    loads[0].start()
    for k in range(PIECES):
        piece(k).start()

    def z_peer(j):
        return lax.rem(z_index + j, DEPTH)

    def x_peer(j):
        return lax.rem(x_index + j, WIDTH)

    def col_peer(j):
        return lax.rem(col_index + j, COLS)

    def at_z(peer):
        return (peer * WIDTH + x_index, col_index)

    def at_x(peer):
        return (z_index * WIDTH + peer, col_index)

    def at_col(peer):
        return (row_index, peer)

    def at_row(j):
        return (lax.rem(row_index + j, ROWS), col_index)

    barrier = pltpu.get_barrier_semaphore()

    def greet(device):
        pl.semaphore_signal(barrier, inc=1, device_id=device, device_id_type=MESH)

    def greet_z(j, carry):
        greet(at_z(z_peer(j)))
        return carry

    def greet_x(j, carry):
        greet(at_x(x_peer(j)))
        return carry

    def greet_col(j, carry):
        greet(at_col(col_peer(j)))
        return carry

    lax.fori_loop(1, DEPTH, greet_z, 0)
    lax.fori_loop(1, WIDTH, greet_x, 0)
    lax.fori_loop(1, COLS, greet_col, 0)
    greet(at_row(1))
    greet(at_row(ROWS - 1))
    loads[0].wait()
    sums = (jnp.zeros((STENCIL, CLUSTERS), F32),) * 3
    for k in range(PIECES):
        piece(k).wait()
        if k == 0:
            for load in loads[1:]:
                load.start()
        sums = spread(interp, density, k, sums)
    corners = corner[...]
    packed[80:PACKED] = jnp.zeros((PACKED - 80, CLUSTERS), F32)
    for c in range(3):
        packed[c * STENCIL : (c + 1) * STENCIL] = sums[c]
    packed[81:82] = ((corners[0:1] - row_index * 8) * 32 + (corners[1:2] - col_index * 32)).astype(F32)
    packed[82:83] = corners[2:3].astype(F32)
    pl.semaphore_wait(barrier, DEPTH + WIDTH + COLS - 3 + 2)

    def near_first(i):
        odd = lax.rem(i, 2)
        return odd * ((i + 1) // 2) + (1 - odd) * (DEPTH - i // 2)

    def slab_copy(j):
        return pltpu.make_async_remote_copy(
            packed,
            gathered.at[z_index],
            slab_send.at[j],
            slab_recv.at[j],
            device_id=at_z(z_peer(j)),
            device_id_type=MESH,
        )

    def send_slab(i, carry):
        slab_copy(near_first(i)).start()
        return carry

    lax.fori_loop(1, DEPTH, send_slab, 0)
    gathered[z_index] = packed[...]

    def plane_copy(source, target, device):
        return pltpu.make_async_remote_copy(
            source, target, plane_sem.at[0], plane_sem.at[1], device_id=device, device_id_type=MESH
        )

    cell = lax.broadcasted_iota(jnp.int32, (G, CLUSTERS), 0).astype(F32)

    def build(zs):
        local, depth = gathered[zs, 81:82], gathered[zs, 82:83]
        for dz in range(3):
            at = jnp.where(cell == depth + float(dz), 1.0, 0.0).astype(BF16)
            both = mm(line[z_index], at)
            phases[zs, dz] = both[:32] + both[32:]
        for d in range(9):
            here = jnp.where(cell == local + float(d // 3 * 32 + d % 3), 1.0, 0.0).astype(BF16)
            hot[zs, :, d * CLUSTERS : (d + 1) * CLUSTERS] = here
        for c in range(3):
            for d in range(9):
                at = c * STENCIL + 3 * d
                value = phases[zs, 0] * gathered[zs, at : at + 1]
                value += phases[zs, 1] * gathered[zs, at + 1 : at + 2]
                value += phases[zs, 2] * gathered[zs, at + 2 : at + 3]
                high, low = split(value)
                upper[c * 64 : c * 64 + 32, d * CLUSTERS : (d + 1) * CLUSTERS] = high
                upper[c * 64 + 32 : c * 64 + 64, d * CLUSTERS : (d + 1) * CLUSTERS] = low
        total = mm_nt(upper[...], hot[zs])
        for c in range(3):
            plane = total[c * 64 : c * 64 + 32] + total[c * 64 + 32 : c * 64 + 64]
            for peer in range(WIDTH):
                sent1[peer, zs, c] = plane[peer * 8 : peer * 8 + 8]

        def send(j, carry):
            peer = x_peer(j)
            plane_copy(sent1.at[peer, zs], got1.at[x_index, zs], at_x(peer)).start()
            return carry

        lax.fori_loop(1, WIDTH, send, 0)

    loads[1].wait()
    build(z_index)

    def next_slab(i, carry):
        j = near_first(i)
        slab_copy(j).wait_recv()
        build(z_peer(DEPTH - j))
        return carry

    lax.fori_loop(1, DEPTH, next_slab, 0)
    got1[x_index] = sent1[x_index]

    def copy(stage, c, source, target, device):
        return pltpu.make_async_remote_copy(
            source,
            target,
            send_sem.at[stage, c],
            recv_sem.at[stage, c],
            device_id=device,
            device_id_type=MESH,
        )

    def to_all(stage, c, source, target, count, mine, peer_of, device_of):
        def one(j, carry):
            peer = peer_of(j)
            copy(stage, c, source.at[c, peer], target.at[c, mine], device_of(peer)).start()
            return carry

        lax.fori_loop(1, count, one, 0)
        target[c, mine] = source[c, mine]

    def whole(stage, c, source, target):
        peers = source.shape[1] - 1
        return copy(stage, c, source.at[c, pl.ds(0, peers)], target.at[c, pl.ds(0, peers)], at_row(1))

    def rows_of(k):
        return rows_table[k, 0], rows_table[k, 1]

    def lanes_of(k):
        return lanes_table[k, 0], lanes_table[k, 1]

    planes = plane_copy(sent1.at[pl.ds(0, WIDTH - 1)], got1.at[pl.ds(0, WIDTH - 1)], at_x(x_peer(1)))
    for load in loads[2:5]:
        load.wait()
    planes.wait_recv()

    def first_dimension(c, carry):
        values = forward(got1[:, :, c].reshape(G, G), *rows_of(1), *lanes_of(1), twiddle[2], twiddle[3])
        sent2[c] = values.reshape(COLS, 32, G)
        to_all(0, c, sent2, got2, COLS, col_index, col_peer, at_col)
        return carry

    lax.fori_loop(0, 3, first_dimension, 0)

    loads[5].wait()
    near_sent[...] = jnp.zeros_like(near_sent)
    picked[...] = jnp.zeros_like(picked)
    nobody = jnp.full((3, PANELS), -1, jnp.int32)
    wanted = [
        jnp.where(jnp.full((3, PANELS), q, jnp.int32) < count[0], jnp.full((3, PANELS), target[q], jnp.int32), nobody)
        for q in range(SLOTS)
    ]

    def pick(i, charges):
        charges = list(charges)
        for k in range(GROUP):
            cluster = i * GROUP + k
            charge = density[:, pl.ds(pl.multiple_of(cluster * PANELS, PANELS), PANELS)]
            for q in range(SLOTS):
                charges[q] = jnp.where(wanted[q] == cluster, charge, charges[q])
        return tuple(charges)

    charges = lax.fori_loop(0, CLUSTERS // GROUP, pick, (jnp.zeros((3, PANELS), F32),) * SLOTS)
    for q in range(SLOTS):
        picked[q, 0:3] = charges[q]

    def slot(q, carry):
        charge = picked[q].astype(BF16)
        for b in range(3):
            total = mm(charge[0:1], blocks[q, 0, b])
            total += mm(charge[1:2], blocks[q, 1, b])
            total += mm(charge[2:3], blocks[q, 2, b])
            near_sent[q, b : b + 1] = total
        return carry

    lax.fori_loop(0, SLOTS, slot, 0)
    near_copies = []
    for side, j in ((0, ROWS - 1), (1, 1)):
        for k in range(4):
            near_copies.append(
                pltpu.make_async_remote_copy(
                    near_sent.at[4 + 2 * k + side],
                    near_got.at[2 * k + side],
                    near_sem.at[0, 2 * k + side],
                    near_sem.at[1, 2 * k + side],
                    device_id=at_row(j),
                    device_id_type=MESH,
                )
            )
    for near_copy in near_copies:
        near_copy.start()

    loads[6].wait()
    below = jnp.zeros((32 - STENCIL, PANELS), F32)

    def halve(i, carry):
        start = pl.multiple_of(i * GROUP * PANELS, GROUP * PANELS)
        for k in range(GROUP):
            block = proj[:, pl.ds(start + k * PANELS, PANELS)]
            high, low = split(jnp.concatenate([block, below], axis=0))
            proj_high[i, k * 32 : (k + 1) * 32] = high
            proj_low[i, k * 32 : (k + 1) * 32] = low
        return carry

    lax.fori_loop(0, CLUSTERS // GROUP, halve, 0)

    w1, w2, w3, inverse, weighting = screen(row_index, col_index)

    def second_dimension(c, carry):
        whole(0, c, sent2, got2).wait_recv()
        modes[c] = forward(got2[c].reshape(G, G), *rows_of(0), *lanes_of(0), twiddle[0], twiddle[1])
        return carry

    lax.fori_loop(0, 3, second_dimension, 0)

    inner = (w1 * modes[0] + w2 * modes[1] + w3 * modes[2]) * inverse
    for c, w in enumerate((w1, w2, w3)):
        modes[c] = (modes[c] - w * inner) * weighting

    def second_back(c, carry):
        values = backward(modes[c], *rows_of(3), *lanes_of(0), twiddle[0], twiddle[1])
        sent3[c] = values.reshape(COLS, 32, G)
        to_all(1, c, sent3, got3, COLS, col_index, col_peer, at_col)
        return carry

    lax.fori_loop(0, 3, second_back, 0)

    def first_back(c, carry):
        whole(1, c, sent3, got3).wait_recv()
        values = backward(got3[c].reshape(G, G), *rows_of(2), *lanes_of(1), twiddle[2], twiddle[3])
        sent4[c] = values.reshape(WIDTH, DEPTH, 8, G)
        to_all(2, c, sent4, got4, WIDTH, x_index, x_peer, at_x)
        return carry

    lax.fori_loop(0, 3, first_back, 0)
    sent5[...] = jnp.zeros_like(sent5)

    for near_copy in near_copies:
        near_copy.wait()
    near_rows[...] = jnp.zeros_like(near_rows)
    row = lax.broadcasted_iota(jnp.int32, (CLUSTERS, CLUSTERS), 0)
    lane = lax.broadcasted_iota(jnp.int32, (CLUSTERS, CLUSTERS), 1)
    lands = jnp.zeros((CLUSTERS, CLUSTERS), F32)
    for q in range(SLOTS):
        lands = jnp.where((lane == q) & (row == landing[q]), 1.0, lands)
        for b in range(3):
            arrived = near_sent[q, b : b + 1] if q < 4 else near_got[q - 4, b : b + 1]
            near_rows[q : q + 1, b * PANELS : (b + 1) * PANELS] = arrived
    lands = lands.astype(BF16)
    high, low = split(near_rows[...])
    near_term[...] = mm(lands, high) + mm(lands, low)

    def sample(c, carry):
        whole(2, c, sent4, got4).wait_recv()

        def slab(zs, carry):
            high, low = split(got4[c, :, zs].reshape(32, G))
            both = mm(jnp.concatenate([high, low], axis=0), hot[zs])
            both = both[:32] + both[32:]
            for d in range(9):
                part = both[:, d * CLUSTERS : (d + 1) * CLUSTERS]
                for dz in range(3):
                    total = jnp.sum(part * phases[zs, dz], axis=0, keepdims=True)
                    sent5[c, zs, 3 * d + dz : 3 * d + dz + 1] = total
            return carry

        lax.fori_loop(0, DEPTH, slab, 0)
        to_all(3, c, sent5, got5, DEPTH, z_index, z_peer, at_z)
        return carry

    lax.fori_loop(0, 3, sample, 0)

    def send_done(j, carry):
        slab_copy(j).wait_send()
        return carry

    lax.fori_loop(1, DEPTH, send_done, 0)
    planes.wait_send()

    def finish(c, carry):
        whole(0, c, sent2, got2).wait_send()
        whole(1, c, sent3, got3).wait_send()
        whole(2, c, sent4, got4).wait_send()
        whole(3, c, sent5, got5).wait()
        total = jnp.sum(got5[c], axis=0)
        turned = jnp.concatenate([total] * 4, axis=0).T
        both = jnp.concatenate([turned, turned], axis=1)
        both = jnp.where(own, both, jnp.zeros_like(both))
        high = both.astype(BF16).astype(F32)
        low = both - high
        for i in range(CLUSTERS // GROUP):
            at = slice(i * GROUP, (i + 1) * GROUP)
            values[i, c] = jnp.concatenate([high[at], low[at]], axis=0).astype(BF16)
        return carry

    own = (lax.broadcasted_iota(jnp.int32, (CLUSTERS, G), 0) & (GROUP - 1)) == (
        lax.broadcasted_iota(jnp.int32, (CLUSTERS, G), 1) >> 5
    )
    lax.fori_loop(0, 3, finish, 0)

    def project(i, carry):
        point_values = values[i].reshape(3 * 2 * GROUP, G)
        both = mm(point_values, proj_high[i]) + mm(point_values, proj_low[i])
        at = pl.ds(pl.multiple_of(i * GROUP, GROUP), GROUP)
        for c in range(3):
            far = both[c * 2 * GROUP : c * 2 * GROUP + GROUP] + both[c * 2 * GROUP + GROUP : (c + 1) * 2 * GROUP]
            out[c, at] = far + near_term[at, c * PANELS : (c + 1) * PANELS]
        return carry

    lax.fori_loop(0, CLUSTERS // GROUP, project, 0)


VMEM = pl.BlockSpec(memory_space=pltpu.VMEM)
SMEM = pl.BlockSpec(memory_space=pltpu.SMEM)
ANY = pl.BlockSpec(memory_space=pl.ANY)
LIMIT = 60 * 1024 * 1024


def shape(dims, dtype=F32):
    return jax.ShapeDtypeStruct(dims, dtype)


def per_device(
    density, interp_weight, proj_weight, stencil_corner, near_tiles, pair_target, pair_landing, pair_count
):
    line, rows_table, lanes_table, twiddle = (jnp.asarray(t) for t in make_tables())
    planes, by_cols = (WIDTH, DEPTH, 3, 8, G), (3, COLS, 32, G)
    by_width, by_depth = (3, WIDTH, DEPTH, 8, G), (3, DEPTH, 32, CLUSTERS)
    held = (density, interp_weight, proj_weight, line, rows_table, lanes_table, twiddle, near_tiles)
    weights = pltpu.VMEM((CLUSTERS // GROUP, G, PANELS), BF16)
    out = pl.pallas_call(
        whole_kernel,
        out_shape=shape((3, CLUSTERS, PANELS)),
        in_specs=[VMEM] + [SMEM] * 3 + [ANY] * 8,
        out_specs=VMEM,
        scratch_shapes=[
            *(pltpu.VMEM(array.shape, array.dtype) for array in held),
            pltpu.VMEM((PACKED, CLUSTERS), F32),
            pltpu.VMEM((SLOTS, 8, PANELS), F32),
            pltpu.VMEM((DEPTH, PACKED, CLUSTERS), F32),
            pltpu.VMEM((DEPTH, G, 9 * CLUSTERS), BF16),
            pltpu.VMEM((DEPTH, 3, 32, CLUSTERS), F32),
            pltpu.VMEM((192, 9 * CLUSTERS), BF16),
            pltpu.VMEM(planes, F32),
            pltpu.VMEM(planes, F32),
            pltpu.VMEM(by_cols, F32),
            pltpu.VMEM(by_cols, F32),
            pltpu.VMEM((3, G, G), F32),
            pltpu.VMEM(by_cols, F32),
            pltpu.VMEM(by_cols, F32),
            pltpu.VMEM(by_width, F32),
            pltpu.VMEM(by_width, F32),
            pltpu.VMEM(by_depth, F32),
            pltpu.VMEM(by_depth, F32),
            pltpu.VMEM((SLOTS, 8, PANELS), F32),
            pltpu.VMEM((8, 8, PANELS), F32),
            pltpu.VMEM((CLUSTERS, 3 * PANELS), F32),
            pltpu.VMEM((CLUSTERS, 3 * PANELS), F32),
            weights,
            weights,
            pltpu.VMEM((CLUSTERS // GROUP, 3, 2 * GROUP, G), BF16),
            pltpu.SemaphoreType.DMA((PIECES + 7,)),
            pltpu.SemaphoreType.DMA((DEPTH,)),
            pltpu.SemaphoreType.DMA((DEPTH,)),
            pltpu.SemaphoreType.DMA((2,)),
            pltpu.SemaphoreType.DMA((4, 3)),
            pltpu.SemaphoreType.DMA((4, 3)),
            pltpu.SemaphoreType.DMA((2, 8)),
        ],
        compiler_params=pltpu.CompilerParams(
            vmem_limit_bytes=LIMIT, collective_id=0, has_side_effects=True
        ),
    )(stencil_corner, pair_target, pair_landing, pair_count, *held)
    return out.reshape(3, CLUSTERS * PANELS)


def solution(mesh):
    flat = P(None, ("row", "col"))
    slots = P(("row", "col"))
    in_specs = (flat, flat, flat, flat, P(("row", "col"), None, None, None, None), slots, slots, slots)
    return jax.shard_map(
        per_device, mesh=mesh, in_specs=in_specs, out_specs=flat, check_vma=False
    )
```

```python
import math

import jax
import jax.numpy as jnp
import ml_dtypes
import numpy as np
from jax import lax
from jax.experimental import pallas as pl
from jax.experimental.pallas import tpu as pltpu
from jax.sharding import PartitionSpec as P

G = 256
STENCIL = 27
ROWS = 32
COLS = 8
DEPTH = 8
WIDTH = 4
PACKED = 88
PIECES = 4
GROUP = 8
CLUSTERS = 128
PANELS = 128
SLOTS = 12
BF16 = jnp.bfloat16
F32 = jnp.float32
MESH = pl.DeviceIdType.MESH
FACTOR = 1.0 / math.sqrt(ROWS * COLS * CLUSTERS * PANELS)


def halves(table):
    table = np.asarray(table, np.float64)
    high = table.astype(np.float32).astype(ml_dtypes.bfloat16)
    low = (table - high.astype(np.float64)).astype(np.float32).astype(ml_dtypes.bfloat16)
    return np.stack([high, low])


def rotation(theta):
    cosine, sine = np.cos(theta), np.sin(theta)
    return np.array([[cosine, sine], [-sine, cosine]])


def make_tables():
    two_pi = 2 * np.pi
    bins, cells = np.arange(128), np.arange(G)
    theta = two_pi * (bins[:, None] * cells[None, :] % G) / G
    line = np.stack([np.cos(theta), -np.sin(theta)]).reshape(2, DEPTH, WIDTH, 4, G)
    line = line.transpose(1, 2, 0, 3, 4).reshape(DEPTH, 32, G)
    line = halves(line).transpose(1, 0, 2, 3).reshape(DEPTH, 64, G)
    step = 2 * np.pi * np.arange(128).reshape(DEPTH, WIDTH, 1, 4) / G
    onward = np.stack([np.cos(step) + np.zeros((2, 1)), np.sin(step) * np.array([[1.0], [-1.0]])], axis=1)
    onward = np.broadcast_to(onward.reshape(DEPTH, 2, 32, 1), (DEPTH, 2, 32, CLUSTERS)).astype(np.float32)
    eight = np.arange(8)
    wide = np.arange(32)
    turn8 = rotation(two_pi * (eight[:, None] * eight[None, :] % 8) / 8)
    turn32 = rotation(two_pi * (wide[:, None] * wide[None, :] % 32) / 32)
    second = np.einsum("oipc,hg,lm->pholcgim", turn8, np.eye(4), np.eye(4)).reshape(G, G)
    by_block = turn32.reshape(2, 2, 32, DEPTH, WIDTH)
    first = np.einsum("oipzx,lm->polxzim", by_block, np.eye(4)).reshape(G, G)
    lane32 = [np.kron(np.eye(8), f(two_pi * (wide[:, None] * wide[None, :] % 32) / 32)) for f in (np.cos, np.sin)]
    lane8 = [np.kron(f(two_pi * (eight[:, None] * eight[None, :] % 8) / 8), np.eye(32)) for f in (np.cos, np.sin)]
    row = np.arange(G)
    lane = np.arange(G)
    part_sign = np.where(row // 4 % 2 == 0, 1.0, -1.0)[:, None]
    twist_y = two_pi * ((row // 32)[:, None] * (lane % 32)[None, :]) / G
    twist_x = two_pi * ((row // 8)[:, None] * (lane // 32)[None, :]) / G
    twiddle = np.stack(
        [np.cos(twist_y), part_sign * np.sin(twist_y), np.cos(twist_x), part_sign * np.sin(twist_x)]
    ).astype(np.float32)
    rows_table = np.stack([halves(t) for t in (second, first, first.T, second.T)])
    lanes_table = np.stack([halves(np.concatenate(t, axis=1)) for t in (lane32, lane8)])
    return line, np.ascontiguousarray(onward), rows_table, lanes_table, twiddle


def split(values):
    high = values.astype(BF16)
    return high, (values - high.astype(F32)).astype(BF16)


def mm(a, b):
    return jnp.dot(a, b, preferred_element_type=F32)


def mm_nt(a, b):
    return lax.dot_general(a, b, (((1,), (1,)), ((), ())), preferred_element_type=F32)


def swap(values):
    grouped = values.reshape(values.shape[0] // 8, 8, values.shape[1])
    return pltpu.roll(grouped, 4, 1).reshape(values.shape)


def on_rows(table_high, table_low, values):
    high, low = split(values)
    return mm(table_high, high) + (mm(table_low, high) + mm(table_high, low))


def on_lanes(values, table_high, table_low, sign):
    high, low = split(values)
    both = mm(high, table_high) + (mm(low, table_high) + mm(high, table_low))
    return both[:, :G] + sign * swap(both[:, G:])


def signs(direction):
    row = lax.broadcasted_iota(jnp.int32, (G, G), 0)
    return jnp.where((row & 4) == 0, direction, -direction).astype(F32)


def forward(values, rows_high, rows_low, lanes_high, lanes_low, cosines, sines):
    values = on_rows(rows_high, rows_low, values)
    values = values * cosines + swap(values) * sines
    return on_lanes(values, lanes_high, lanes_low, signs(1.0))


def backward(values, rows_high, rows_low, lanes_high, lanes_low, cosines, sines):
    values = on_lanes(values, lanes_high, lanes_low, signs(-1.0))
    values = values * cosines - swap(values) * sines
    return on_rows(rows_high, rows_low, values)


def wave(index):
    return jnp.where(index < G // 2, index, index - G).astype(F32)


def wavevector(row_index, col_index):
    row = lax.broadcasted_iota(jnp.int32, (G, G), 0)
    lane = lax.broadcasted_iota(jnp.int32, (G, G), 1)
    m1 = 4 * col_index + ((row >> 3) & 3) + (lane & -32)
    m2 = (row >> 5) + 8 * (lane & 31)
    m3 = 4 * row_index + (row & 3)
    return m1, m2, m3


def screen(row_index, col_index):
    m1, m2, m3 = wavevector(row_index, col_index)
    w1, w2, w3 = wave(m1), wave(m2), m3.astype(F32)
    squared = w1 * w1 + w2 * w2 + w3 * w3
    kept = jnp.where((m1 == G // 2) | (m2 == G // 2), 0.0, FACTOR).astype(F32)
    fold = jnp.where(m3 == 0, 1.0, 2.0).astype(F32)
    return w1, w2, w3, 1.0 / jnp.maximum(squared, 1.0), kept * fold / (squared + 0.5)


def spread(weight, density, first, sums):
    lane = lax.broadcasted_iota(jnp.int32, (STENCIL, CLUSTERS), 1)
    group = 8

    def some(i, sums):
        start = pl.multiple_of(i * group * PANELS, group * PANELS)
        block = weight[:, pl.ds(start, group * PANELS)]
        charge = density[:, pl.ds(start, group * PANELS)]
        sums = list(sums)
        for c in range(3):
            product = block * charge[c : c + 1]
            for k in range(group):
                total = jnp.sum(product[:, k * PANELS : (k + 1) * PANELS], axis=1, keepdims=True)
                sums[c] = jnp.where(lane == i * group + k, total, sums[c])
        return tuple(sums)

    groups = CLUSTERS // PIECES // group
    return lax.fori_loop(first * groups, (first + 1) * groups, some, sums, unroll=4)


def whole_kernel(
    corner, target, landing, count, density_in, interp_in, proj_in, line_in, onward_in, rows_in, lanes_in, twiddle_in, tiles_in,
    out,
    density, interp, proj, line, onward, rows_table, lanes_table, twiddle, blocks,
    packed, picked, gathered, hot, phases, upper, sent1, got1, sent2, got2, modes, sent3, got3, sent4, got4, sent5, got5,
    near_sent, near_got, near_rows, near_term, proj_high, proj_low, values,
    load_sem, slab_send, slab_recv, plane_sem, send_sem, recv_sem, near_sem,
):
    row_index, col_index = lax.axis_index("row"), lax.axis_index("col")
    z_index, x_index = row_index // WIDTH, lax.rem(row_index, WIDTH)
    width = CLUSTERS * PANELS // PIECES

    def piece(k):
        at = pl.ds(k * width, width)
        return pltpu.make_async_copy(interp_in.at[:, at], interp.at[:, at], load_sem.at[k])

    loads = [
        pltpu.make_async_copy(source, target_ref, load_sem.at[PIECES + k])
        for k, (source, target_ref) in enumerate(
            (
                (density_in, density),
                (line_in, line),
                (onward_in, onward),
                (rows_in, rows_table),
                (lanes_in, lanes_table),
                (twiddle_in, twiddle),
                (tiles_in, blocks),
                (proj_in, proj),
            )
        )
    ]
    loads[0].start()
    for k in range(PIECES):
        piece(k).start()

    def z_peer(j):
        return lax.rem(z_index + j, DEPTH)

    def x_peer(j):
        return lax.rem(x_index + j, WIDTH)

    def col_peer(j):
        return lax.rem(col_index + j, COLS)

    def at_z(peer):
        return (peer * WIDTH + x_index, col_index)

    def at_x(peer):
        return (z_index * WIDTH + peer, col_index)

    def at_col(peer):
        return (row_index, peer)

    def at_row(j):
        return (lax.rem(row_index + j, ROWS), col_index)

    barrier = pltpu.get_barrier_semaphore()

    def greet(device):
        pl.semaphore_signal(barrier, inc=1, device_id=device, device_id_type=MESH)

    def greet_z(j, carry):
        greet(at_z(z_peer(j)))
        return carry

    def greet_x(j, carry):
        greet(at_x(x_peer(j)))
        return carry

    def greet_col(j, carry):
        greet(at_col(col_peer(j)))
        return carry

    lax.fori_loop(1, DEPTH, greet_z, 0)
    lax.fori_loop(1, WIDTH, greet_x, 0)
    lax.fori_loop(1, COLS, greet_col, 0)
    greet(at_row(1))
    greet(at_row(ROWS - 1))
    loads[0].wait()
    sums = (jnp.zeros((STENCIL, CLUSTERS), F32),) * 3
    for k in range(PIECES):
        piece(k).wait()
        if k == 0:
            for load in loads[1:]:
                load.start()
        sums = spread(interp, density, k, sums)
    corners = corner[...]
    packed[80:PACKED] = jnp.zeros((PACKED - 80, CLUSTERS), F32)
    for c in range(3):
        packed[c * STENCIL : (c + 1) * STENCIL] = sums[c]
    packed[81:82] = ((corners[0:1] - row_index * 8) * 32 + (corners[1:2] - col_index * 32)).astype(F32)
    packed[82:83] = corners[2:3].astype(F32)
    pl.semaphore_wait(barrier, DEPTH + WIDTH + COLS - 3 + 2)

    def distance(i):
        odd = lax.rem(i, 2)
        return odd * (DEPTH - (i + 1) // 2) + (1 - odd) * (i // 2)

    def slab_copy(i):
        return pltpu.make_async_remote_copy(
            packed,
            gathered.at[z_index],
            slab_send.at[i],
            slab_recv.at[i],
            device_id=at_z(z_peer(DEPTH - distance(i))),
            device_id_type=MESH,
        )

    slab_copy(1).start()
    slab_copy(2).start()
    gathered[z_index] = packed[...]

    def plane_copy(source, target, device):
        return pltpu.make_async_remote_copy(
            source, target, plane_sem.at[0], plane_sem.at[1], device_id=device, device_id_type=MESH
        )

    cell = lax.broadcasted_iota(jnp.int32, (G, CLUSTERS), 0).astype(F32)

    def build(zs):
        local, depth = gathered[zs, 81:82], gathered[zs, 82:83]
        at = jnp.where(cell == depth, 1.0, 0.0).astype(BF16)
        both = mm(line[z_index], at)
        turn = [both[:32] + both[32:]]
        for dz in range(1, 3):
            turn.append(turn[-1] * onward[z_index, 0] + swap(turn[-1]) * onward[z_index, 1])
        for dz in range(3):
            phases[zs, dz] = turn[dz]
        for dy in range(3):
            here = jnp.where(cell == local + float(dy), 1.0, 0.0).astype(BF16)
            hot[zs, :, dy * CLUSTERS : (dy + 1) * CLUSTERS] = here
        for dx in range(3):
            for c in range(3):
                for dy in range(3):
                    at = c * STENCIL + 9 * dx + 3 * dy
                    value = turn[0] * gathered[zs, at : at + 1]
                    value += turn[1] * gathered[zs, at + 1 : at + 2]
                    value += turn[2] * gathered[zs, at + 2 : at + 3]
                    high, low = split(value)
                    top = dx * 192 + c * 64
                    upper[top : top + 32, dy * CLUSTERS : (dy + 1) * CLUSTERS] = high
                    upper[top + 32 : top + 64, dy * CLUSTERS : (dy + 1) * CLUSTERS] = low
        total = mm_nt(upper[...], hot[zs])
        for c in range(3):
            plane = jnp.zeros((32, G), F32)
            for dx in range(3):
                top = dx * 192 + c * 64
                part = total[top : top + 32] + total[top + 32 : top + 64]
                plane += pltpu.roll(part, 32 * dx, 1) if dx else part
            for peer in range(WIDTH):
                sent1[peer, zs, c] = plane[peer * 8 : peer * 8 + 8]

        def send(j, carry):
            peer = x_peer(j)
            plane_copy(sent1.at[peer, zs], got1.at[x_index, zs], at_x(peer)).start()
            return carry

        lax.fori_loop(1, WIDTH, send, 0)

    loads[1].wait()
    loads[2].wait()

    def next_slab(i, carry):
        @pl.when(i == 1)
        def _():
            slab_copy(3).start()
            slab_copy(4).start()

        @pl.when(i >= 1)
        def _():
            slab_copy(i).wait_recv()

        @pl.when(i == 2)
        def _():
            slab_copy(5).start()
            slab_copy(6).start()

        @pl.when(i == 4)
        def _():
            slab_copy(7).start()

        build(z_peer(distance(i)))
        return carry

    lax.fori_loop(0, DEPTH, next_slab, 0)
    got1[x_index] = sent1[x_index]

    def copy(stage, c, source, target, device):
        return pltpu.make_async_remote_copy(
            source,
            target,
            send_sem.at[stage, c],
            recv_sem.at[stage, c],
            device_id=device,
            device_id_type=MESH,
        )

    def to_all(stage, c, source, target, count, mine, peer_of, device_of):
        def one(j, carry):
            peer = peer_of(j)
            copy(stage, c, source.at[c, peer], target.at[c, mine], device_of(peer)).start()
            return carry

        lax.fori_loop(1, count, one, 0)
        target[c, mine] = source[c, mine]

    def whole(stage, c, source, target):
        peers = source.shape[1] - 1
        return copy(stage, c, source.at[c, pl.ds(0, peers)], target.at[c, pl.ds(0, peers)], at_row(1))

    def rows_of(k):
        return rows_table[k, 0], rows_table[k, 1]

    def lanes_of(k):
        return lanes_table[k, 0], lanes_table[k, 1]

    planes = plane_copy(sent1.at[pl.ds(0, WIDTH - 1)], got1.at[pl.ds(0, WIDTH - 1)], at_x(x_peer(1)))
    for load in loads[3:6]:
        load.wait()
    planes.wait_recv()

    def first_dimension(c, carry):
        values = forward(got1[:, :, c].reshape(G, G), *rows_of(1), *lanes_of(1), twiddle[2], twiddle[3])
        sent2[c] = values.reshape(COLS, 32, G)
        to_all(0, c, sent2, got2, COLS, col_index, col_peer, at_col)
        return carry

    lax.fori_loop(0, 3, first_dimension, 0)

    loads[6].wait()
    near_sent[...] = jnp.zeros_like(near_sent)
    picked[...] = jnp.zeros_like(picked)
    nobody = jnp.full((3, PANELS), -1, jnp.int32)
    wanted = [
        jnp.where(jnp.full((3, PANELS), q, jnp.int32) < count[0], jnp.full((3, PANELS), target[q], jnp.int32), nobody)
        for q in range(SLOTS)
    ]

    def pick(i, charges):
        charges = list(charges)
        for k in range(GROUP):
            cluster = i * GROUP + k
            charge = density[:, pl.ds(pl.multiple_of(cluster * PANELS, PANELS), PANELS)]
            for q in range(SLOTS):
                charges[q] = jnp.where(wanted[q] == cluster, charge, charges[q])
        return tuple(charges)

    charges = lax.fori_loop(0, CLUSTERS // GROUP, pick, (jnp.zeros((3, PANELS), F32),) * SLOTS)
    for q in range(SLOTS):
        picked[q, 0:3] = charges[q]

    def slot(q, carry):
        charge = picked[q].astype(BF16)
        for b in range(3):
            total = mm(charge[0:1], blocks[q, 0, b])
            total += mm(charge[1:2], blocks[q, 1, b])
            total += mm(charge[2:3], blocks[q, 2, b])
            near_sent[q, b : b + 1] = total
        return carry

    lax.fori_loop(0, SLOTS, slot, 0)
    near_copies = []
    for side, j in ((0, ROWS - 1), (1, 1)):
        for k in range(4):
            near_copies.append(
                pltpu.make_async_remote_copy(
                    near_sent.at[4 + 2 * k + side],
                    near_got.at[2 * k + side],
                    near_sem.at[0, 2 * k + side],
                    near_sem.at[1, 2 * k + side],
                    device_id=at_row(j),
                    device_id_type=MESH,
                )
            )
    for near_copy in near_copies:
        near_copy.start()

    loads[7].wait()
    below = jnp.zeros((32 - STENCIL, PANELS), F32)

    def halve(i, carry):
        start = pl.multiple_of(i * GROUP * PANELS, GROUP * PANELS)
        for k in range(GROUP):
            block = proj[:, pl.ds(start + k * PANELS, PANELS)]
            high, low = split(jnp.concatenate([block, below], axis=0))
            proj_high[i, k * 32 : (k + 1) * 32] = high
            proj_low[i, k * 32 : (k + 1) * 32] = low
        return carry

    lax.fori_loop(0, CLUSTERS // GROUP, halve, 0)

    w1, w2, w3, inverse, weighting = screen(row_index, col_index)

    def second_dimension(c, carry):
        whole(0, c, sent2, got2).wait_recv()
        modes[c] = forward(got2[c].reshape(G, G), *rows_of(0), *lanes_of(0), twiddle[0], twiddle[1])
        return carry

    lax.fori_loop(0, 3, second_dimension, 0)

    inner = (w1 * modes[0] + w2 * modes[1] + w3 * modes[2]) * inverse
    for c, w in enumerate((w1, w2, w3)):
        modes[c] = (modes[c] - w * inner) * weighting

    def second_back(c, carry):
        values = backward(modes[c], *rows_of(3), *lanes_of(0), twiddle[0], twiddle[1])
        sent3[c] = values.reshape(COLS, 32, G)
        to_all(1, c, sent3, got3, COLS, col_index, col_peer, at_col)
        return carry

    lax.fori_loop(0, 3, second_back, 0)

    def first_back(c, carry):
        whole(1, c, sent3, got3).wait_recv()
        values = backward(got3[c].reshape(G, G), *rows_of(2), *lanes_of(1), twiddle[2], twiddle[3])
        sent4[c] = values.reshape(WIDTH, DEPTH, 8, G)
        to_all(2, c, sent4, got4, WIDTH, x_index, x_peer, at_x)
        return carry

    lax.fori_loop(0, 3, first_back, 0)
    sent5[...] = jnp.zeros_like(sent5)

    for near_copy in near_copies:
        near_copy.wait()
    near_rows[...] = jnp.zeros_like(near_rows)
    row = lax.broadcasted_iota(jnp.int32, (CLUSTERS, CLUSTERS), 0)
    lane = lax.broadcasted_iota(jnp.int32, (CLUSTERS, CLUSTERS), 1)
    lands = jnp.zeros((CLUSTERS, CLUSTERS), F32)
    for q in range(SLOTS):
        lands = jnp.where((lane == q) & (row == landing[q]), 1.0, lands)
        for b in range(3):
            arrived = near_sent[q, b : b + 1] if q < 4 else near_got[q - 4, b : b + 1]
            near_rows[q : q + 1, b * PANELS : (b + 1) * PANELS] = arrived
    lands = lands.astype(BF16)
    high, low = split(near_rows[...])
    near_term[...] = mm(lands, high) + mm(lands, low)

    def sample(c, carry):
        whole(2, c, sent4, got4).wait_recv()

        def slab(i, carry):
            zs = z_peer(distance(DEPTH - 1 - i))
            here = got4[c, :, zs].reshape(32, G)
            shifted = jnp.concatenate([here] + [pltpu.roll(here, G - 32 * dx, 1) for dx in (1, 2)], axis=0)
            high, low = split(shifted)
            both = mm(high, hot[zs]) + mm(low, hot[zs])
            for dx in range(3):
                for dy in range(3):
                    part = both[dx * 32 : dx * 32 + 32, dy * CLUSTERS : (dy + 1) * CLUSTERS]
                    for dz in range(3):
                        point = 9 * dx + 3 * dy + dz
                        sent5[c, zs, point : point + 1] = jnp.sum(part * phases[zs, dz], axis=0, keepdims=True)

            @pl.when(i < DEPTH - 1)
            def _():
                copy(3, c, sent5.at[c, zs], got5.at[c, z_index], at_z(zs)).start()

            return carry

        lax.fori_loop(0, DEPTH, slab, 0, unroll=2)
        got5[c, z_index] = sent5[c, z_index]
        return carry

    lax.fori_loop(0, 3, sample, 0)

    def send_done(j, carry):
        slab_copy(j).wait_send()
        return carry

    lax.fori_loop(1, DEPTH, send_done, 0)
    planes.wait_send()

    def finish(c, carry):
        whole(0, c, sent2, got2).wait_send()
        whole(1, c, sent3, got3).wait_send()
        whole(2, c, sent4, got4).wait_send()
        whole(3, c, sent5, got5).wait()
        total = jnp.sum(got5[c], axis=0)
        turned = jnp.concatenate([total] * 4, axis=0).T
        both = jnp.concatenate([turned, turned], axis=1)
        both = jnp.where(own, both, jnp.zeros_like(both))
        high = both.astype(BF16).astype(F32)
        low = both - high
        for i in range(CLUSTERS // GROUP):
            at = slice(i * GROUP, (i + 1) * GROUP)
            values[i, c] = jnp.concatenate([high[at], low[at]], axis=0).astype(BF16)
        return carry

    own = (lax.broadcasted_iota(jnp.int32, (CLUSTERS, G), 0) & (GROUP - 1)) == (
        lax.broadcasted_iota(jnp.int32, (CLUSTERS, G), 1) >> 5
    )
    lax.fori_loop(0, 3, finish, 0)

    def project(i, carry):
        point_values = values[i].reshape(3 * 2 * GROUP, G)
        both = mm(point_values, proj_high[i]) + mm(point_values, proj_low[i])
        at = pl.ds(pl.multiple_of(i * GROUP, GROUP), GROUP)
        for c in range(3):
            far = both[c * 2 * GROUP : c * 2 * GROUP + GROUP] + both[c * 2 * GROUP + GROUP : (c + 1) * 2 * GROUP]
            far += near_term[at, c * PANELS : (c + 1) * PANELS]
            for k in range(GROUP):
                place = pl.multiple_of((i * GROUP + k) * PANELS, PANELS)
                out[c : c + 1, pl.ds(place, PANELS)] = far[k : k + 1]
        return carry

    lax.fori_loop(0, CLUSTERS // GROUP, project, 0, unroll=8)


VMEM = pl.BlockSpec(memory_space=pltpu.VMEM)
SMEM = pl.BlockSpec(memory_space=pltpu.SMEM)
ANY = pl.BlockSpec(memory_space=pl.ANY)
LIMIT = 60 * 1024 * 1024


def shape(dims, dtype=F32):
    return jax.ShapeDtypeStruct(dims, dtype)


def per_device(
    density, interp_weight, proj_weight, stencil_corner, near_tiles, pair_target, pair_landing, pair_count
):
    line, onward, rows_table, lanes_table, twiddle = (jnp.asarray(t) for t in make_tables())
    planes, by_cols = (WIDTH, DEPTH, 3, 8, G), (3, COLS, 32, G)
    by_width, by_depth = (3, WIDTH, DEPTH, 8, G), (3, DEPTH, 32, CLUSTERS)
    held = (density, interp_weight, proj_weight, line, onward, rows_table, lanes_table, twiddle, near_tiles)
    weights = pltpu.VMEM((CLUSTERS // GROUP, G, PANELS), BF16)
    return pl.pallas_call(
        whole_kernel,
        out_shape=shape((3, CLUSTERS * PANELS)),
        in_specs=[VMEM] + [SMEM] * 3 + [ANY] * 9,
        out_specs=VMEM,
        scratch_shapes=[
            *(pltpu.VMEM(array.shape, array.dtype) for array in held),
            pltpu.VMEM((PACKED, CLUSTERS), F32),
            pltpu.VMEM((SLOTS, 8, PANELS), F32),
            pltpu.VMEM((DEPTH, PACKED, CLUSTERS), F32),
            pltpu.VMEM((DEPTH, G, 3 * CLUSTERS), BF16),
            pltpu.VMEM((DEPTH, 3, 32, CLUSTERS), F32),
            pltpu.VMEM((576, 3 * CLUSTERS), BF16),
            pltpu.VMEM(planes, F32),
            pltpu.VMEM(planes, F32),
            pltpu.VMEM(by_cols, F32),
            pltpu.VMEM(by_cols, F32),
            pltpu.VMEM((3, G, G), F32),
            pltpu.VMEM(by_cols, F32),
            pltpu.VMEM(by_cols, F32),
            pltpu.VMEM(by_width, F32),
            pltpu.VMEM(by_width, F32),
            pltpu.VMEM(by_depth, F32),
            pltpu.VMEM(by_depth, F32),
            pltpu.VMEM((SLOTS, 8, PANELS), F32),
            pltpu.VMEM((8, 8, PANELS), F32),
            pltpu.VMEM((CLUSTERS, 3 * PANELS), F32),
            pltpu.VMEM((CLUSTERS, 3 * PANELS), F32),
            weights,
            weights,
            pltpu.VMEM((CLUSTERS // GROUP, 3, 2 * GROUP, G), BF16),
            pltpu.SemaphoreType.DMA((PIECES + 8,)),
            pltpu.SemaphoreType.DMA((DEPTH,)),
            pltpu.SemaphoreType.DMA((DEPTH,)),
            pltpu.SemaphoreType.DMA((2,)),
            pltpu.SemaphoreType.DMA((4, 3)),
            pltpu.SemaphoreType.DMA((4, 3)),
            pltpu.SemaphoreType.DMA((2, 8)),
        ],
        compiler_params=pltpu.CompilerParams(
            vmem_limit_bytes=LIMIT, collective_id=0, has_side_effects=True
        ),
    )(stencil_corner, pair_target, pair_landing, pair_count, *held)


def solution(mesh):
    flat = P(None, ("row", "col"))
    slots = P(("row", "col"))
    in_specs = (flat, flat, flat, flat, P(("row", "col"), None, None, None, None), slots, slots, slots)
    return jax.shard_map(
        per_device, mesh=mesh, in_specs=in_specs, out_specs=flat, check_vma=False
    )
```

```python
import math

import jax
import jax.numpy as jnp
import ml_dtypes
import numpy as np
from jax import lax
from jax.experimental import pallas as pl
from jax.experimental.pallas import tpu as pltpu
from jax.sharding import PartitionSpec as P

G = 256
STENCIL = 27
ROWS = 32
COLS = 8
DEPTH = 8
WIDTH = 4
PACKED = 88
PIECES = 4
GROUP = 8
HALF = 128
CLUSTERS = 128
PANELS = 128
SLOTS = 12
BF16 = jnp.bfloat16
F32 = jnp.float32
MESH = pl.DeviceIdType.MESH
FACTOR = 1.0 / math.sqrt(ROWS * COLS * CLUSTERS * PANELS)


def halves(table):
    table = np.asarray(table, np.float64)
    high = table.astype(np.float32).astype(ml_dtypes.bfloat16)
    low = (table - high.astype(np.float64)).astype(np.float32).astype(ml_dtypes.bfloat16)
    return np.stack([high, low])


def rotation(theta):
    cosine, sine = np.cos(theta), np.sin(theta)
    return np.array([[cosine, sine], [-sine, cosine]])


def make_tables():
    two_pi = 2 * np.pi
    bins, cells = np.arange(128), np.arange(G)
    theta = two_pi * (bins[:, None] * cells[None, :] % G) / G
    line = np.stack([np.cos(theta), -np.sin(theta)]).reshape(2, DEPTH, 4, 4, G)
    line = line.transpose(1, 2, 0, 3, 4).reshape(DEPTH, 32, G)
    line = halves(line).transpose(1, 0, 2, 3).reshape(DEPTH, 64, G)
    step = 2 * np.pi * np.arange(128).reshape(DEPTH, 4, 1, 4) / G
    onward = np.stack([np.cos(step) + np.zeros((2, 1)), np.sin(step) * np.array([[1.0], [-1.0]])], axis=1)
    onward = np.broadcast_to(onward.reshape(DEPTH, 2, 32, 1), (DEPTH, 2, 32, CLUSTERS)).astype(np.float32)
    eight = np.arange(8)
    wide = np.arange(32)
    turn8 = rotation(two_pi * (eight[:, None] * eight[None, :] % 8) / 8)
    turn32 = rotation(two_pi * (wide[:, None] * wide[None, :] % 32) / 32)
    second = np.einsum("oipc,hg,lm->pholcgim", turn8, np.eye(2), np.eye(4)).reshape(HALF, HALF)
    by_block = turn32.reshape(2, 2, 16, 2, DEPTH, WIDTH)
    first = []
    for z in range(DEPTH):
        order = [(z + d) % DEPTH for d in (0, 7, 1, 6, 2, 5, 3, 4)]
        mine = by_block[:, :, :, :, order]
        first_a = np.einsum("oihlabx,km->holkxaibm", mine.reshape(2, 2, 16, 2, 4, 2, WIDTH), np.eye(2))
        first_b = np.einsum("oihlabx,km->holkxmaib", mine.reshape(2, 2, 16, 2, 2, 4, WIDTH), np.eye(2))
        both = [t.reshape(HALF, HALF) for t in (first_a, first_b)]
        first.append(np.stack([halves(t) for t in (*both, both[0].T, both[1].T)]))
    first = np.stack(first)
    lane32 = [np.kron(np.eye(8), f(two_pi * (wide[:, None] * wide[None, :] % 32) / 32)) for f in (np.cos, np.sin)]
    lane8 = [np.kron(f(two_pi * (eight[:, None] * eight[None, :] % 8) / 8), np.eye(32)) for f in (np.cos, np.sin)]
    row = np.arange(HALF)
    lane = np.arange(G)
    part_sign = np.where(row // 4 % 2 == 0, 1.0, -1.0)[:, None]
    twist_y = two_pi * ((row // 16)[:, None] * (lane % 32)[None, :]) / G
    twist_x = two_pi * ((row // 8 * 2 + row // 2 % 2)[:, None] * (lane // 32)[None, :]) / G
    twiddle = np.stack(
        [np.cos(twist_y), part_sign * np.sin(twist_y), np.cos(twist_x), part_sign * np.sin(twist_x)]
    ).astype(np.float32)
    second = np.stack([halves(t) for t in (second, second.T)])
    lanes_table = np.stack([halves(np.concatenate(t, axis=1)) for t in (lane32, lane8)])
    return line, np.ascontiguousarray(onward), first, second, lanes_table, twiddle


def split(values):
    high = values.astype(BF16)
    return high, (values - high.astype(F32)).astype(BF16)


def mm(a, b):
    return jnp.dot(a, b, preferred_element_type=F32)


def mm_nt(a, b):
    return lax.dot_general(a, b, (((1,), (1,)), ((), ())), preferred_element_type=F32)


def swap(values):
    grouped = values.reshape(values.shape[0] // 8, 8, values.shape[1])
    return pltpu.roll(grouped, 4, 1).reshape(values.shape)


def on_rows(table_high, table_low, values):
    high, low = split(values)
    both = mm(jnp.concatenate([table_high, table_low], axis=0), high)
    return both[:HALF] + (both[HALF:] + mm(table_high, low))


def on_lanes(values, table_high, table_low, sign):
    high, low = split(values)
    both = mm(jnp.concatenate([high, low], axis=0), table_high)
    both = both[:HALF] + (both[HALF:] + mm(high, table_low))
    return both[:, :G] + sign * swap(both[:, G:])


def row_sums(tiles):
    row = lax.broadcasted_iota(jnp.int32, (8, CLUSTERS), 0)
    for step in (4, 2, 1):
        clear = (row & step) == 0
        merged = []
        for j in range(step):
            here = jnp.where(clear, tiles[j], tiles[j + step])
            there = jnp.where(clear, tiles[j + step], tiles[j])
            if step == 4:
                moved = pltpu.roll(there, 4, 0)
            else:
                moved = jnp.where(clear, pltpu.roll(there, 8 - step, 0), pltpu.roll(there, step, 0))
            merged.append(here + moved)
        tiles = merged
    return tiles[0]


def signs(direction):
    row = lax.broadcasted_iota(jnp.int32, (HALF, G), 0)
    return jnp.where((row & 4) == 0, direction, -direction).astype(F32)


def forward(values, rows_high, rows_low, lanes_high, lanes_low, cosines, sines):
    values = on_rows(rows_high, rows_low, values)
    values = values * cosines + swap(values) * sines
    return on_lanes(values, lanes_high, lanes_low, signs(1.0))


def backward(values, rows_high, rows_low, lanes_high, lanes_low, cosines, sines):
    values = on_lanes(values, lanes_high, lanes_low, signs(-1.0))
    values = values * cosines - swap(values) * sines
    return on_rows(rows_high, rows_low, values)


def wave(index):
    return jnp.where(index < G // 2, index, index - G).astype(F32)


def wavevectors(row_index, col_index):
    z_index, x_index = row_index // WIDTH, lax.rem(row_index, WIDTH)
    row = lax.broadcasted_iota(jnp.int32, (HALF, G), 0)
    lane = lax.broadcasted_iota(jnp.int32, (HALF, G), 1)
    low, above, q = (row >> 1) & 1, lane & -32, 8 * (lane & 31)
    ours = 4 * col_index + 2 * ((row >> 3) & 1) + low + above, (row >> 4) + q, 16 * z_index + 2 * x_index + (row & 1)
    theirs = 2 * (row >> 3) + low + above, 2 * x_index + (row & 1) + q, 16 * z_index + 8 + col_index + 0 * row
    return ours, theirs


def screen(m1, m2, m3):
    w1, w2, w3 = wave(m1), wave(m2), m3.astype(F32)
    squared = w1 * w1 + w2 * w2 + w3 * w3
    kept = jnp.where((m1 == G // 2) | (m2 == G // 2), 0.0, FACTOR).astype(F32)
    fold = jnp.where(m3 == 0, 1.0, 2.0).astype(F32)
    return w1, w2, w3, 1.0 / jnp.maximum(squared, 1.0), kept * fold / (squared + 0.5)


def spread(weight, density, first, sums):
    lane = lax.broadcasted_iota(jnp.int32, (STENCIL, CLUSTERS), 1)
    group = 8

    def some(i, sums):
        start = pl.multiple_of(i * group * PANELS, group * PANELS)
        block = weight[:, pl.ds(start, group * PANELS)]
        charge = density[:, pl.ds(start, group * PANELS)]
        sums = list(sums)
        for c in range(3):
            product = block * charge[c : c + 1]
            for k in range(group):
                total = jnp.sum(product[:, k * PANELS : (k + 1) * PANELS], axis=1, keepdims=True)
                sums[c] = jnp.where(lane == i * group + k, total, sums[c])
        return tuple(sums)

    groups = CLUSTERS // PIECES // group
    return lax.fori_loop(first * groups, (first + 1) * groups, some, sums, unroll=4)


def whole_kernel(
    corner, target, landing, count,
    density_in, interp_in, proj_in, line_in, onward_in, first_in, second_in, lanes_in, twiddle_in, tiles_in,
    out,
    density, interp, proj, line, onward, first, second, lanes_table, twiddle, blocks,
    packed, picked, gathered, hot, phases, upper, plane,
    sent1a, got1a, sent1b, got1b, sent2a, got2a, sent2b, got2b, modes_a, modes_b,
    sent3a, got3a, sent3b, got3b, sent4a, got4a, sent4b, got4b, sent5, got5,
    near_sent, near_got, near_rows, near_term, proj_high, proj_low, values,
    load_sem, slab_send, slab_recv, plane_sem, send_sem, recv_sem, near_sem,
):
    row_index, col_index = lax.axis_index("row"), lax.axis_index("col")
    z_index, x_index = row_index // WIDTH, lax.rem(row_index, WIDTH)
    width = CLUSTERS * PANELS // PIECES

    def piece(k):
        at = pl.ds(k * width, width)
        return pltpu.make_async_copy(interp_in.at[:, at], interp.at[:, at], load_sem.at[k])

    loads = [
        pltpu.make_async_copy(source, target_ref, load_sem.at[PIECES + k])
        for k, (source, target_ref) in enumerate(
            (
                (density_in, density),
                (line_in, line),
                (onward_in, onward),
                (first_in.at[lax.axis_index("row") // WIDTH], first),
                (second_in, second),
                (lanes_in, lanes_table),
                (twiddle_in, twiddle),
                (tiles_in, blocks),
                (proj_in, proj),
            )
        )
    ]
    loads[0].start()
    for k in range(PIECES):
        piece(k).start()

    def z_peer(j):
        return lax.rem(z_index + j, DEPTH)

    def x_peer(j):
        return lax.rem(x_index + j, WIDTH)

    def col_peer(j):
        return lax.rem(col_index + j, COLS)

    def at_z(peer):
        return (peer * WIDTH + x_index, col_index)

    def at_x(peer):
        return (z_index * WIDTH + peer, col_index)

    def at_col(peer):
        return (row_index, peer)

    def at_row(j):
        return (lax.rem(row_index + j, ROWS), col_index)

    barrier = pltpu.get_barrier_semaphore()

    def greet(device):
        pl.semaphore_signal(barrier, inc=1, device_id=device, device_id_type=MESH)

    def greet_z(j, carry):
        greet(at_z(z_peer(j)))
        return carry

    def greet_x(j, carry):
        greet(at_x(x_peer(j)))
        return carry

    def greet_col(j, carry):
        greet(at_col(col_peer(j)))
        return carry

    lax.fori_loop(1, DEPTH, greet_z, 0)
    lax.fori_loop(1, WIDTH, greet_x, 0)
    lax.fori_loop(1, COLS, greet_col, 0)
    greet(at_row(1))
    greet(at_row(ROWS - 1))
    loads[0].wait()
    sums = (jnp.zeros((STENCIL, CLUSTERS), F32),) * 3
    for k in range(PIECES):
        piece(k).wait()
        if k == 0:
            for load in loads[1:]:
                load.start()
        sums = spread(interp, density, k, sums)
    corners = corner[...]
    packed[80:PACKED] = jnp.zeros((PACKED - 80, CLUSTERS), F32)
    for c in range(3):
        packed[c * STENCIL : (c + 1) * STENCIL] = sums[c]
    packed[81:82] = ((corners[0:1] - row_index * 8) * 32 + (corners[1:2] - col_index * 32)).astype(F32)
    packed[82:83] = corners[2:3].astype(F32)
    pl.semaphore_wait(barrier, DEPTH + WIDTH + COLS - 3 + 2)

    def distance(i):
        odd = lax.rem(i, 2)
        return odd * (DEPTH - (i + 1) // 2) + (1 - odd) * (i // 2)

    def slab_copy(i):
        return pltpu.make_async_remote_copy(
            packed,
            gathered.at[z_index],
            slab_send.at[i],
            slab_recv.at[i],
            device_id=at_z(z_peer(DEPTH - distance(i))),
            device_id_type=MESH,
        )

    slab_copy(1).start()
    slab_copy(2).start()
    gathered[z_index] = packed[...]

    def plane_copy(kind, source, target, device):
        return pltpu.make_async_remote_copy(
            source, target, plane_sem.at[kind, 0], plane_sem.at[kind, 1], device_id=device, device_id_type=MESH
        )

    cell = lax.broadcasted_iota(jnp.int32, (G, CLUSTERS), 0).astype(F32)

    def build(zs, place):
        local, depth = gathered[zs, 81:82], gathered[zs, 82:83]
        at = jnp.where(cell == depth, 1.0, 0.0).astype(BF16)
        both = mm(line[z_index], at)
        turn = [both[:32] + both[32:]]
        for dz in range(1, 3):
            turn.append(turn[-1] * onward[z_index, 0] + swap(turn[-1]) * onward[z_index, 1])
        for dz in range(3):
            phases[zs, dz] = turn[dz]
        for dy in range(3):
            here = jnp.where(cell == local + float(dy), 1.0, 0.0).astype(BF16)
            hot[zs, :, dy * CLUSTERS : (dy + 1) * CLUSTERS] = here
        for dx in range(3):
            for c in range(3):
                for dy in range(3):
                    at = c * STENCIL + 9 * dx + 3 * dy
                    value = turn[0] * gathered[zs, at : at + 1]
                    value += turn[1] * gathered[zs, at + 1 : at + 2]
                    value += turn[2] * gathered[zs, at + 2 : at + 3]
                    high, low = split(value)
                    top = dx * 192 + c * 64
                    upper[top : top + 32, dy * CLUSTERS : (dy + 1) * CLUSTERS] = high
                    upper[top + 32 : top + 64, dy * CLUSTERS : (dy + 1) * CLUSTERS] = low
        total = mm_nt(upper[...], hot[zs])
        for c in range(3):
            sum_of = jnp.zeros((32, G), F32)
            for dx in range(3):
                top = dx * 192 + c * 64
                part = total[top : top + 32] + total[top + 32 : top + 64]
                sum_of += pltpu.roll(part, 32 * dx, 1) if dx else part
            plane[place, c] = sum_of.reshape(4, 8, G)

    tile_row = lax.broadcasted_iota(jnp.int32, (8, G), 0)

    def shifted(tile, by):
        return pltpu.roll(tile, by % 8, 0) if by % 8 else tile

    def mix2(tiles, to):
        return jnp.where((tile_row & 2) == 0, shifted(tiles[0], -2 * to), shifted(tiles[1], 2 - 2 * to))

    def mix4(tiles, to):
        mixed = shifted(tiles[0], -to)
        for j in range(1, 4):
            mixed = jnp.where((tile_row & 3) == j, shifted(tiles[j], j - to), mixed)
        return mixed

    def send_quad(quad):
        for c in range(3):
            for peer in range(WIDTH):
                for pair in range(2):
                    tiles = [plane[2 * pair + b, c, peer // 2] for b in range(2)]
                    sent1a[peer, 2 * quad + pair, c] = mix2(tiles, peer % 2)
            for peer in range(COLS):
                tiles = [plane[j, c, 2 + peer // 4] for j in range(4)]
                sent1b[peer, quad, c] = mix4(tiles, peer % 4)

        def send_a(j, carry):
            peer = x_peer(j)
            pair = pl.ds(2 * quad, 2)
            plane_copy(0, sent1a.at[peer, pair], got1a.at[x_index, pair], at_x(peer)).start()
            return carry

        def send_b(j, carry):
            peer = col_peer(j)
            plane_copy(1, sent1b.at[peer, quad], got1b.at[col_index, quad], at_col(peer)).start()
            return carry

        lax.fori_loop(1, WIDTH, send_a, 0)
        lax.fori_loop(1, COLS, send_b, 0)

    loads[1].wait()
    loads[2].wait()

    def next_slab(i, carry):
        @pl.when(i == 1)
        def _():
            slab_copy(3).start()
            slab_copy(4).start()

        @pl.when(i >= 1)
        def _():
            slab_copy(i).wait_recv()

        @pl.when(i == 2)
        def _():
            slab_copy(5).start()
            slab_copy(6).start()

        @pl.when(i == 4)
        def _():
            slab_copy(7).start()

        build(z_peer(distance(i)), lax.rem(i, 4))
        return carry

    def four_slabs(quad, carry):
        lax.fori_loop(4 * quad, 4 * quad + 4, next_slab, 0)
        send_quad(quad)
        return carry

    lax.fori_loop(0, 2, four_slabs, 0)
    got1a[x_index] = sent1a[x_index]
    got1b[col_index] = sent1b[col_index]

    def copy(stage, c, source, target, device):
        return pltpu.make_async_remote_copy(
            source,
            target,
            send_sem.at[stage, c],
            recv_sem.at[stage, c],
            device_id=device,
            device_id_type=MESH,
        )

    def to_all(stage, c, source, target, count, mine, peer_of, device_of):
        def one(j, carry):
            peer = peer_of(j)
            copy(stage, c, source.at[c, peer], target.at[c, mine], device_of(peer)).start()
            return carry

        lax.fori_loop(1, count, one, 0)
        target[c, mine] = source[c, mine]

    def whole(stage, c, source, target):
        peers = source.shape[1] - 1
        return copy(stage, c, source.at[c, pl.ds(0, peers)], target.at[c, pl.ds(0, peers)], at_row(1))

    def first_of(k):
        return first[k, 0], first[k, 1]

    def second_of(k):
        return second[k, 0], second[k, 1]

    def lanes_of(k):
        return lanes_table[k, 0], lanes_table[k, 1]

    def first_forward(values, k):
        return forward(values.reshape(HALF, G), *first_of(k), *lanes_of(1), twiddle[2], twiddle[3])

    def second_forward(values):
        return forward(values.reshape(HALF, G), *second_of(0), *lanes_of(0), twiddle[0], twiddle[1])

    def first_backward(values, k):
        return backward(values.reshape(HALF, G), *first_of(2 + k), *lanes_of(1), twiddle[2], twiddle[3])

    def second_backward(values):
        return backward(values.reshape(HALF, G), *second_of(1), *lanes_of(0), twiddle[0], twiddle[1])

    def to_cols(stage, c, source, target):
        to_all(stage, c, source, target, COLS, col_index, col_peer, at_col)

    def to_width(stage, c, source, target):
        to_all(stage, c, source, target, WIDTH, x_index, x_peer, at_x)

    waits = (
        plane_copy(0, sent1a.at[pl.ds(0, WIDTH - 1)], got1a.at[pl.ds(0, WIDTH - 1)], at_x(x_peer(1))),
        plane_copy(1, sent1b.at[pl.ds(0, COLS - 1)], got1b.at[pl.ds(0, COLS - 1)], at_col(col_peer(1))),
    )
    for load in loads[3:7]:
        load.wait()
    for wait in waits:
        wait.wait_recv()

    def step_one(c, carry):
        sent2a[c] = first_forward(got1a[:, :, c], 0).reshape(COLS, 16, G)
        to_cols(0, c, sent2a, got2a)
        sent2b[c] = second_forward(got1b[:, :, c]).reshape(WIDTH, 32, G)
        to_width(1, c, sent2b, got2b)
        return carry

    lax.fori_loop(0, 3, step_one, 0, unroll=3)

    loads[7].wait()
    near_sent[...] = jnp.zeros_like(near_sent)
    picked[...] = jnp.zeros_like(picked)
    nobody = jnp.full((3, PANELS), -1, jnp.int32)
    wanted = [
        jnp.where(jnp.full((3, PANELS), q, jnp.int32) < count[0], jnp.full((3, PANELS), target[q], jnp.int32), nobody)
        for q in range(SLOTS)
    ]

    def pick(i, charges):
        charges = list(charges)
        for k in range(GROUP):
            cluster = i * GROUP + k
            charge = density[:, pl.ds(pl.multiple_of(cluster * PANELS, PANELS), PANELS)]
            for q in range(SLOTS):
                charges[q] = jnp.where(wanted[q] == cluster, charge, charges[q])
        return tuple(charges)

    charges = lax.fori_loop(0, CLUSTERS // GROUP, pick, (jnp.zeros((3, PANELS), F32),) * SLOTS)
    for q in range(SLOTS):
        picked[q, 0:3] = charges[q]

    def slot(q, carry):
        charge = picked[q].astype(BF16)
        for b in range(3):
            total = mm(charge[0:1], blocks[q, 0, b])
            total += mm(charge[1:2], blocks[q, 1, b])
            total += mm(charge[2:3], blocks[q, 2, b])
            near_sent[q, b : b + 1] = total
        return carry

    lax.fori_loop(0, SLOTS, slot, 0)
    near_copies = []
    for side, j in ((0, ROWS - 1), (1, 1)):
        for k in range(4):
            near_copies.append(
                pltpu.make_async_remote_copy(
                    near_sent.at[4 + 2 * k + side],
                    near_got.at[2 * k + side],
                    near_sem.at[0, 2 * k + side],
                    near_sem.at[1, 2 * k + side],
                    device_id=at_row(j),
                    device_id_type=MESH,
                )
            )
    for near_copy in near_copies:
        near_copy.start()

    loads[8].wait()
    below = jnp.zeros((32 - STENCIL, PANELS), F32)

    def halve(i, carry):
        start = pl.multiple_of(i * GROUP * PANELS, GROUP * PANELS)
        for k in range(GROUP):
            block = proj[:, pl.ds(start + k * PANELS, PANELS)]
            high, low = split(jnp.concatenate([block, below], axis=0))
            proj_high[i, k * 32 : (k + 1) * 32] = high
            proj_low[i, k * 32 : (k + 1) * 32] = low
        return carry

    lax.fori_loop(0, CLUSTERS // GROUP, halve, 0)

    screens = [screen(*index) for index in wavevectors(row_index, col_index)]

    def step_two(c, carry):
        whole(0, c, sent2a, got2a).wait_recv()
        whole(1, c, sent2b, got2b).wait_recv()
        modes_a[c] = second_forward(got2a[c])
        modes_b[c] = first_forward(got2b[c], 1)
        return carry

    lax.fori_loop(0, 3, step_two, 0)

    for modes, (w1, w2, w3, inverse, weighting) in zip((modes_a, modes_b), screens):
        inner = (w1 * modes[0] + w2 * modes[1] + w3 * modes[2]) * inverse
        for c, w in enumerate((w1, w2, w3)):
            modes[c] = (modes[c] - w * inner) * weighting

    def step_three(c, carry):
        sent3a[c] = second_backward(modes_a[c]).reshape(COLS, 16, G)
        to_cols(2, c, sent3a, got3a)
        sent3b[c] = first_backward(modes_b[c], 1).reshape(WIDTH, 32, G)
        to_width(3, c, sent3b, got3b)
        return carry

    lax.fori_loop(0, 3, step_three, 0, unroll=3)

    def step_four(c, carry):
        whole(2, c, sent3a, got3a).wait_recv()
        whole(3, c, sent3b, got3b).wait_recv()
        sent4a[c] = first_backward(got3a[c], 0).reshape(WIDTH, 4, 8, G)
        to_width(4, c, sent4a, got4a)
        sent4b[c] = second_backward(got3b[c]).reshape(COLS, 2, 8, G)
        to_cols(5, c, sent4b, got4b)
        return carry

    lax.fori_loop(0, 3, step_four, 0)

    for near_copy in near_copies:
        near_copy.wait()
    near_rows[...] = jnp.zeros_like(near_rows)
    row = lax.broadcasted_iota(jnp.int32, (CLUSTERS, CLUSTERS), 0)
    lane = lax.broadcasted_iota(jnp.int32, (CLUSTERS, CLUSTERS), 1)
    lands = jnp.zeros((CLUSTERS, CLUSTERS), F32)
    for q in range(SLOTS):
        lands = jnp.where((lane == q) & (row == landing[q]), 1.0, lands)
        for b in range(3):
            arrived = near_sent[q, b : b + 1] if q < 4 else near_got[q - 4, b : b + 1]
            near_rows[q : q + 1, b * PANELS : (b + 1) * PANELS] = arrived
    lands = lands.astype(BF16)
    high, low = split(near_rows[...])
    near_term[...] = mm(lands, high) + mm(lands, low)

    def sample(c, carry):
        whole(4, c, sent4a, got4a).wait_recv()
        whole(5, c, sent4b, got4b).wait_recv()

        def unpack(quad, carry):
            for j in range(4):
                pair, b = 2 * quad + j // 2, j % 2
                for high in range(2):
                    plane[4 * quad + j, 0, high] = mix2([got4a[c, 2 * high + k, pair] for k in range(2)], b)
                    plane[4 * quad + j, 0, 2 + high] = mix4([got4b[c, 4 * high + k, quad] for k in range(4)], j)
            return carry

        lax.fori_loop(0, 2, unpack, 0)

        def slab(i, carry):
            step = DEPTH - 1 - i
            zs = z_peer(distance(step))
            here = plane[step, 0].reshape(32, G)
            around = jnp.concatenate([here] + [pltpu.roll(here, G - 32 * dx, 1) for dx in (1, 2)], axis=0)
            high, low = split(around)
            both = mm(jnp.concatenate([high, low], axis=0), hot[zs])
            both = both[:96] + both[96:]
            parts = []
            for dx in range(3):
                for dy in range(3):
                    part = both[dx * 32 : dx * 32 + 32, dy * CLUSTERS : (dy + 1) * CLUSTERS]
                    for dz in range(3):
                        product = (part * phases[zs, dz]).reshape(4, 8, CLUSTERS)
                        parts.append((product[0] + product[1]) + (product[2] + product[3]))
            parts += [jnp.zeros((8, CLUSTERS), F32)] * (32 - STENCIL)
            for k in range(4):
                sent5[c, zs, 8 * k : 8 * k + 8] = row_sums(parts[8 * k : 8 * k + 8])

            @pl.when(i < DEPTH - 1)
            def _():
                copy(6, c, sent5.at[c, zs], got5.at[c, z_index], at_z(zs)).start()

            return carry

        lax.fori_loop(0, DEPTH, slab, 0, unroll=2)
        got5[c, z_index] = sent5[c, z_index]
        return carry

    lax.fori_loop(0, 3, sample, 0)

    def send_done(j, carry):
        slab_copy(j).wait_send()
        return carry

    lax.fori_loop(1, DEPTH, send_done, 0)
    for wait in waits:
        wait.wait_send()

    def finish(c, carry):
        whole(0, c, sent2a, got2a).wait_send()
        whole(1, c, sent2b, got2b).wait_send()
        whole(2, c, sent3a, got3a).wait_send()
        whole(3, c, sent3b, got3b).wait_send()
        whole(4, c, sent4a, got4a).wait_send()
        whole(5, c, sent4b, got4b).wait_send()
        whole(6, c, sent5, got5).wait()
        total = jnp.sum(got5[c], axis=0)
        turned = jnp.concatenate([total] * 4, axis=0).T
        both = jnp.concatenate([turned, turned], axis=1)
        both = jnp.where(own, both, jnp.zeros_like(both))
        high = both.astype(BF16).astype(F32)
        low = both - high
        for i in range(CLUSTERS // GROUP):
            at = slice(i * GROUP, (i + 1) * GROUP)
            values[i, c] = jnp.concatenate([high[at], low[at]], axis=0).astype(BF16)
        return carry

    own = (lax.broadcasted_iota(jnp.int32, (CLUSTERS, G), 0) & (GROUP - 1)) == (
        lax.broadcasted_iota(jnp.int32, (CLUSTERS, G), 1) >> 5
    )
    lax.fori_loop(0, 3, finish, 0)

    def project(i, carry):
        point_values = values[i].reshape(3 * 2 * GROUP, G)
        both = mm(point_values, proj_high[i]) + mm(point_values, proj_low[i])
        at = pl.ds(pl.multiple_of(i * GROUP, GROUP), GROUP)
        for c in range(3):
            far = both[c * 2 * GROUP : c * 2 * GROUP + GROUP] + both[c * 2 * GROUP + GROUP : (c + 1) * 2 * GROUP]
            far += near_term[at, c * PANELS : (c + 1) * PANELS]
            for k in range(GROUP):
                place = pl.multiple_of((i * GROUP + k) * PANELS, PANELS)
                out[c : c + 1, pl.ds(place, PANELS)] = far[k : k + 1]
        return carry

    lax.fori_loop(0, CLUSTERS // GROUP, project, 0, unroll=8)


VMEM = pl.BlockSpec(memory_space=pltpu.VMEM)
SMEM = pl.BlockSpec(memory_space=pltpu.SMEM)
ANY = pl.BlockSpec(memory_space=pl.ANY)
LIMIT = 60 * 1024 * 1024


def shape(dims, dtype=F32):
    return jax.ShapeDtypeStruct(dims, dtype)


def per_device(
    density, interp_weight, proj_weight, stencil_corner, near_tiles, pair_target, pair_landing, pair_count
):
    line, onward, first, second, lanes_table, twiddle = (jnp.asarray(t) for t in make_tables())
    planes_a, planes_b = pltpu.VMEM((WIDTH, 4, 3, 8, G), F32), pltpu.VMEM((COLS, 2, 3, 8, G), F32)
    by_cols, by_width = pltpu.VMEM((3, COLS, 16, G), F32), pltpu.VMEM((3, WIDTH, 32, G), F32)
    modes = pltpu.VMEM((3, HALF, G), F32)
    last_a, last_b = pltpu.VMEM((3, WIDTH, 4, 8, G), F32), pltpu.VMEM((3, COLS, 2, 8, G), F32)
    by_depth = (3, DEPTH, 32, CLUSTERS)
    held = (density, interp_weight, proj_weight, line, onward, first, second, lanes_table, twiddle, near_tiles)
    weights = pltpu.VMEM((CLUSTERS // GROUP, G, PANELS), BF16)
    return pl.pallas_call(
        whole_kernel,
        out_shape=shape((3, CLUSTERS * PANELS)),
        in_specs=[VMEM] + [SMEM] * 3 + [ANY] * 10,
        out_specs=VMEM,
        scratch_shapes=[
            *(pltpu.VMEM(array.shape[1:] if array is first else array.shape, array.dtype) for array in held),
            pltpu.VMEM((PACKED, CLUSTERS), F32),
            pltpu.VMEM((SLOTS, 8, PANELS), F32),
            pltpu.VMEM((DEPTH, PACKED, CLUSTERS), F32),
            pltpu.VMEM((DEPTH, G, 3 * CLUSTERS), BF16),
            pltpu.VMEM((DEPTH, 3, 32, CLUSTERS), F32),
            pltpu.VMEM((576, 3 * CLUSTERS), BF16),
            pltpu.VMEM((DEPTH, 3, 4, 8, G), F32),
            *(planes_a, planes_a, planes_b, planes_b),
            *(by_cols, by_cols, by_width, by_width, modes, modes),
            *(by_cols, by_cols, by_width, by_width),
            *(last_a, last_a, last_b, last_b),
            pltpu.VMEM(by_depth, F32),
            pltpu.VMEM(by_depth, F32),
            pltpu.VMEM((SLOTS, 8, PANELS), F32),
            pltpu.VMEM((8, 8, PANELS), F32),
            pltpu.VMEM((CLUSTERS, 3 * PANELS), F32),
            pltpu.VMEM((CLUSTERS, 3 * PANELS), F32),
            weights,
            weights,
            pltpu.VMEM((CLUSTERS // GROUP, 3, 2 * GROUP, G), BF16),
            pltpu.SemaphoreType.DMA((PIECES + 9,)),
            pltpu.SemaphoreType.DMA((DEPTH,)),
            pltpu.SemaphoreType.DMA((DEPTH,)),
            pltpu.SemaphoreType.DMA((2, 2)),
            pltpu.SemaphoreType.DMA((7, 3)),
            pltpu.SemaphoreType.DMA((7, 3)),
            pltpu.SemaphoreType.DMA((2, 8)),
        ],
        compiler_params=pltpu.CompilerParams(
            vmem_limit_bytes=LIMIT, collective_id=0, has_side_effects=True
        ),
    )(stencil_corner, pair_target, pair_landing, pair_count, *held)


def solution(mesh):
    flat = P(None, ("row", "col"))
    slots = P(("row", "col"))
    in_specs = (flat, flat, flat, flat, P(("row", "col"), None, None, None, None), slots, slots, slots)
    return jax.shard_map(
        per_device, mesh=mesh, in_specs=in_specs, out_specs=flat, check_vma=False
    )
```

```python
import math

import jax
import jax.numpy as jnp
import ml_dtypes
import numpy as np
from jax import lax
from jax.experimental import pallas as pl
from jax.experimental.pallas import tpu as pltpu
from jax.sharding import PartitionSpec as P

G = 256
STENCIL = 27
ROWS = 32
COLS = 8
DEPTH = 8
WIDTH = 4
PACKED = 88
PIECES = 4
GROUP = 8
HALF = 128
CLUSTERS = 128
PANELS = 128
SLOTS = 12
BF16 = jnp.bfloat16
F32 = jnp.float32
MESH = pl.DeviceIdType.MESH
FACTOR = 1.0 / math.sqrt(ROWS * COLS * CLUSTERS * PANELS)


def halves(table):
    table = np.asarray(table, np.float64)
    high = table.astype(np.float32).astype(ml_dtypes.bfloat16)
    low = (table - high.astype(np.float64)).astype(np.float32).astype(ml_dtypes.bfloat16)
    return np.stack([high, low])


def rotation(theta):
    cosine, sine = np.cos(theta), np.sin(theta)
    return np.array([[cosine, sine], [-sine, cosine]])


def make_tables():
    two_pi = 2 * np.pi
    bins, cells = np.arange(128), np.arange(G)
    theta = two_pi * (bins[:, None] * cells[None, :] % G) / G
    line = np.stack([np.cos(theta), -np.sin(theta)]).reshape(2, DEPTH, 4, 4, G)
    line = line.transpose(1, 2, 0, 3, 4).reshape(DEPTH, 32, G)
    line = halves(line).transpose(1, 0, 2, 3).reshape(DEPTH, 64, G)
    step = 2 * np.pi * np.arange(128).reshape(DEPTH, 4, 1, 4) / G
    onward = np.stack([np.cos(step) + np.zeros((2, 1)), np.sin(step) * np.array([[1.0], [-1.0]])], axis=1)
    onward = np.broadcast_to(onward.reshape(DEPTH, 2, 32, 1), (DEPTH, 2, 32, CLUSTERS)).astype(np.float32)
    eight = np.arange(8)
    wide = np.arange(32)
    turn8 = rotation(two_pi * (eight[:, None] * eight[None, :] % 8) / 8)
    turn32 = rotation(two_pi * (wide[:, None] * wide[None, :] % 32) / 32)
    second = np.einsum("oipc,hg,lm->pholcgim", turn8, np.eye(2), np.eye(4)).reshape(HALF, HALF)
    by_block = turn32.reshape(2, 2, 16, 2, DEPTH, WIDTH)
    first = []
    for z in range(DEPTH):
        order = [(z + d) % DEPTH for d in (0, 7, 1, 6, 2, 5, 3, 4)]
        mine = by_block[:, :, :, :, order]
        first_a = np.einsum("oihlabx,km->holkxaibm", mine.reshape(2, 2, 16, 2, 4, 2, WIDTH), np.eye(2))
        first_b = np.einsum("oihlabx,km->holkxmaib", mine.reshape(2, 2, 16, 2, 2, 4, WIDTH), np.eye(2))
        both = [t.reshape(HALF, HALF) for t in (first_a, first_b)]
        first.append(np.stack([halves(t) for t in (*both, both[0].T, both[1].T)]))
    first = np.stack(first)
    lane32 = [np.kron(np.eye(8), f(two_pi * (wide[:, None] * wide[None, :] % 32) / 32)) for f in (np.cos, np.sin)]
    lane8 = [np.kron(f(two_pi * (eight[:, None] * eight[None, :] % 8) / 8), np.eye(32)) for f in (np.cos, np.sin)]
    row = np.arange(HALF)
    lane = np.arange(G)
    part_sign = np.where(row // 4 % 2 == 0, 1.0, -1.0)[:, None]
    twist_y = two_pi * ((row // 16)[:, None] * (lane % 32)[None, :]) / G
    twist_x = two_pi * ((row // 8 * 2 + row // 2 % 2)[:, None] * (lane // 32)[None, :]) / G
    twiddle = np.stack(
        [np.cos(twist_y), part_sign * np.sin(twist_y), np.cos(twist_x), part_sign * np.sin(twist_x)]
    ).astype(np.float32)
    second = np.stack([halves(t) for t in (second, second.T)])
    lanes_table = np.stack([halves(np.concatenate(t, axis=1)) for t in (lane32, lane8)])
    return line, np.ascontiguousarray(onward), first, second, lanes_table, twiddle


def split(values):
    high = values.astype(BF16)
    return high, (values - high.astype(F32)).astype(BF16)


def mm(a, b):
    return jnp.dot(a, b, preferred_element_type=F32)


def mm_nt(a, b):
    return lax.dot_general(a, b, (((1,), (1,)), ((), ())), preferred_element_type=F32)


def swap(values):
    grouped = values.reshape(values.shape[0] // 8, 8, values.shape[1])
    return pltpu.roll(grouped, 4, 1).reshape(values.shape)


def on_rows(table_high, table_low, values):
    high, low = split(values)
    both = mm(jnp.concatenate([table_high, table_low], axis=0), high)
    return both[:HALF] + (both[HALF:] + mm(table_high, low))


def on_lanes(values, table_high, table_low, sign):
    high, low = split(values)
    both = mm(jnp.concatenate([high, low], axis=0), table_high)
    both = both[:HALF] + (both[HALF:] + mm(high, table_low))
    return both[:, :G] + sign * swap(both[:, G:])


def row_sums(tiles):
    row = lax.broadcasted_iota(jnp.int32, (8, CLUSTERS), 0)
    for step in (4, 2, 1):
        clear = (row & step) == 0
        merged = []
        for j in range(step):
            here = jnp.where(clear, tiles[j], tiles[j + step])
            there = jnp.where(clear, tiles[j + step], tiles[j])
            if step == 4:
                moved = pltpu.roll(there, 4, 0)
            else:
                moved = jnp.where(clear, pltpu.roll(there, 8 - step, 0), pltpu.roll(there, step, 0))
            merged.append(here + moved)
        tiles = merged
    return tiles[0]


def signs(direction):
    row = lax.broadcasted_iota(jnp.int32, (HALF, G), 0)
    return jnp.where((row & 4) == 0, direction, -direction).astype(F32)


def forward(values, rows_high, rows_low, lanes_high, lanes_low, cosines, sines):
    values = on_rows(rows_high, rows_low, values)
    values = values * cosines + swap(values) * sines
    return on_lanes(values, lanes_high, lanes_low, signs(1.0))


def backward(values, rows_high, rows_low, lanes_high, lanes_low, cosines, sines):
    values = on_lanes(values, lanes_high, lanes_low, signs(-1.0))
    values = values * cosines - swap(values) * sines
    return on_rows(rows_high, rows_low, values)


def wave(index):
    return jnp.where(index < G // 2, index, index - G).astype(F32)


def wavevectors(row_index, col_index):
    z_index, x_index = row_index // WIDTH, lax.rem(row_index, WIDTH)
    row = lax.broadcasted_iota(jnp.int32, (HALF, G), 0)
    lane = lax.broadcasted_iota(jnp.int32, (HALF, G), 1)
    low, above, q = (row >> 1) & 1, lane & -32, 8 * (lane & 31)
    ours = 4 * col_index + 2 * ((row >> 3) & 1) + low + above, (row >> 4) + q, 16 * z_index + 2 * x_index + (row & 1)
    theirs = 2 * (row >> 3) + low + above, 2 * x_index + (row & 1) + q, 16 * z_index + 8 + col_index + 0 * row
    return ours, theirs


def screen(m1, m2, m3):
    w1, w2, w3 = wave(m1), wave(m2), m3.astype(F32)
    squared = w1 * w1 + w2 * w2 + w3 * w3
    kept = jnp.where((m1 == G // 2) | (m2 == G // 2), 0.0, FACTOR).astype(F32)
    fold = jnp.where(m3 == 0, 1.0, 2.0).astype(F32)
    return w1, w2, w3, 1.0 / jnp.maximum(squared, 1.0), kept * fold / (squared + 0.5)


def spread(weight, density, first, sums):
    lane = lax.broadcasted_iota(jnp.int32, (STENCIL, CLUSTERS), 1)
    group = 8

    def some(i, sums):
        start = pl.multiple_of(i * group * PANELS, group * PANELS)
        block = weight[:, pl.ds(start, group * PANELS)]
        charge = density[:, pl.ds(start, group * PANELS)]
        sums = list(sums)
        for c in range(3):
            product = block * charge[c : c + 1]
            for k in range(group):
                total = jnp.sum(product[:, k * PANELS : (k + 1) * PANELS], axis=1, keepdims=True)
                sums[c] = jnp.where(lane == i * group + k, total, sums[c])
        return tuple(sums)

    groups = CLUSTERS // PIECES // group
    return lax.fori_loop(first * groups, (first + 1) * groups, some, sums, unroll=4)


def whole_kernel(
    corner, target, landing, count,
    density_in, interp_in, proj_in, line_in, onward_in, first_in, second_in, lanes_in, twiddle_in, tiles_in,
    out,
    density, interp, proj, line, onward, first, second, lanes_table, twiddle, blocks,
    packed, picked, gathered, hot, phases, upper, plane,
    sent1a, got1a, sent1b, got1b, sent2a, got2a, sent2b, got2b, modes_a, modes_b,
    sent3a, got3a, sent3b, got3b, sent4a, got4a, sent4b, got4b, sent5, got5,
    near_sent, near_got, near_rows, near_term, proj_high, proj_low, values,
    load_sem, slab_send, slab_recv, plane_sem, send_sem, recv_sem, near_sem,
):
    row_index, col_index = lax.axis_index("row"), lax.axis_index("col")
    z_index, x_index = row_index // WIDTH, lax.rem(row_index, WIDTH)
    width = CLUSTERS * PANELS // PIECES

    def piece(k):
        at = pl.ds(k * width, width)
        return pltpu.make_async_copy(interp_in.at[:, at], interp.at[:, at], load_sem.at[k])

    loads = [
        pltpu.make_async_copy(source, target_ref, load_sem.at[PIECES + k])
        for k, (source, target_ref) in enumerate(
            (
                (density_in, density),
                (line_in, line),
                (onward_in, onward),
                (first_in.at[lax.axis_index("row") // WIDTH], first),
                (second_in, second),
                (lanes_in, lanes_table),
                (twiddle_in, twiddle),
                (tiles_in, blocks),
                (proj_in, proj),
            )
        )
    ]
    loads[0].start()
    for k in range(PIECES):
        piece(k).start()

    def z_peer(j):
        return lax.rem(z_index + j, DEPTH)

    def x_peer(j):
        return lax.rem(x_index + j, WIDTH)

    def col_peer(j):
        return lax.rem(col_index + j, COLS)

    def at_z(peer):
        return (peer * WIDTH + x_index, col_index)

    def at_x(peer):
        return (z_index * WIDTH + peer, col_index)

    def at_col(peer):
        return (row_index, peer)

    def at_row(j):
        return (lax.rem(row_index + j, ROWS), col_index)

    barrier = pltpu.get_barrier_semaphore()

    def greet(device):
        pl.semaphore_signal(barrier, inc=1, device_id=device, device_id_type=MESH)

    def greet_z(j, carry):
        greet(at_z(z_peer(j)))
        return carry

    def greet_x(j, carry):
        greet(at_x(x_peer(j)))
        return carry

    def greet_col(j, carry):
        greet(at_col(col_peer(j)))
        return carry

    lax.fori_loop(1, DEPTH, greet_z, 0)
    lax.fori_loop(1, WIDTH, greet_x, 0)
    lax.fori_loop(1, COLS, greet_col, 0)
    greet(at_row(1))
    greet(at_row(ROWS - 1))
    loads[0].wait()
    sums = (jnp.zeros((STENCIL, CLUSTERS), F32),) * 3
    for k in range(PIECES):
        piece(k).wait()
        if k == 0:
            for load in loads[1:]:
                load.start()
        sums = spread(interp, density, k, sums)
    corners = corner[...]
    packed[80:PACKED] = jnp.zeros((PACKED - 80, CLUSTERS), F32)
    for c in range(3):
        packed[c * STENCIL : (c + 1) * STENCIL] = sums[c]
    packed[81:82] = ((corners[0:1] - row_index * 8) * 32 + (corners[1:2] - col_index * 32)).astype(F32)
    packed[82:83] = corners[2:3].astype(F32)
    pl.semaphore_wait(barrier, DEPTH + WIDTH + COLS - 3 + 2)

    def distance(i):
        odd = lax.rem(i, 2)
        return odd * (DEPTH - (i + 1) // 2) + (1 - odd) * (i // 2)

    def slab_copy(i):
        return pltpu.make_async_remote_copy(
            packed,
            gathered.at[z_index],
            slab_send.at[i],
            slab_recv.at[i],
            device_id=at_z(z_peer(DEPTH - distance(i))),
            device_id_type=MESH,
        )

    slab_copy(1).start()
    slab_copy(2).start()
    slab_copy(3).start()
    slab_copy(4).start()
    gathered[z_index] = packed[...]

    def plane_copy(kind, source, target, device):
        return pltpu.make_async_remote_copy(
            source, target, plane_sem.at[kind, 0], plane_sem.at[kind, 1], device_id=device, device_id_type=MESH
        )

    cell = lax.broadcasted_iota(jnp.int32, (G, CLUSTERS), 0).astype(F32)

    def build(zs, place):
        local, depth = gathered[zs, 81:82], gathered[zs, 82:83]
        at = jnp.where(cell == depth, 1.0, 0.0).astype(BF16)
        both = mm(line[z_index], at)
        turn = [both[:32] + both[32:]]
        for dz in range(1, 3):
            turn.append(turn[-1] * onward[z_index, 0] + swap(turn[-1]) * onward[z_index, 1])
        for dz in range(3):
            phases[zs, dz] = turn[dz]
        for dy in range(3):
            here = jnp.where(cell == local + float(dy), 1.0, 0.0).astype(BF16)
            hot[zs, :, dy * CLUSTERS : (dy + 1) * CLUSTERS] = here
        for dx in range(3):
            for c in range(3):
                for dy in range(3):
                    at = c * STENCIL + 9 * dx + 3 * dy
                    value = turn[0] * gathered[zs, at : at + 1]
                    value += turn[1] * gathered[zs, at + 1 : at + 2]
                    value += turn[2] * gathered[zs, at + 2 : at + 3]
                    high, low = split(value)
                    top = dx * 192 + c * 64
                    upper[top : top + 32, dy * CLUSTERS : (dy + 1) * CLUSTERS] = high
                    upper[top + 32 : top + 64, dy * CLUSTERS : (dy + 1) * CLUSTERS] = low
        total = mm_nt(upper[...], hot[zs])
        for c in range(3):
            sum_of = jnp.zeros((32, G), F32)
            for dx in range(3):
                top = dx * 192 + c * 64
                part = total[top : top + 32] + total[top + 32 : top + 64]
                sum_of += pltpu.roll(part, 32 * dx, 1) if dx else part
            plane[place, c] = sum_of.reshape(4, 8, G)

    tile_row = lax.broadcasted_iota(jnp.int32, (8, G), 0)

    def shifted(tile, by):
        return pltpu.roll(tile, by % 8, 0) if by % 8 else tile

    def mix2(tiles, to):
        return jnp.where((tile_row & 2) == 0, shifted(tiles[0], -2 * to), shifted(tiles[1], 2 - 2 * to))

    def mix4(tiles, to):
        mixed = shifted(tiles[0], -to)
        for j in range(1, 4):
            mixed = jnp.where((tile_row & 3) == j, shifted(tiles[j], j - to), mixed)
        return mixed

    def send_quad(quad):
        for c in range(3):
            for peer in range(WIDTH):
                for pair in range(2):
                    tiles = [plane[2 * pair + b, c, peer // 2] for b in range(2)]
                    sent1a[peer, 2 * quad + pair, c] = mix2(tiles, peer % 2)
            for peer in range(COLS):
                tiles = [plane[j, c, 2 + peer // 4] for j in range(4)]
                sent1b[peer, quad, c] = mix4(tiles, peer % 4)

        def send_a(j, carry):
            peer = x_peer(j)
            pair = pl.ds(2 * quad, 2)
            plane_copy(0, sent1a.at[peer, pair], got1a.at[x_index, pair], at_x(peer)).start()
            return carry

        def send_b(j, carry):
            peer = col_peer(j)
            plane_copy(1, sent1b.at[peer, quad], got1b.at[col_index, quad], at_col(peer)).start()
            return carry

        lax.fori_loop(1, WIDTH, send_a, 0)
        lax.fori_loop(1, COLS, send_b, 0)

    loads[1].wait()
    loads[2].wait()

    def next_slab(i, carry):
        @pl.when(i == 1)
        def _():
            slab_copy(5).start()
            slab_copy(6).start()
            slab_copy(7).start()

        @pl.when(i >= 1)
        def _():
            slab_copy(i).wait_recv()

        build(z_peer(distance(i)), lax.rem(i, 4))
        return carry

    def four_slabs(quad, carry):
        lax.fori_loop(4 * quad, 4 * quad + 4, next_slab, 0)
        send_quad(quad)
        return carry

    lax.fori_loop(0, 2, four_slabs, 0)
    got1a[x_index] = sent1a[x_index]
    got1b[col_index] = sent1b[col_index]

    def copy(stage, c, source, target, device):
        return pltpu.make_async_remote_copy(
            source,
            target,
            send_sem.at[stage, c],
            recv_sem.at[stage, c],
            device_id=device,
            device_id_type=MESH,
        )

    def to_all(stage, c, source, target, count, mine, peer_of, device_of):
        def one(j, carry):
            peer = peer_of(j)
            copy(stage, c, source.at[c, peer], target.at[c, mine], device_of(peer)).start()
            return carry

        lax.fori_loop(1, count, one, 0)
        target[c, mine] = source[c, mine]

    def whole(stage, c, source, target):
        peers = source.shape[1] - 1
        return copy(stage, c, source.at[c, pl.ds(0, peers)], target.at[c, pl.ds(0, peers)], at_row(1))

    def first_of(k):
        return first[k, 0], first[k, 1]

    def second_of(k):
        return second[k, 0], second[k, 1]

    def lanes_of(k):
        return lanes_table[k, 0], lanes_table[k, 1]

    def first_forward(values, k):
        return forward(values.reshape(HALF, G), *first_of(k), *lanes_of(1), twiddle[2], twiddle[3])

    def second_forward(values):
        return forward(values.reshape(HALF, G), *second_of(0), *lanes_of(0), twiddle[0], twiddle[1])

    def first_backward(values, k):
        return backward(values.reshape(HALF, G), *first_of(2 + k), *lanes_of(1), twiddle[2], twiddle[3])

    def second_backward(values):
        return backward(values.reshape(HALF, G), *second_of(1), *lanes_of(0), twiddle[0], twiddle[1])

    def to_cols(stage, c, source, target):
        to_all(stage, c, source, target, COLS, col_index, col_peer, at_col)

    def to_width(stage, c, source, target):
        to_all(stage, c, source, target, WIDTH, x_index, x_peer, at_x)

    waits = (
        plane_copy(0, sent1a.at[pl.ds(0, WIDTH - 1)], got1a.at[pl.ds(0, WIDTH - 1)], at_x(x_peer(1))),
        plane_copy(1, sent1b.at[pl.ds(0, COLS - 1)], got1b.at[pl.ds(0, COLS - 1)], at_col(col_peer(1))),
    )
    for load in loads[3:7]:
        load.wait()
    for wait in waits:
        wait.wait_recv()

    def step_one(c, carry):
        sent2a[c] = first_forward(got1a[:, :, c], 0).reshape(COLS, 16, G)
        to_cols(0, c, sent2a, got2a)
        sent2b[c] = second_forward(got1b[:, :, c]).reshape(WIDTH, 32, G)
        to_width(1, c, sent2b, got2b)
        return carry

    lax.fori_loop(0, 3, step_one, 0, unroll=3)

    loads[7].wait()
    near_sent[...] = jnp.zeros_like(near_sent)
    picked[...] = jnp.zeros_like(picked)
    nobody = jnp.full((3, PANELS), -1, jnp.int32)
    wanted = [
        jnp.where(jnp.full((3, PANELS), q, jnp.int32) < count[0], jnp.full((3, PANELS), target[q], jnp.int32), nobody)
        for q in range(SLOTS)
    ]

    def pick(i, charges):
        charges = list(charges)
        for k in range(GROUP):
            cluster = i * GROUP + k
            charge = density[:, pl.ds(pl.multiple_of(cluster * PANELS, PANELS), PANELS)]
            for q in range(SLOTS):
                charges[q] = jnp.where(wanted[q] == cluster, charge, charges[q])
        return tuple(charges)

    charges = lax.fori_loop(0, CLUSTERS // GROUP, pick, (jnp.zeros((3, PANELS), F32),) * SLOTS)
    for q in range(SLOTS):
        picked[q, 0:3] = charges[q]

    def slot(q, carry):
        charge = picked[q].astype(BF16)
        for b in range(3):
            total = mm(charge[0:1], blocks[q, 0, b])
            total += mm(charge[1:2], blocks[q, 1, b])
            total += mm(charge[2:3], blocks[q, 2, b])
            near_sent[q, b : b + 1] = total
        return carry

    lax.fori_loop(0, SLOTS, slot, 0)
    near_copies = []
    for side, j in ((0, ROWS - 1), (1, 1)):
        for k in range(4):
            near_copies.append(
                pltpu.make_async_remote_copy(
                    near_sent.at[4 + 2 * k + side],
                    near_got.at[2 * k + side],
                    near_sem.at[0, 2 * k + side],
                    near_sem.at[1, 2 * k + side],
                    device_id=at_row(j),
                    device_id_type=MESH,
                )
            )
    for near_copy in near_copies:
        near_copy.start()

    loads[8].wait()
    below = jnp.zeros((32 - STENCIL, PANELS), F32)

    def halve(i, carry):
        start = pl.multiple_of(i * GROUP * PANELS, GROUP * PANELS)
        for k in range(GROUP):
            block = proj[:, pl.ds(start + k * PANELS, PANELS)]
            high, low = split(jnp.concatenate([block, below], axis=0))
            proj_high[i, k * 32 : (k + 1) * 32] = high
            proj_low[i, k * 32 : (k + 1) * 32] = low
        return carry

    lax.fori_loop(0, CLUSTERS // GROUP, halve, 0)

    screens = [screen(*index) for index in wavevectors(row_index, col_index)]

    def step_two(c, carry):
        whole(0, c, sent2a, got2a).wait_recv()
        whole(1, c, sent2b, got2b).wait_recv()
        modes_a[c] = second_forward(got2a[c])
        modes_b[c] = first_forward(got2b[c], 1)
        return carry

    lax.fori_loop(0, 3, step_two, 0)

    for modes, (w1, w2, w3, inverse, weighting) in zip((modes_a, modes_b), screens):
        inner = (w1 * modes[0] + w2 * modes[1] + w3 * modes[2]) * inverse
        for c, w in enumerate((w1, w2, w3)):
            modes[c] = (modes[c] - w * inner) * weighting

    def step_three(c, carry):
        sent3a[c] = second_backward(modes_a[c]).reshape(COLS, 16, G)
        to_cols(2, c, sent3a, got3a)
        sent3b[c] = first_backward(modes_b[c], 1).reshape(WIDTH, 32, G)
        to_width(3, c, sent3b, got3b)
        return carry

    lax.fori_loop(0, 3, step_three, 0, unroll=3)

    def step_four(c, carry):
        whole(2, c, sent3a, got3a).wait_recv()
        whole(3, c, sent3b, got3b).wait_recv()
        sent4a[c] = first_backward(got3a[c], 0).reshape(WIDTH, 4, 8, G)
        to_width(4, c, sent4a, got4a)
        sent4b[c] = second_backward(got3b[c]).reshape(COLS, 2, 8, G)
        to_cols(5, c, sent4b, got4b)
        return carry

    lax.fori_loop(0, 3, step_four, 0)

    for near_copy in near_copies:
        near_copy.wait()
    near_rows[...] = jnp.zeros_like(near_rows)
    row = lax.broadcasted_iota(jnp.int32, (CLUSTERS, CLUSTERS), 0)
    lane = lax.broadcasted_iota(jnp.int32, (CLUSTERS, CLUSTERS), 1)
    lands = jnp.zeros((CLUSTERS, CLUSTERS), F32)
    for q in range(SLOTS):
        lands = jnp.where((lane == q) & (row == landing[q]), 1.0, lands)
        for b in range(3):
            arrived = near_sent[q, b : b + 1] if q < 4 else near_got[q - 4, b : b + 1]
            near_rows[q : q + 1, b * PANELS : (b + 1) * PANELS] = arrived
    lands = lands.astype(BF16)
    high, low = split(near_rows[...])
    near_term[...] = mm(lands, high) + mm(lands, low)

    points = pl.ds(0, STENCIL)
    others = pl.ds(0, DEPTH - 1)

    def sample(c, carry):
        whole(4, c, sent4a, got4a).wait_recv()
        whole(5, c, sent4b, got4b).wait_recv()

        def unpack(quad, carry):
            for j in range(4):
                pair, b = 2 * quad + j // 2, j % 2
                for high in range(2):
                    plane[4 * quad + j, 0, high] = mix2([got4a[c, 2 * high + k, pair] for k in range(2)], b)
                    plane[4 * quad + j, 0, 2 + high] = mix4([got4b[c, 4 * high + k, quad] for k in range(4)], j)
            return carry

        lax.fori_loop(0, 2, unpack, 0)

        def slab(i, carry):
            step = DEPTH - 1 - i
            zs = z_peer(distance(step))
            here = plane[step, 0].reshape(32, G)
            around = jnp.concatenate([here] + [pltpu.roll(here, G - 32 * dx, 1) for dx in (1, 2)], axis=0)
            high, low = split(around)
            both = mm(jnp.concatenate([high, low], axis=0), hot[zs])
            both = both[:96] + both[96:]
            parts = []
            for dx in range(3):
                for dy in range(3):
                    part = both[dx * 32 : dx * 32 + 32, dy * CLUSTERS : (dy + 1) * CLUSTERS]
                    for dz in range(3):
                        product = (part * phases[zs, dz]).reshape(4, 8, CLUSTERS)
                        parts.append((product[0] + product[1]) + (product[2] + product[3]))
            parts += [jnp.zeros((8, CLUSTERS), F32)] * (32 - STENCIL)
            for k in range(4):
                sent5[c, zs, 8 * k : 8 * k + 8] = row_sums(parts[8 * k : 8 * k + 8])

            @pl.when(i < DEPTH - 1)
            def _():
                copy(6, c, sent5.at[c, zs, points], got5.at[c, z_index, points], at_z(zs)).start()

            return carry

        lax.fori_loop(0, DEPTH, slab, 0, unroll=2)
        got5[c, z_index] = sent5[c, z_index]
        return carry

    lax.fori_loop(0, 3, sample, 0)

    def send_done(j, carry):
        slab_copy(j).wait_send()
        return carry

    lax.fori_loop(1, DEPTH, send_done, 0)
    for wait in waits:
        wait.wait_send()

    def finish(c, carry):
        whole(0, c, sent2a, got2a).wait_send()
        whole(1, c, sent2b, got2b).wait_send()
        whole(2, c, sent3a, got3a).wait_send()
        whole(3, c, sent3b, got3b).wait_send()
        whole(4, c, sent4a, got4a).wait_send()
        whole(5, c, sent4b, got4b).wait_send()
        copy(6, c, sent5.at[c, others, points], got5.at[c, others, points], at_row(1)).wait()
        total = jnp.sum(got5[c, :, :STENCIL], axis=0)
        total = jnp.concatenate([total, below], axis=0)
        turned = jnp.concatenate([total] * 4, axis=0).T
        both = jnp.concatenate([turned, turned], axis=1)
        both = jnp.where(own, both, jnp.zeros_like(both))
        high = both.astype(BF16).astype(F32)
        low = both - high
        for i in range(CLUSTERS // GROUP):
            at = slice(i * GROUP, (i + 1) * GROUP)
            values[i, c] = jnp.concatenate([high[at], low[at]], axis=0).astype(BF16)
        return carry

    own = (lax.broadcasted_iota(jnp.int32, (CLUSTERS, G), 0) & (GROUP - 1)) == (
        lax.broadcasted_iota(jnp.int32, (CLUSTERS, G), 1) >> 5
    )
    lax.fori_loop(0, 3, finish, 0)

    def project(i, carry):
        point_values = values[i].reshape(3 * 2 * GROUP, G)
        both = mm(point_values, proj_high[i]) + mm(point_values, proj_low[i])
        at = pl.ds(pl.multiple_of(i * GROUP, GROUP), GROUP)
        for c in range(3):
            far = both[c * 2 * GROUP : c * 2 * GROUP + GROUP] + both[c * 2 * GROUP + GROUP : (c + 1) * 2 * GROUP]
            far += near_term[at, c * PANELS : (c + 1) * PANELS]
            for k in range(GROUP):
                place = pl.multiple_of((i * GROUP + k) * PANELS, PANELS)
                out[c : c + 1, pl.ds(place, PANELS)] = far[k : k + 1]
        return carry

    lax.fori_loop(0, CLUSTERS // GROUP, project, 0, unroll=8)


VMEM = pl.BlockSpec(memory_space=pltpu.VMEM)
SMEM = pl.BlockSpec(memory_space=pltpu.SMEM)
ANY = pl.BlockSpec(memory_space=pl.ANY)
LIMIT = 60 * 1024 * 1024


def shape(dims, dtype=F32):
    return jax.ShapeDtypeStruct(dims, dtype)


def per_device(
    density, interp_weight, proj_weight, stencil_corner, near_tiles, pair_target, pair_landing, pair_count
):
    line, onward, first, second, lanes_table, twiddle = (jnp.asarray(t) for t in make_tables())
    planes_a, planes_b = pltpu.VMEM((WIDTH, 4, 3, 8, G), F32), pltpu.VMEM((COLS, 2, 3, 8, G), F32)
    by_cols, by_width = pltpu.VMEM((3, COLS, 16, G), F32), pltpu.VMEM((3, WIDTH, 32, G), F32)
    modes = pltpu.VMEM((3, HALF, G), F32)
    last_a, last_b = pltpu.VMEM((3, WIDTH, 4, 8, G), F32), pltpu.VMEM((3, COLS, 2, 8, G), F32)
    by_depth = (3, DEPTH, 32, CLUSTERS)
    held = (density, interp_weight, proj_weight, line, onward, first, second, lanes_table, twiddle, near_tiles)
    weights = pltpu.VMEM((CLUSTERS // GROUP, G, PANELS), BF16)
    return pl.pallas_call(
        whole_kernel,
        out_shape=shape((3, CLUSTERS * PANELS)),
        in_specs=[VMEM] + [SMEM] * 3 + [ANY] * 10,
        out_specs=VMEM,
        scratch_shapes=[
            *(pltpu.VMEM(array.shape[1:] if array is first else array.shape, array.dtype) for array in held),
            pltpu.VMEM((PACKED, CLUSTERS), F32),
            pltpu.VMEM((SLOTS, 8, PANELS), F32),
            pltpu.VMEM((DEPTH, PACKED, CLUSTERS), F32),
            pltpu.VMEM((DEPTH, G, 3 * CLUSTERS), BF16),
            pltpu.VMEM((DEPTH, 3, 32, CLUSTERS), F32),
            pltpu.VMEM((576, 3 * CLUSTERS), BF16),
            pltpu.VMEM((DEPTH, 3, 4, 8, G), F32),
            *(planes_a, planes_a, planes_b, planes_b),
            *(by_cols, by_cols, by_width, by_width, modes, modes),
            *(by_cols, by_cols, by_width, by_width),
            *(last_a, last_a, last_b, last_b),
            pltpu.VMEM(by_depth, F32),
            pltpu.VMEM(by_depth, F32),
            pltpu.VMEM((SLOTS, 8, PANELS), F32),
            pltpu.VMEM((8, 8, PANELS), F32),
            pltpu.VMEM((CLUSTERS, 3 * PANELS), F32),
            pltpu.VMEM((CLUSTERS, 3 * PANELS), F32),
            weights,
            weights,
            pltpu.VMEM((CLUSTERS // GROUP, 3, 2 * GROUP, G), BF16),
            pltpu.SemaphoreType.DMA((PIECES + 9,)),
            pltpu.SemaphoreType.DMA((DEPTH,)),
            pltpu.SemaphoreType.DMA((DEPTH,)),
            pltpu.SemaphoreType.DMA((2, 2)),
            pltpu.SemaphoreType.DMA((7, 3)),
            pltpu.SemaphoreType.DMA((7, 3)),
            pltpu.SemaphoreType.DMA((2, 8)),
        ],
        compiler_params=pltpu.CompilerParams(
            vmem_limit_bytes=LIMIT, collective_id=0, has_side_effects=True
        ),
    )(stencil_corner, pair_target, pair_landing, pair_count, *held)


def solution(mesh):
    flat = P(None, ("row", "col"))
    slots = P(("row", "col"))
    in_specs = (flat, flat, flat, flat, P(("row", "col"), None, None, None, None), slots, slots, slots)
    return jax.shard_map(
        per_device, mesh=mesh, in_specs=in_specs, out_specs=flat, check_vma=False
    )
```

```python
import math

import jax
import jax.numpy as jnp
import ml_dtypes
import numpy as np
from jax import lax
from jax.experimental import pallas as pl
from jax.experimental.pallas import tpu as pltpu
from jax.sharding import PartitionSpec as P

G = 256
STENCIL = 27
ROWS = 32
COLS = 8
DEPTH = 8
WIDTH = 4
PACKED = 88
USED = 83
PIECES = 4
GROUP = 8
HALF = 128
CLUSTERS = 128
PANELS = 128
SLOTS = 12
BF16 = jnp.bfloat16
F32 = jnp.float32
MESH = pl.DeviceIdType.MESH
FACTOR = 1.0 / math.sqrt(ROWS * COLS * CLUSTERS * PANELS)


def halves(table):
    table = np.asarray(table, np.float64)
    high = table.astype(np.float32).astype(ml_dtypes.bfloat16)
    low = (table - high.astype(np.float64)).astype(np.float32).astype(ml_dtypes.bfloat16)
    return np.stack([high, low])


def rotation(theta):
    cosine, sine = np.cos(theta), np.sin(theta)
    return np.array([[cosine, sine], [-sine, cosine]])


def make_tables():
    two_pi = 2 * np.pi
    bins, cells = np.arange(128), np.arange(G)
    theta = two_pi * (bins[:, None] * cells[None, :] % G) / G
    line = np.stack([np.cos(theta), -np.sin(theta)]).reshape(2, DEPTH, 4, 4, G)
    line = line.transpose(1, 2, 0, 3, 4).reshape(DEPTH, 32, G)
    line = halves(line).transpose(1, 0, 2, 3).reshape(DEPTH, 64, G)
    step = 2 * np.pi * np.arange(128).reshape(DEPTH, 4, 1, 4) / G
    onward = np.stack([np.cos(step) + np.zeros((2, 1)), np.sin(step) * np.array([[1.0], [-1.0]])], axis=1)
    onward = np.broadcast_to(onward.reshape(DEPTH, 2, 32, 1), (DEPTH, 2, 32, CLUSTERS)).astype(np.float32)
    eight = np.arange(8)
    wide = np.arange(32)
    turn8 = rotation(two_pi * (eight[:, None] * eight[None, :] % 8) / 8)
    turn32 = rotation(two_pi * (wide[:, None] * wide[None, :] % 32) / 32)
    second = np.einsum("oipc,hg,lm->pholcgim", turn8, np.eye(2), np.eye(4)).reshape(HALF, HALF)
    by_block = turn32.reshape(2, 2, 16, 2, DEPTH, WIDTH)
    first = []
    for z in range(DEPTH):
        order = [(z + d) % DEPTH for d in (0, 7, 1, 6, 2, 5, 3, 4)]
        mine = by_block[:, :, :, :, order]
        first_a = np.einsum("oihlabx,km->holkxaibm", mine.reshape(2, 2, 16, 2, 4, 2, WIDTH), np.eye(2))
        first_b = np.einsum("oihlabx,km->holkxmaib", mine.reshape(2, 2, 16, 2, 2, 4, WIDTH), np.eye(2))
        both = [t.reshape(HALF, HALF) for t in (first_a, first_b)]
        first.append(np.stack([halves(t) for t in (*both, both[0].T, both[1].T)]))
    first = np.stack(first)
    lane32 = [np.kron(np.eye(8), f(two_pi * (wide[:, None] * wide[None, :] % 32) / 32)) for f in (np.cos, np.sin)]
    lane8 = [np.kron(f(two_pi * (eight[:, None] * eight[None, :] % 8) / 8), np.eye(32)) for f in (np.cos, np.sin)]
    row = np.arange(HALF)
    lane = np.arange(G)
    part_sign = np.where(row // 4 % 2 == 0, 1.0, -1.0)[:, None]
    twist_y = two_pi * ((row // 16)[:, None] * (lane % 32)[None, :]) / G
    twist_x = two_pi * ((row // 8 * 2 + row // 2 % 2)[:, None] * (lane // 32)[None, :]) / G
    twiddle = np.stack(
        [np.cos(twist_y), part_sign * np.sin(twist_y), np.cos(twist_x), part_sign * np.sin(twist_x)]
    ).astype(np.float32)
    second = np.stack([halves(t) for t in (second, second.T)])
    lanes_table = np.stack([halves(np.concatenate(t, axis=1)) for t in (lane32, lane8)])
    return line, np.ascontiguousarray(onward), first, second, lanes_table, twiddle


def split(values):
    high = values.astype(BF16)
    return high, (values - high.astype(F32)).astype(BF16)


def mm(a, b):
    return jnp.dot(a, b, preferred_element_type=F32)


def mm_nt(a, b):
    return lax.dot_general(a, b, (((1,), (1,)), ((), ())), preferred_element_type=F32)


def swap(values):
    grouped = values.reshape(values.shape[0] // 8, 8, values.shape[1])
    return pltpu.roll(grouped, 4, 1).reshape(values.shape)


def on_rows(table_high, table_low, values):
    high, low = split(values)
    both = mm(jnp.concatenate([table_high, table_low], axis=0), high)
    return both[:HALF] + (both[HALF:] + mm(table_high, low))


def on_lanes(values, table_high, table_low, sign):
    high, low = split(values)
    both = mm(jnp.concatenate([high, low], axis=0), table_high)
    both = both[:HALF] + (both[HALF:] + mm(high, table_low))
    return both[:, :G] + sign * swap(both[:, G:])


def row_sums(tiles):
    row = lax.broadcasted_iota(jnp.int32, (8, CLUSTERS), 0)
    for step in (4, 2, 1):
        clear = (row & step) == 0
        merged = []
        for j in range(step):
            here = jnp.where(clear, tiles[j], tiles[j + step])
            there = jnp.where(clear, tiles[j + step], tiles[j])
            if step == 4:
                moved = pltpu.roll(there, 4, 0)
            else:
                moved = jnp.where(clear, pltpu.roll(there, 8 - step, 0), pltpu.roll(there, step, 0))
            merged.append(here + moved)
        tiles = merged
    return tiles[0]


def signs(direction):
    row = lax.broadcasted_iota(jnp.int32, (HALF, G), 0)
    return jnp.where((row & 4) == 0, direction, -direction).astype(F32)


def forward(values, rows_high, rows_low, lanes_high, lanes_low, cosines, sines):
    values = on_rows(rows_high, rows_low, values)
    values = values * cosines + swap(values) * sines
    return on_lanes(values, lanes_high, lanes_low, signs(1.0))


def backward(values, rows_high, rows_low, lanes_high, lanes_low, cosines, sines):
    values = on_lanes(values, lanes_high, lanes_low, signs(-1.0))
    values = values * cosines - swap(values) * sines
    return on_rows(rows_high, rows_low, values)


def wave(index):
    return jnp.where(index < G // 2, index, index - G).astype(F32)


def wavevectors(row_index, col_index):
    z_index, x_index = row_index // WIDTH, lax.rem(row_index, WIDTH)
    row = lax.broadcasted_iota(jnp.int32, (HALF, G), 0)
    lane = lax.broadcasted_iota(jnp.int32, (HALF, G), 1)
    low, above, q = (row >> 1) & 1, lane & -32, 8 * (lane & 31)
    ours = 4 * col_index + 2 * ((row >> 3) & 1) + low + above, (row >> 4) + q, 16 * z_index + 2 * x_index + (row & 1)
    theirs = 2 * (row >> 3) + low + above, 2 * x_index + (row & 1) + q, 16 * z_index + 8 + col_index + 0 * row
    return ours, theirs


def screen(m1, m2, m3):
    w1, w2, w3 = wave(m1), wave(m2), m3.astype(F32)
    squared = w1 * w1 + w2 * w2 + w3 * w3
    kept = jnp.where((m1 == G // 2) | (m2 == G // 2), 0.0, FACTOR).astype(F32)
    fold = jnp.where(m3 == 0, 1.0, 2.0).astype(F32)
    return w1, w2, w3, 1.0 / jnp.maximum(squared, 1.0), kept * fold / (squared + 0.5)


def spread(weight, density, first, sums):
    lane = lax.broadcasted_iota(jnp.int32, (STENCIL, CLUSTERS), 1)
    group = 8

    def some(i, sums):
        start = pl.multiple_of(i * group * PANELS, group * PANELS)
        block = weight[:, pl.ds(start, group * PANELS)]
        charge = density[:, pl.ds(start, group * PANELS)]
        sums = list(sums)
        for c in range(3):
            product = block * charge[c : c + 1]
            for k in range(group):
                total = jnp.sum(product[:, k * PANELS : (k + 1) * PANELS], axis=1, keepdims=True)
                sums[c] = jnp.where(lane == i * group + k, total, sums[c])
        return tuple(sums)

    groups = CLUSTERS // PIECES // group
    return lax.fori_loop(first * groups, (first + 1) * groups, some, sums, unroll=4)


def whole_kernel(
    corner, target, landing, count,
    density_in, interp_in, proj_in, line_in, onward_in, first_in, second_in, lanes_in, twiddle_in, tiles_in,
    out,
    density, interp, proj, line, onward, first, second, lanes_table, twiddle, blocks,
    packed, picked, gathered, hot, phases, upper, plane,
    sent1a, got1a, sent1b, got1b, sent2a, got2a, sent2b, got2b, modes_a, modes_b,
    sent3a, got3a, sent3b, got3b, sent4a, got4a, sent4b, got4b, sent5, got5,
    near_sent, near_got, near_rows, near_term, proj_high, proj_low, values,
    load_sem, slab_send, slab_recv, plane_sem, send_sem, recv_sem, near_sem,
):
    row_index, col_index = lax.axis_index("row"), lax.axis_index("col")
    z_index, x_index = row_index // WIDTH, lax.rem(row_index, WIDTH)
    width = CLUSTERS * PANELS // PIECES

    def piece(k):
        at = pl.ds(k * width, width)
        return pltpu.make_async_copy(interp_in.at[:, at], interp.at[:, at], load_sem.at[k])

    loads = [
        pltpu.make_async_copy(source, target_ref, load_sem.at[PIECES + k])
        for k, (source, target_ref) in enumerate(
            (
                (density_in, density),
                (line_in, line),
                (onward_in, onward),
                (first_in.at[lax.axis_index("row") // WIDTH], first),
                (second_in, second),
                (lanes_in, lanes_table),
                (twiddle_in, twiddle),
                (tiles_in, blocks),
                (proj_in, proj),
            )
        )
    ]
    loads[0].start()
    for k in range(PIECES):
        piece(k).start()

    def z_peer(j):
        return lax.rem(z_index + j, DEPTH)

    def x_peer(j):
        return lax.rem(x_index + j, WIDTH)

    def col_peer(j):
        return lax.rem(col_index + j, COLS)

    def at_z(peer):
        return (peer * WIDTH + x_index, col_index)

    def at_x(peer):
        return (z_index * WIDTH + peer, col_index)

    def at_col(peer):
        return (row_index, peer)

    def at_row(j):
        return (lax.rem(row_index + j, ROWS), col_index)

    barrier = pltpu.get_barrier_semaphore()

    def greet(device):
        pl.semaphore_signal(barrier, inc=1, device_id=device, device_id_type=MESH)

    def greet_z(j, carry):
        greet(at_z(z_peer(j)))
        return carry

    def greet_x(j, carry):
        greet(at_x(x_peer(j)))
        return carry

    def greet_col(j, carry):
        greet(at_col(col_peer(j)))
        return carry

    lax.fori_loop(1, DEPTH, greet_z, 0)
    lax.fori_loop(1, WIDTH, greet_x, 0)
    lax.fori_loop(1, COLS, greet_col, 0)
    greet(at_row(1))
    greet(at_row(ROWS - 1))
    loads[0].wait()
    sums = (jnp.zeros((STENCIL, CLUSTERS), F32),) * 3
    for k in range(PIECES):
        piece(k).wait()
        if k == 0:
            for load in loads[1:]:
                load.start()
        sums = spread(interp, density, k, sums)
    corners = corner[...]
    packed[80:PACKED] = jnp.zeros((PACKED - 80, CLUSTERS), F32)
    for c in range(3):
        packed[c * STENCIL : (c + 1) * STENCIL] = sums[c]
    packed[81:82] = ((corners[0:1] - row_index * 8) * 32 + (corners[1:2] - col_index * 32)).astype(F32)
    packed[82:83] = corners[2:3].astype(F32)
    pl.semaphore_wait(barrier, DEPTH + WIDTH + COLS - 3 + 2)

    def distance(i):
        odd = lax.rem(i, 2)
        return odd * (DEPTH - (i + 1) // 2) + (1 - odd) * (i // 2)

    def slab_copy(i):
        return pltpu.make_async_remote_copy(
            packed.at[pl.ds(0, USED)],
            gathered.at[z_index, pl.ds(0, USED)],
            slab_send.at[i],
            slab_recv.at[i],
            device_id=at_z(z_peer(DEPTH - distance(i))),
            device_id_type=MESH,
        )

    slab_copy(1).start()
    slab_copy(2).start()
    slab_copy(3).start()
    slab_copy(4).start()
    gathered[z_index] = packed[...]

    def plane_copy(kind, source, target, device):
        return pltpu.make_async_remote_copy(
            source, target, plane_sem.at[kind, 0], plane_sem.at[kind, 1], device_id=device, device_id_type=MESH
        )

    cell = lax.broadcasted_iota(jnp.int32, (G, CLUSTERS), 0).astype(F32)

    def build(zs, place):
        local, depth = gathered[zs, 81:82], gathered[zs, 82:83]
        at = jnp.where(cell == depth, 1.0, 0.0).astype(BF16)
        both = mm(line[z_index], at)
        turn = [both[:32] + both[32:]]
        for dz in range(1, 3):
            turn.append(turn[-1] * onward[z_index, 0] + swap(turn[-1]) * onward[z_index, 1])
        for dz in range(3):
            phases[zs, dz] = turn[dz]
        for dy in range(3):
            here = jnp.where(cell == local + float(dy), 1.0, 0.0).astype(BF16)
            hot[zs, :, dy * CLUSTERS : (dy + 1) * CLUSTERS] = here
        for dx in range(3):
            for c in range(3):
                for dy in range(3):
                    at = c * STENCIL + 9 * dx + 3 * dy
                    value = turn[0] * gathered[zs, at : at + 1]
                    value += turn[1] * gathered[zs, at + 1 : at + 2]
                    value += turn[2] * gathered[zs, at + 2 : at + 3]
                    high, low = split(value)
                    top = dx * 192 + c * 64
                    upper[top : top + 32, dy * CLUSTERS : (dy + 1) * CLUSTERS] = high
                    upper[top + 32 : top + 64, dy * CLUSTERS : (dy + 1) * CLUSTERS] = low
        total = mm_nt(upper[...], hot[zs])
        for c in range(3):
            sum_of = jnp.zeros((32, G), F32)
            for dx in range(3):
                top = dx * 192 + c * 64
                part = total[top : top + 32] + total[top + 32 : top + 64]
                sum_of += pltpu.roll(part, 32 * dx, 1) if dx else part
            plane[place, c] = sum_of.reshape(4, 8, G)

    tile_row = lax.broadcasted_iota(jnp.int32, (8, G), 0)

    def shifted(tile, by):
        return pltpu.roll(tile, by % 8, 0) if by % 8 else tile

    def mix2(tiles, to):
        return jnp.where((tile_row & 2) == 0, shifted(tiles[0], -2 * to), shifted(tiles[1], 2 - 2 * to))

    def mix4(tiles, to):
        mixed = shifted(tiles[0], -to)
        for j in range(1, 4):
            mixed = jnp.where((tile_row & 3) == j, shifted(tiles[j], j - to), mixed)
        return mixed

    def send_quad(quad):
        for c in range(3):
            for peer in range(WIDTH):
                for pair in range(2):
                    tiles = [plane[2 * pair + b, c, peer // 2] for b in range(2)]
                    sent1a[peer, 2 * quad + pair, c] = mix2(tiles, peer % 2)
            for peer in range(COLS):
                tiles = [plane[j, c, 2 + peer // 4] for j in range(4)]
                sent1b[peer, quad, c] = mix4(tiles, peer % 4)

        def send_a(j, carry):
            peer = x_peer(j)
            pair = pl.ds(2 * quad, 2)
            plane_copy(0, sent1a.at[peer, pair], got1a.at[x_index, pair], at_x(peer)).start()
            return carry

        def send_b(j, carry):
            peer = col_peer(j)
            plane_copy(1, sent1b.at[peer, quad], got1b.at[col_index, quad], at_col(peer)).start()
            return carry

        lax.fori_loop(1, WIDTH, send_a, 0)
        lax.fori_loop(1, COLS, send_b, 0)

    loads[1].wait()
    loads[2].wait()

    def next_slab(i, carry):
        @pl.when(i == 1)
        def _():
            slab_copy(5).start()
            slab_copy(6).start()
            slab_copy(7).start()

        @pl.when(i >= 1)
        def _():
            slab_copy(i).wait_recv()

        build(z_peer(distance(i)), lax.rem(i, 4))
        return carry

    def four_slabs(quad, carry):
        lax.fori_loop(4 * quad, 4 * quad + 4, next_slab, 0)
        send_quad(quad)
        return carry

    lax.fori_loop(0, 2, four_slabs, 0)
    got1a[x_index] = sent1a[x_index]
    got1b[col_index] = sent1b[col_index]

    def copy(stage, c, source, target, device):
        return pltpu.make_async_remote_copy(
            source,
            target,
            send_sem.at[stage, c],
            recv_sem.at[stage, c],
            device_id=device,
            device_id_type=MESH,
        )

    def to_all(stage, c, source, target, count, mine, peer_of, device_of):
        def one(j, carry):
            peer = peer_of(j)
            copy(stage, c, source.at[c, peer], target.at[c, mine], device_of(peer)).start()
            return carry

        lax.fori_loop(1, count, one, 0)
        target[c, mine] = source[c, mine]

    def whole(stage, c, source, target):
        peers = source.shape[1] - 1
        return copy(stage, c, source.at[c, pl.ds(0, peers)], target.at[c, pl.ds(0, peers)], at_row(1))

    def first_of(k):
        return first[k, 0], first[k, 1]

    def second_of(k):
        return second[k, 0], second[k, 1]

    def lanes_of(k):
        return lanes_table[k, 0], lanes_table[k, 1]

    def first_forward(values, k):
        return forward(values.reshape(HALF, G), *first_of(k), *lanes_of(1), twiddle[2], twiddle[3])

    def second_forward(values):
        return forward(values.reshape(HALF, G), *second_of(0), *lanes_of(0), twiddle[0], twiddle[1])

    def first_backward(values, k):
        return backward(values.reshape(HALF, G), *first_of(2 + k), *lanes_of(1), twiddle[2], twiddle[3])

    def second_backward(values):
        return backward(values.reshape(HALF, G), *second_of(1), *lanes_of(0), twiddle[0], twiddle[1])

    def to_cols(stage, c, source, target):
        to_all(stage, c, source, target, COLS, col_index, col_peer, at_col)

    def to_width(stage, c, source, target):
        to_all(stage, c, source, target, WIDTH, x_index, x_peer, at_x)

    waits = (
        plane_copy(0, sent1a.at[pl.ds(0, WIDTH - 1)], got1a.at[pl.ds(0, WIDTH - 1)], at_x(x_peer(1))),
        plane_copy(1, sent1b.at[pl.ds(0, COLS - 1)], got1b.at[pl.ds(0, COLS - 1)], at_col(col_peer(1))),
    )
    for load in loads[3:7]:
        load.wait()
    for wait in waits:
        wait.wait_recv()

    def step_one(c, carry):
        sent2a[c] = first_forward(got1a[:, :, c], 0).reshape(COLS, 16, G)
        to_cols(0, c, sent2a, got2a)
        sent2b[c] = second_forward(got1b[:, :, c]).reshape(WIDTH, 32, G)
        to_width(1, c, sent2b, got2b)
        return carry

    lax.fori_loop(0, 3, step_one, 0, unroll=3)

    loads[7].wait()
    near_sent[...] = jnp.zeros_like(near_sent)
    picked[...] = jnp.zeros_like(picked)
    nobody = jnp.full((3, PANELS), -1, jnp.int32)
    wanted = [
        jnp.where(jnp.full((3, PANELS), q, jnp.int32) < count[0], jnp.full((3, PANELS), target[q], jnp.int32), nobody)
        for q in range(SLOTS)
    ]

    def pick(i, charges):
        charges = list(charges)
        for k in range(GROUP):
            cluster = i * GROUP + k
            charge = density[:, pl.ds(pl.multiple_of(cluster * PANELS, PANELS), PANELS)]
            for q in range(SLOTS):
                charges[q] = jnp.where(wanted[q] == cluster, charge, charges[q])
        return tuple(charges)

    charges = lax.fori_loop(0, CLUSTERS // GROUP, pick, (jnp.zeros((3, PANELS), F32),) * SLOTS)
    for q in range(SLOTS):
        picked[q, 0:3] = charges[q]

    def slot(q, carry):
        charge = picked[q].astype(BF16)
        for b in range(3):
            total = mm(charge[0:1], blocks[q, 0, b])
            total += mm(charge[1:2], blocks[q, 1, b])
            total += mm(charge[2:3], blocks[q, 2, b])
            near_sent[q, b : b + 1] = total
        return carry

    lax.fori_loop(0, SLOTS, slot, 0)
    near_copies = []
    for side, j in ((0, ROWS - 1), (1, 1)):
        for k in range(4):
            near_copies.append(
                pltpu.make_async_remote_copy(
                    near_sent.at[4 + 2 * k + side],
                    near_got.at[2 * k + side],
                    near_sem.at[0, 2 * k + side],
                    near_sem.at[1, 2 * k + side],
                    device_id=at_row(j),
                    device_id_type=MESH,
                )
            )
    for near_copy in near_copies:
        near_copy.start()

    loads[8].wait()
    below = jnp.zeros((32 - STENCIL, PANELS), F32)

    def halve(i, carry):
        start = pl.multiple_of(i * GROUP * PANELS, GROUP * PANELS)
        for k in range(GROUP):
            block = proj[:, pl.ds(start + k * PANELS, PANELS)]
            high, low = split(jnp.concatenate([block, below], axis=0))
            proj_high[i, k * 32 : (k + 1) * 32] = high
            proj_low[i, k * 32 : (k + 1) * 32] = low
        return carry

    lax.fori_loop(0, CLUSTERS // GROUP, halve, 0)

    screens = [screen(*index) for index in wavevectors(row_index, col_index)]

    def step_two(c, carry):
        whole(0, c, sent2a, got2a).wait_recv()
        whole(1, c, sent2b, got2b).wait_recv()
        modes_a[c] = second_forward(got2a[c])
        modes_b[c] = first_forward(got2b[c], 1)
        return carry

    lax.fori_loop(0, 3, step_two, 0)

    for modes, (w1, w2, w3, inverse, weighting) in zip((modes_a, modes_b), screens):
        inner = (w1 * modes[0] + w2 * modes[1] + w3 * modes[2]) * inverse
        for c, w in enumerate((w1, w2, w3)):
            modes[c] = (modes[c] - w * inner) * weighting

    def step_three(c, carry):
        sent3a[c] = second_backward(modes_a[c]).reshape(COLS, 16, G)
        to_cols(2, c, sent3a, got3a)
        sent3b[c] = first_backward(modes_b[c], 1).reshape(WIDTH, 32, G)
        to_width(3, c, sent3b, got3b)
        return carry

    lax.fori_loop(0, 3, step_three, 0, unroll=3)

    def step_four(c, carry):
        whole(2, c, sent3a, got3a).wait_recv()
        whole(3, c, sent3b, got3b).wait_recv()
        sent4a[c] = first_backward(got3a[c], 0).reshape(WIDTH, 4, 8, G)
        to_width(4, c, sent4a, got4a)
        sent4b[c] = second_backward(got3b[c]).reshape(COLS, 2, 8, G)
        to_cols(5, c, sent4b, got4b)
        return carry

    lax.fori_loop(0, 3, step_four, 0)

    for near_copy in near_copies:
        near_copy.wait()
    near_rows[...] = jnp.zeros_like(near_rows)
    row = lax.broadcasted_iota(jnp.int32, (CLUSTERS, CLUSTERS), 0)
    lane = lax.broadcasted_iota(jnp.int32, (CLUSTERS, CLUSTERS), 1)
    lands = jnp.zeros((CLUSTERS, CLUSTERS), F32)
    for q in range(SLOTS):
        lands = jnp.where((lane == q) & (row == landing[q]), 1.0, lands)
        for b in range(3):
            arrived = near_sent[q, b : b + 1] if q < 4 else near_got[q - 4, b : b + 1]
            near_rows[q : q + 1, b * PANELS : (b + 1) * PANELS] = arrived
    lands = lands.astype(BF16)
    high, low = split(near_rows[...])
    near_term[...] = mm(lands, high) + mm(lands, low)

    points = pl.ds(0, STENCIL)
    others = pl.ds(0, DEPTH - 1)

    def sample(c, carry):
        whole(4, c, sent4a, got4a).wait_recv()
        whole(5, c, sent4b, got4b).wait_recv()

        def unpack(quad, carry):
            for j in range(4):
                pair, b = 2 * quad + j // 2, j % 2
                for high in range(2):
                    plane[4 * quad + j, 0, high] = mix2([got4a[c, 2 * high + k, pair] for k in range(2)], b)
                    plane[4 * quad + j, 0, 2 + high] = mix4([got4b[c, 4 * high + k, quad] for k in range(4)], j)
            return carry

        lax.fori_loop(0, 2, unpack, 0)

        def slab(i, carry):
            step = DEPTH - 1 - i
            zs = z_peer(distance(step))
            here = plane[step, 0].reshape(32, G)
            around = jnp.concatenate([here] + [pltpu.roll(here, G - 32 * dx, 1) for dx in (1, 2)], axis=0)
            high, low = split(around)
            both = mm(jnp.concatenate([high, low], axis=0), hot[zs])
            both = both[:96] + both[96:]
            parts = []
            for dx in range(3):
                for dy in range(3):
                    part = both[dx * 32 : dx * 32 + 32, dy * CLUSTERS : (dy + 1) * CLUSTERS]
                    for dz in range(3):
                        product = (part * phases[zs, dz]).reshape(4, 8, CLUSTERS)
                        parts.append((product[0] + product[1]) + (product[2] + product[3]))
            parts += [jnp.zeros((8, CLUSTERS), F32)] * (32 - STENCIL)
            for k in range(4):
                sent5[c, zs, 8 * k : 8 * k + 8] = row_sums(parts[8 * k : 8 * k + 8])

            @pl.when(i < DEPTH - 1)
            def _():
                copy(6, c, sent5.at[c, zs, points], got5.at[c, z_index, points], at_z(zs)).start()

            return carry

        lax.fori_loop(0, DEPTH, slab, 0, unroll=4)
        got5[c, z_index] = sent5[c, z_index]
        return carry

    lax.fori_loop(0, 3, sample, 0)

    def send_done(j, carry):
        slab_copy(j).wait_send()
        return carry

    lax.fori_loop(1, DEPTH, send_done, 0)
    for wait in waits:
        wait.wait_send()

    def finish(c, carry):
        whole(0, c, sent2a, got2a).wait_send()
        whole(1, c, sent2b, got2b).wait_send()
        whole(2, c, sent3a, got3a).wait_send()
        whole(3, c, sent3b, got3b).wait_send()
        whole(4, c, sent4a, got4a).wait_send()
        whole(5, c, sent4b, got4b).wait_send()
        copy(6, c, sent5.at[c, others, points], got5.at[c, others, points], at_row(1)).wait()
        total = jnp.sum(got5[c, :, :STENCIL], axis=0)
        total = jnp.concatenate([total, below], axis=0)
        turned = jnp.concatenate([total] * 4, axis=0).T
        both = jnp.concatenate([turned, turned], axis=1)
        both = jnp.where(own, both, jnp.zeros_like(both))
        high = both.astype(BF16).astype(F32)
        low = both - high
        for i in range(CLUSTERS // GROUP):
            at = slice(i * GROUP, (i + 1) * GROUP)
            values[i, c] = jnp.concatenate([high[at], low[at]], axis=0).astype(BF16)
        return carry

    own = (lax.broadcasted_iota(jnp.int32, (CLUSTERS, G), 0) & (GROUP - 1)) == (
        lax.broadcasted_iota(jnp.int32, (CLUSTERS, G), 1) >> 5
    )
    lax.fori_loop(0, 3, finish, 0)

    def project(i, carry):
        point_values = values[i].reshape(3 * 2 * GROUP, G)
        both = mm(point_values, proj_high[i]) + mm(point_values, proj_low[i])
        at = pl.ds(pl.multiple_of(i * GROUP, GROUP), GROUP)
        for c in range(3):
            far = both[c * 2 * GROUP : c * 2 * GROUP + GROUP] + both[c * 2 * GROUP + GROUP : (c + 1) * 2 * GROUP]
            far += near_term[at, c * PANELS : (c + 1) * PANELS]
            for k in range(GROUP):
                place = pl.multiple_of((i * GROUP + k) * PANELS, PANELS)
                out[c : c + 1, pl.ds(place, PANELS)] = far[k : k + 1]
        return carry

    lax.fori_loop(0, CLUSTERS // GROUP, project, 0, unroll=8)


VMEM = pl.BlockSpec(memory_space=pltpu.VMEM)
SMEM = pl.BlockSpec(memory_space=pltpu.SMEM)
ANY = pl.BlockSpec(memory_space=pl.ANY)
LIMIT = 60 * 1024 * 1024


def shape(dims, dtype=F32):
    return jax.ShapeDtypeStruct(dims, dtype)


def per_device(
    density, interp_weight, proj_weight, stencil_corner, near_tiles, pair_target, pair_landing, pair_count
):
    line, onward, first, second, lanes_table, twiddle = (jnp.asarray(t) for t in make_tables())
    planes_a, planes_b = pltpu.VMEM((WIDTH, 4, 3, 8, G), F32), pltpu.VMEM((COLS, 2, 3, 8, G), F32)
    by_cols, by_width = pltpu.VMEM((3, COLS, 16, G), F32), pltpu.VMEM((3, WIDTH, 32, G), F32)
    modes = pltpu.VMEM((3, HALF, G), F32)
    last_a, last_b = pltpu.VMEM((3, WIDTH, 4, 8, G), F32), pltpu.VMEM((3, COLS, 2, 8, G), F32)
    by_depth = (3, DEPTH, 32, CLUSTERS)
    held = (density, interp_weight, proj_weight, line, onward, first, second, lanes_table, twiddle, near_tiles)
    weights = pltpu.VMEM((CLUSTERS // GROUP, G, PANELS), BF16)
    return pl.pallas_call(
        whole_kernel,
        out_shape=shape((3, CLUSTERS * PANELS)),
        in_specs=[VMEM] + [SMEM] * 3 + [ANY] * 10,
        out_specs=VMEM,
        scratch_shapes=[
            *(pltpu.VMEM(array.shape[1:] if array is first else array.shape, array.dtype) for array in held),
            pltpu.VMEM((PACKED, CLUSTERS), F32),
            pltpu.VMEM((SLOTS, 8, PANELS), F32),
            pltpu.VMEM((DEPTH, PACKED, CLUSTERS), F32),
            pltpu.VMEM((DEPTH, G, 3 * CLUSTERS), BF16),
            pltpu.VMEM((DEPTH, 3, 32, CLUSTERS), F32),
            pltpu.VMEM((576, 3 * CLUSTERS), BF16),
            pltpu.VMEM((DEPTH, 3, 4, 8, G), F32),
            *(planes_a, planes_a, planes_b, planes_b),
            *(by_cols, by_cols, by_width, by_width, modes, modes),
            *(by_cols, by_cols, by_width, by_width),
            *(last_a, last_a, last_b, last_b),
            pltpu.VMEM(by_depth, F32),
            pltpu.VMEM(by_depth, F32),
            pltpu.VMEM((SLOTS, 8, PANELS), F32),
            pltpu.VMEM((8, 8, PANELS), F32),
            pltpu.VMEM((CLUSTERS, 3 * PANELS), F32),
            pltpu.VMEM((CLUSTERS, 3 * PANELS), F32),
            weights,
            weights,
            pltpu.VMEM((CLUSTERS // GROUP, 3, 2 * GROUP, G), BF16),
            pltpu.SemaphoreType.DMA((PIECES + 9,)),
            pltpu.SemaphoreType.DMA((DEPTH,)),
            pltpu.SemaphoreType.DMA((DEPTH,)),
            pltpu.SemaphoreType.DMA((2, 2)),
            pltpu.SemaphoreType.DMA((7, 3)),
            pltpu.SemaphoreType.DMA((7, 3)),
            pltpu.SemaphoreType.DMA((2, 8)),
        ],
        compiler_params=pltpu.CompilerParams(
            vmem_limit_bytes=LIMIT, collective_id=0, has_side_effects=True
        ),
    )(stencil_corner, pair_target, pair_landing, pair_count, *held)


def solution(mesh):
    flat = P(None, ("row", "col"))
    slots = P(("row", "col"))
    in_specs = (flat, flat, flat, flat, P(("row", "col"), None, None, None, None), slots, slots, slots)
    return jax.shard_map(
        per_device, mesh=mesh, in_specs=in_specs, out_specs=flat, check_vma=False
    )
```

```python
import math

import jax
import jax.numpy as jnp
import ml_dtypes
import numpy as np
from jax import lax
from jax.experimental import pallas as pl
from jax.experimental.pallas import tpu as pltpu
from jax.sharding import PartitionSpec as P

G = 256
STENCIL = 27
ROWS = 32
COLS = 8
DEPTH = 8
WIDTH = 4
PACKED = 88
USED = 83
PIECES = 4
GROUP = 8
HALF = 128
CLUSTERS = 128
PANELS = 128
SLOTS = 12
BF16 = jnp.bfloat16
F32 = jnp.float32
MESH = pl.DeviceIdType.MESH
FACTOR = 1.0 / math.sqrt(ROWS * COLS * CLUSTERS * PANELS)


def halves(table):
    table = np.asarray(table, np.float64)
    high = table.astype(np.float32).astype(ml_dtypes.bfloat16)
    low = (table - high.astype(np.float64)).astype(np.float32).astype(ml_dtypes.bfloat16)
    return np.stack([high, low])


def rotation(theta):
    cosine, sine = np.cos(theta), np.sin(theta)
    return np.array([[cosine, sine], [-sine, cosine]])


def make_tables():
    two_pi = 2 * np.pi
    bins, cells = np.arange(128), np.arange(G)
    theta = two_pi * (bins[:, None] * cells[None, :] % G) / G
    line = np.stack([np.cos(theta), -np.sin(theta)]).reshape(2, DEPTH, 4, 4, G)
    line = line.transpose(1, 2, 0, 3, 4).reshape(DEPTH, 32, G)
    line = halves(line).transpose(1, 0, 2, 3).reshape(DEPTH, 64, G)
    step = 2 * np.pi * np.arange(128).reshape(DEPTH, 4, 1, 4) / G
    onward = np.stack([np.cos(step) + np.zeros((2, 1)), np.sin(step) * np.array([[1.0], [-1.0]])], axis=1)
    onward = np.broadcast_to(onward.reshape(DEPTH, 2, 32, 1), (DEPTH, 2, 32, CLUSTERS)).astype(np.float32)
    eight = np.arange(8)
    wide = np.arange(32)
    turn8 = rotation(two_pi * (eight[:, None] * eight[None, :] % 8) / 8)
    turn32 = rotation(two_pi * (wide[:, None] * wide[None, :] % 32) / 32)
    second = np.einsum("oipc,hg,lm->pholcgim", turn8, np.eye(2), np.eye(4)).reshape(HALF, HALF)
    by_block = turn32.reshape(2, 2, 16, 2, DEPTH, WIDTH)
    first = []
    for z in range(DEPTH):
        order = [(z + d) % DEPTH for d in (0, 7, 1, 6, 2, 5, 3, 4)]
        mine = by_block[:, :, :, :, order]
        first_a = np.einsum("oihlabx,km->holkxaibm", mine.reshape(2, 2, 16, 2, 4, 2, WIDTH), np.eye(2))
        first_b = np.einsum("oihlabx,km->holkxmaib", mine.reshape(2, 2, 16, 2, 2, 4, WIDTH), np.eye(2))
        both = [t.reshape(HALF, HALF) for t in (first_a, first_b)]
        first.append(np.stack([halves(t) for t in (*both, both[0].T, both[1].T)]))
    first = np.stack(first)
    lane32 = [np.kron(np.eye(8), f(two_pi * (wide[:, None] * wide[None, :] % 32) / 32)) for f in (np.cos, np.sin)]
    lane8 = [np.kron(f(two_pi * (eight[:, None] * eight[None, :] % 8) / 8), np.eye(32)) for f in (np.cos, np.sin)]
    row = np.arange(HALF)
    lane = np.arange(G)
    part_sign = np.where(row // 4 % 2 == 0, 1.0, -1.0)[:, None]
    twist_y = two_pi * ((row // 16)[:, None] * (lane % 32)[None, :]) / G
    twist_x = two_pi * ((row // 8 * 2 + row // 2 % 2)[:, None] * (lane // 32)[None, :]) / G
    twiddle = np.stack(
        [np.cos(twist_y), part_sign * np.sin(twist_y), np.cos(twist_x), part_sign * np.sin(twist_x)]
    ).astype(np.float32)
    second = np.stack([halves(t) for t in (second, second.T)])
    lanes_table = np.stack([halves(np.concatenate(t, axis=1)) for t in (lane32, lane8)])
    return line, np.ascontiguousarray(onward), first, second, lanes_table, twiddle


def split(values):
    high = values.astype(BF16)
    return high, (values - high.astype(F32)).astype(BF16)


def mm(a, b):
    return jnp.dot(a, b, preferred_element_type=F32)


def mm_nt(a, b):
    return lax.dot_general(a, b, (((1,), (1,)), ((), ())), preferred_element_type=F32)


def swap(values):
    grouped = values.reshape(values.shape[0] // 8, 8, values.shape[1])
    return pltpu.roll(grouped, 4, 1).reshape(values.shape)


def on_rows(table_high, table_low, values):
    high, low = split(values)
    both = mm(jnp.concatenate([table_high, table_low], axis=0), high)
    return both[:HALF] + (both[HALF:] + mm(table_high, low))


def on_lanes(values, table_high, table_low, sign):
    high, low = split(values)
    both = mm(jnp.concatenate([high, low], axis=0), table_high)
    both = both[:HALF] + (both[HALF:] + mm(high, table_low))
    return both[:, :G] + sign * swap(both[:, G:])


def row_sums(tiles):
    row = lax.broadcasted_iota(jnp.int32, (8, CLUSTERS), 0)
    for step in (4, 2, 1):
        clear = (row & step) == 0
        merged = []
        for j in range(step):
            here = jnp.where(clear, tiles[j], tiles[j + step])
            there = jnp.where(clear, tiles[j + step], tiles[j])
            if step == 4:
                moved = pltpu.roll(there, 4, 0)
            else:
                moved = jnp.where(clear, pltpu.roll(there, 8 - step, 0), pltpu.roll(there, step, 0))
            merged.append(here + moved)
        tiles = merged
    return tiles[0]


def signs(direction):
    row = lax.broadcasted_iota(jnp.int32, (HALF, G), 0)
    return jnp.where((row & 4) == 0, direction, -direction).astype(F32)


def forward(values, rows_high, rows_low, lanes_high, lanes_low, cosines, sines):
    values = on_rows(rows_high, rows_low, values)
    values = values * cosines + swap(values) * sines
    return on_lanes(values, lanes_high, lanes_low, signs(1.0))


def backward(values, rows_high, rows_low, lanes_high, lanes_low, cosines, sines):
    values = on_lanes(values, lanes_high, lanes_low, signs(-1.0))
    values = values * cosines - swap(values) * sines
    return on_rows(rows_high, rows_low, values)


def wave(index):
    return jnp.where(index < G // 2, index, index - G).astype(F32)


def wavevectors(row_index, col_index):
    z_index, x_index = row_index // WIDTH, lax.rem(row_index, WIDTH)
    row = lax.broadcasted_iota(jnp.int32, (HALF, G), 0)
    lane = lax.broadcasted_iota(jnp.int32, (HALF, G), 1)
    low, above, q = (row >> 1) & 1, lane & -32, 8 * (lane & 31)
    ours = 4 * col_index + 2 * ((row >> 3) & 1) + low + above, (row >> 4) + q, 16 * z_index + 2 * x_index + (row & 1)
    theirs = 2 * (row >> 3) + low + above, 2 * x_index + (row & 1) + q, 16 * z_index + 8 + col_index + 0 * row
    return ours, theirs


def screen(m1, m2, m3):
    w1, w2, w3 = wave(m1), wave(m2), m3.astype(F32)
    squared = w1 * w1 + w2 * w2 + w3 * w3
    kept = jnp.where((m1 == G // 2) | (m2 == G // 2), 0.0, FACTOR).astype(F32)
    fold = jnp.where(m3 == 0, 1.0, 2.0).astype(F32)
    return w1, w2, w3, 1.0 / jnp.maximum(squared, 1.0), kept * fold / (squared + 0.5)


def spread(weight, density, first, sums):
    lane = lax.broadcasted_iota(jnp.int32, (STENCIL, CLUSTERS), 1)
    group = 8

    def some(i, sums):
        start = pl.multiple_of(i * group * PANELS, group * PANELS)
        block = weight[:, pl.ds(start, group * PANELS)]
        charge = density[:, pl.ds(start, group * PANELS)]
        sums = list(sums)
        for c in range(3):
            product = block * charge[c : c + 1]
            for k in range(group):
                total = jnp.sum(product[:, k * PANELS : (k + 1) * PANELS], axis=1, keepdims=True)
                sums[c] = jnp.where(lane == i * group + k, total, sums[c])
        return tuple(sums)

    groups = CLUSTERS // PIECES // group
    return lax.fori_loop(first * groups, (first + 1) * groups, some, sums, unroll=4)


def whole_kernel(
    corner, target, landing, count,
    density_in, interp_in, proj_in, line_in, onward_in, first_in, second_in, lanes_in, twiddle_in, tiles_in,
    out,
    density, interp, proj, line, onward, first, second, lanes_table, twiddle, blocks,
    packed, picked, gathered, hot, phases, upper, plane,
    sent1a, got1a, sent1b, got1b, sent2a, got2a, sent2b, got2b, modes_a, modes_b,
    sent3a, got3a, sent3b, got3b, sent4a, got4a, sent4b, got4b, sent5, got5,
    near_sent, near_got, near_rows, near_term, proj_high, proj_low, values,
    load_sem, slab_send, slab_recv, plane_sem, send_sem, recv_sem, near_sem,
):
    row_index, col_index = lax.axis_index("row"), lax.axis_index("col")
    z_index, x_index = row_index // WIDTH, lax.rem(row_index, WIDTH)
    width = CLUSTERS * PANELS // PIECES

    def piece(k):
        at = pl.ds(k * width, width)
        return pltpu.make_async_copy(interp_in.at[:, at], interp.at[:, at], load_sem.at[k])

    loads = [
        pltpu.make_async_copy(source, target_ref, load_sem.at[PIECES + k])
        for k, (source, target_ref) in enumerate(
            (
                (density_in, density),
                (line_in, line),
                (onward_in, onward),
                (first_in.at[lax.axis_index("row") // WIDTH], first),
                (second_in, second),
                (lanes_in, lanes_table),
                (twiddle_in, twiddle),
                (tiles_in, blocks),
                (proj_in, proj),
            )
        )
    ]
    loads[0].start()
    for k in range(PIECES):
        piece(k).start()

    def z_peer(j):
        return lax.rem(z_index + j, DEPTH)

    def x_peer(j):
        return lax.rem(x_index + j, WIDTH)

    def col_peer(j):
        return lax.rem(col_index + j, COLS)

    def at_z(peer):
        return (peer * WIDTH + x_index, col_index)

    def at_x(peer):
        return (z_index * WIDTH + peer, col_index)

    def at_col(peer):
        return (row_index, peer)

    def at_row(j):
        return (lax.rem(row_index + j, ROWS), col_index)

    barrier = pltpu.get_barrier_semaphore()

    def greet(device):
        pl.semaphore_signal(barrier, inc=1, device_id=device, device_id_type=MESH)

    def greet_z(j, carry):
        greet(at_z(z_peer(j)))
        return carry

    def greet_x(j, carry):
        greet(at_x(x_peer(j)))
        return carry

    def greet_col(j, carry):
        greet(at_col(col_peer(j)))
        return carry

    lax.fori_loop(1, DEPTH, greet_z, 0)
    lax.fori_loop(1, WIDTH, greet_x, 0)
    lax.fori_loop(1, COLS, greet_col, 0)
    greet(at_row(1))
    greet(at_row(ROWS - 1))
    loads[0].wait()
    sums = (jnp.zeros((STENCIL, CLUSTERS), F32),) * 3
    for k in range(PIECES):
        piece(k).wait()
        if k == 0:
            for load in loads[1:]:
                load.start()
        sums = spread(interp, density, k, sums)
    corners = corner[...]
    packed[80:PACKED] = jnp.zeros((PACKED - 80, CLUSTERS), F32)
    for c in range(3):
        packed[c * STENCIL : (c + 1) * STENCIL] = sums[c]
    packed[81:82] = ((corners[0:1] - row_index * 8) * 32 + (corners[1:2] - col_index * 32)).astype(F32)
    packed[82:83] = corners[2:3].astype(F32)
    pl.semaphore_wait(barrier, DEPTH + WIDTH + COLS - 3 + 2)

    def distance(i):
        odd = lax.rem(i, 2)
        return odd * (DEPTH - (i + 1) // 2) + (1 - odd) * (i // 2)

    def slab_copy(i):
        return pltpu.make_async_remote_copy(
            packed.at[pl.ds(0, USED)],
            gathered.at[z_index, pl.ds(0, USED)],
            slab_send.at[i],
            slab_recv.at[i],
            device_id=at_z(z_peer(DEPTH - distance(i))),
            device_id_type=MESH,
        )

    slab_copy(1).start()
    slab_copy(2).start()
    slab_copy(3).start()
    slab_copy(4).start()
    gathered[z_index] = packed[...]

    def plane_copy(kind, source, target, device):
        return pltpu.make_async_remote_copy(
            source, target, plane_sem.at[kind, 0], plane_sem.at[kind, 1], device_id=device, device_id_type=MESH
        )

    cell = lax.broadcasted_iota(jnp.int32, (G, CLUSTERS), 0).astype(F32)

    def build(zs, place):
        local, depth = gathered[zs, 81:82], gathered[zs, 82:83]
        at = jnp.where(cell == depth, 1.0, 0.0).astype(BF16)
        both = mm(line[z_index], at)
        turn = [both[:32] + both[32:]]
        for dz in range(1, 3):
            turn.append(turn[-1] * onward[z_index, 0] + swap(turn[-1]) * onward[z_index, 1])
        for dz in range(3):
            phases[zs, dz] = turn[dz]
        for dy in range(3):
            here = jnp.where(cell == local + float(dy), 1.0, 0.0).astype(BF16)
            hot[zs, :, dy * CLUSTERS : (dy + 1) * CLUSTERS] = here
        for dx in range(3):
            for c in range(3):
                for dy in range(3):
                    at = c * STENCIL + 9 * dx + 3 * dy
                    value = turn[0] * gathered[zs, at : at + 1]
                    value += turn[1] * gathered[zs, at + 1 : at + 2]
                    value += turn[2] * gathered[zs, at + 2 : at + 3]
                    high, low = split(value)
                    top = dx * 192 + c * 64
                    upper[top : top + 32, dy * CLUSTERS : (dy + 1) * CLUSTERS] = high
                    upper[top + 32 : top + 64, dy * CLUSTERS : (dy + 1) * CLUSTERS] = low
        total = mm_nt(upper[...], hot[zs])
        for c in range(3):
            sum_of = jnp.zeros((32, G), F32)
            for dx in range(3):
                top = dx * 192 + c * 64
                part = total[top : top + 32] + total[top + 32 : top + 64]
                sum_of += pltpu.roll(part, 32 * dx, 1) if dx else part
            plane[place, c] = sum_of.reshape(4, 8, G)

    tile_row = lax.broadcasted_iota(jnp.int32, (8, G), 0)

    def shifted(tile, by):
        return pltpu.roll(tile, by % 8, 0) if by % 8 else tile

    def mix2(tiles, to):
        return jnp.where((tile_row & 2) == 0, shifted(tiles[0], -2 * to), shifted(tiles[1], 2 - 2 * to))

    def mix4(tiles, to):
        mixed = shifted(tiles[0], -to)
        for j in range(1, 4):
            mixed = jnp.where((tile_row & 3) == j, shifted(tiles[j], j - to), mixed)
        return mixed

    def send_quad(quad):
        for c in range(3):
            for peer in range(WIDTH):
                for pair in range(2):
                    tiles = [plane[2 * pair + b, c, peer // 2] for b in range(2)]
                    sent1a[peer, 2 * quad + pair, c] = mix2(tiles, peer % 2)
            for peer in range(COLS):
                tiles = [plane[j, c, 2 + peer // 4] for j in range(4)]
                sent1b[peer, quad, c] = mix4(tiles, peer % 4)

        def send_a(j, carry):
            peer = x_peer(j)
            pair = pl.ds(2 * quad, 2)
            plane_copy(0, sent1a.at[peer, pair], got1a.at[x_index, pair], at_x(peer)).start()
            return carry

        def send_b(j, carry):
            peer = col_peer(j)
            plane_copy(1, sent1b.at[peer, quad], got1b.at[col_index, quad], at_col(peer)).start()
            return carry

        lax.fori_loop(1, WIDTH, send_a, 0)
        lax.fori_loop(1, COLS, send_b, 0)

    loads[1].wait()
    loads[2].wait()

    def next_slab(i, carry):
        @pl.when(i == 1)
        def _():
            slab_copy(5).start()
            slab_copy(6).start()
            slab_copy(7).start()

        @pl.when(i >= 1)
        def _():
            slab_copy(i).wait_recv()

        build(z_peer(distance(i)), lax.rem(i, 4))
        return carry

    def four_slabs(quad, carry):
        lax.fori_loop(4 * quad, 4 * quad + 4, next_slab, 0)
        send_quad(quad)
        return carry

    lax.fori_loop(0, 2, four_slabs, 0)
    got1a[x_index] = sent1a[x_index]
    got1b[col_index] = sent1b[col_index]

    def copy(stage, c, source, target, device):
        return pltpu.make_async_remote_copy(
            source,
            target,
            send_sem.at[stage, c],
            recv_sem.at[stage, c],
            device_id=device,
            device_id_type=MESH,
        )

    def to_all(stage, c, source, target, count, mine, peer_of, device_of):
        def one(j, carry):
            peer = peer_of(j)
            copy(stage, c, source.at[c, peer], target.at[c, mine], device_of(peer)).start()
            return carry

        lax.fori_loop(1, count, one, 0)
        target[c, mine] = source[c, mine]

    def whole(stage, c, source, target):
        peers = source.shape[1] - 1
        return copy(stage, c, source.at[c, pl.ds(0, peers)], target.at[c, pl.ds(0, peers)], at_row(1))

    def first_of(k):
        return first[k, 0], first[k, 1]

    def second_of(k):
        return second[k, 0], second[k, 1]

    def lanes_of(k):
        return lanes_table[k, 0], lanes_table[k, 1]

    def first_forward(values, k):
        return forward(values.reshape(HALF, G), *first_of(k), *lanes_of(1), twiddle[2], twiddle[3])

    def second_forward(values):
        return forward(values.reshape(HALF, G), *second_of(0), *lanes_of(0), twiddle[0], twiddle[1])

    def first_backward(values, k):
        return backward(values.reshape(HALF, G), *first_of(2 + k), *lanes_of(1), twiddle[2], twiddle[3])

    def second_backward(values):
        return backward(values.reshape(HALF, G), *second_of(1), *lanes_of(0), twiddle[0], twiddle[1])

    def to_cols(stage, c, source, target):
        to_all(stage, c, source, target, COLS, col_index, col_peer, at_col)

    def to_width(stage, c, source, target):
        to_all(stage, c, source, target, WIDTH, x_index, x_peer, at_x)

    waits = (
        plane_copy(0, sent1a.at[pl.ds(0, WIDTH - 1)], got1a.at[pl.ds(0, WIDTH - 1)], at_x(x_peer(1))),
        plane_copy(1, sent1b.at[pl.ds(0, COLS - 1)], got1b.at[pl.ds(0, COLS - 1)], at_col(col_peer(1))),
    )
    for load in loads[3:7]:
        load.wait()
    for wait in waits:
        wait.wait_recv()

    def step_one(c, carry):
        sent2a[c] = first_forward(got1a[:, :, c], 0).reshape(COLS, 16, G)
        to_cols(0, c, sent2a, got2a)
        sent2b[c] = second_forward(got1b[:, :, c]).reshape(WIDTH, 32, G)
        to_width(1, c, sent2b, got2b)
        return carry

    lax.fori_loop(0, 3, step_one, 0, unroll=3)

    loads[7].wait()
    near_sent[...] = jnp.zeros_like(near_sent)
    picked[...] = jnp.zeros_like(picked)
    nobody = jnp.full((3, PANELS), -1, jnp.int32)
    wanted = [
        jnp.where(jnp.full((3, PANELS), q, jnp.int32) < count[0], jnp.full((3, PANELS), target[q], jnp.int32), nobody)
        for q in range(SLOTS)
    ]

    def pick(i, charges):
        charges = list(charges)
        for k in range(GROUP):
            cluster = i * GROUP + k
            charge = density[:, pl.ds(pl.multiple_of(cluster * PANELS, PANELS), PANELS)]
            for q in range(SLOTS):
                charges[q] = jnp.where(wanted[q] == cluster, charge, charges[q])
        return tuple(charges)

    charges = lax.fori_loop(0, CLUSTERS // GROUP, pick, (jnp.zeros((3, PANELS), F32),) * SLOTS)
    for q in range(SLOTS):
        picked[q, 0:3] = charges[q]

    def slot(q, carry):
        charge = picked[q].astype(BF16)
        for b in range(3):
            total = mm(charge[0:1], blocks[q, 0, b])
            total += mm(charge[1:2], blocks[q, 1, b])
            total += mm(charge[2:3], blocks[q, 2, b])
            near_sent[q, b : b + 1] = total
        return carry

    lax.fori_loop(0, SLOTS, slot, 0)
    near_copies = []
    for side, j in ((0, ROWS - 1), (1, 1)):
        for k in range(4):
            near_copies.append(
                pltpu.make_async_remote_copy(
                    near_sent.at[4 + 2 * k + side],
                    near_got.at[2 * k + side],
                    near_sem.at[0, 2 * k + side],
                    near_sem.at[1, 2 * k + side],
                    device_id=at_row(j),
                    device_id_type=MESH,
                )
            )
    for near_copy in near_copies:
        near_copy.start()

    loads[8].wait()
    below = jnp.zeros((32 - STENCIL, PANELS), F32)

    def halve(i, carry):
        start = pl.multiple_of(i * GROUP * PANELS, GROUP * PANELS)
        for k in range(GROUP):
            block = proj[:, pl.ds(start + k * PANELS, PANELS)]
            high, low = split(jnp.concatenate([block, below], axis=0))
            proj_high[i, k * 32 : (k + 1) * 32] = high
            proj_low[i, k * 32 : (k + 1) * 32] = low
        return carry

    lax.fori_loop(0, CLUSTERS // GROUP, halve, 0)

    screens = [screen(*index) for index in wavevectors(row_index, col_index)]

    def step_two(c, carry):
        whole(0, c, sent2a, got2a).wait_recv()
        whole(1, c, sent2b, got2b).wait_recv()
        modes_a[c] = second_forward(got2a[c])
        modes_b[c] = first_forward(got2b[c], 1)
        return carry

    lax.fori_loop(0, 3, step_two, 0)

    for modes, (w1, w2, w3, inverse, weighting) in zip((modes_a, modes_b), screens):
        inner = (w1 * modes[0] + w2 * modes[1] + w3 * modes[2]) * inverse
        for c, w in enumerate((w1, w2, w3)):
            modes[c] = (modes[c] - w * inner) * weighting

    def step_three(c, carry):
        sent3a[c] = second_backward(modes_a[c]).reshape(COLS, 16, G)
        to_cols(2, c, sent3a, got3a)
        sent3b[c] = first_backward(modes_b[c], 1).reshape(WIDTH, 32, G)
        to_width(3, c, sent3b, got3b)
        return carry

    lax.fori_loop(0, 3, step_three, 0, unroll=3)

    for near_copy in near_copies:
        near_copy.wait()
    near_rows[...] = jnp.zeros_like(near_rows)
    row = lax.broadcasted_iota(jnp.int32, (CLUSTERS, CLUSTERS), 0)
    lane = lax.broadcasted_iota(jnp.int32, (CLUSTERS, CLUSTERS), 1)
    lands = jnp.zeros((CLUSTERS, CLUSTERS), F32)
    for q in range(SLOTS):
        lands = jnp.where((lane == q) & (row == landing[q]), 1.0, lands)
        for b in range(3):
            arrived = near_sent[q, b : b + 1] if q < 4 else near_got[q - 4, b : b + 1]
            near_rows[q : q + 1, b * PANELS : (b + 1) * PANELS] = arrived
    lands = lands.astype(BF16)
    high, low = split(near_rows[...])
    near_term[...] = mm(lands, high) + mm(lands, low)

    def step_four(c, carry):
        whole(2, c, sent3a, got3a).wait_recv()
        whole(3, c, sent3b, got3b).wait_recv()
        sent4a[c] = first_backward(got3a[c], 0).reshape(WIDTH, 4, 8, G)
        to_width(4, c, sent4a, got4a)
        sent4b[c] = second_backward(got3b[c]).reshape(COLS, 2, 8, G)
        to_cols(5, c, sent4b, got4b)
        return carry

    lax.fori_loop(0, 3, step_four, 0)


    points = pl.ds(0, STENCIL)
    others = pl.ds(0, DEPTH - 1)

    def sample(c, carry):
        whole(4, c, sent4a, got4a).wait_recv()
        whole(5, c, sent4b, got4b).wait_recv()

        def unpack(quad, carry):
            for j in range(4):
                pair, b = 2 * quad + j // 2, j % 2
                for high in range(2):
                    plane[4 * quad + j, 0, high] = mix2([got4a[c, 2 * high + k, pair] for k in range(2)], b)
                    plane[4 * quad + j, 0, 2 + high] = mix4([got4b[c, 4 * high + k, quad] for k in range(4)], j)
            return carry

        lax.fori_loop(0, 2, unpack, 0)

        def slab(i, carry):
            step = DEPTH - 1 - i
            zs = z_peer(distance(step))
            here = plane[step, 0].reshape(32, G)
            around = jnp.concatenate([here] + [pltpu.roll(here, G - 32 * dx, 1) for dx in (1, 2)], axis=0)
            high, low = split(around)
            both = mm(jnp.concatenate([high, low], axis=0), hot[zs])
            both = both[:96] + both[96:]
            parts = []
            for dx in range(3):
                for dy in range(3):
                    part = both[dx * 32 : dx * 32 + 32, dy * CLUSTERS : (dy + 1) * CLUSTERS]
                    for dz in range(3):
                        product = (part * phases[zs, dz]).reshape(4, 8, CLUSTERS)
                        parts.append((product[0] + product[1]) + (product[2] + product[3]))
            parts += [jnp.zeros((8, CLUSTERS), F32)] * (32 - STENCIL)
            for k in range(4):
                sent5[c, zs, 8 * k : 8 * k + 8] = row_sums(parts[8 * k : 8 * k + 8])

            @pl.when(i < DEPTH - 1)
            def _():
                copy(6, c, sent5.at[c, zs, points], got5.at[c, z_index, points], at_z(zs)).start()

            return carry

        lax.fori_loop(0, DEPTH, slab, 0, unroll=4)
        got5[c, z_index] = sent5[c, z_index]
        return carry

    lax.fori_loop(0, 3, sample, 0)

    def send_done(j, carry):
        slab_copy(j).wait_send()
        return carry

    lax.fori_loop(1, DEPTH, send_done, 0)
    for wait in waits:
        wait.wait_send()

    def finish(c, carry):
        whole(0, c, sent2a, got2a).wait_send()
        whole(1, c, sent2b, got2b).wait_send()
        whole(2, c, sent3a, got3a).wait_send()
        whole(3, c, sent3b, got3b).wait_send()
        whole(4, c, sent4a, got4a).wait_send()
        whole(5, c, sent4b, got4b).wait_send()
        copy(6, c, sent5.at[c, others, points], got5.at[c, others, points], at_row(1)).wait()
        total = jnp.sum(got5[c, :, :STENCIL], axis=0)
        total = jnp.concatenate([total, below], axis=0)
        turned = jnp.concatenate([total] * 4, axis=0).T
        both = jnp.concatenate([turned, turned], axis=1)
        both = jnp.where(own, both, jnp.zeros_like(both))
        high = both.astype(BF16).astype(F32)
        low = both - high
        for i in range(CLUSTERS // GROUP):
            at = slice(i * GROUP, (i + 1) * GROUP)
            values[i, c] = jnp.concatenate([high[at], low[at]], axis=0).astype(BF16)
        return carry

    own = (lax.broadcasted_iota(jnp.int32, (CLUSTERS, G), 0) & (GROUP - 1)) == (
        lax.broadcasted_iota(jnp.int32, (CLUSTERS, G), 1) >> 5
    )
    lax.fori_loop(0, 3, finish, 0)

    def project(i, carry):
        point_values = values[i].reshape(3 * 2 * GROUP, G)
        both = mm(point_values, proj_high[i]) + mm(point_values, proj_low[i])
        at = pl.ds(pl.multiple_of(i * GROUP, GROUP), GROUP)
        for c in range(3):
            far = both[c * 2 * GROUP : c * 2 * GROUP + GROUP] + both[c * 2 * GROUP + GROUP : (c + 1) * 2 * GROUP]
            far += near_term[at, c * PANELS : (c + 1) * PANELS]
            for k in range(GROUP):
                place = pl.multiple_of((i * GROUP + k) * PANELS, PANELS)
                out[c : c + 1, pl.ds(place, PANELS)] = far[k : k + 1]
        return carry

    lax.fori_loop(0, CLUSTERS // GROUP, project, 0, unroll=8)


VMEM = pl.BlockSpec(memory_space=pltpu.VMEM)
SMEM = pl.BlockSpec(memory_space=pltpu.SMEM)
ANY = pl.BlockSpec(memory_space=pl.ANY)
LIMIT = 60 * 1024 * 1024


def shape(dims, dtype=F32):
    return jax.ShapeDtypeStruct(dims, dtype)


def per_device(
    density, interp_weight, proj_weight, stencil_corner, near_tiles, pair_target, pair_landing, pair_count
):
    line, onward, first, second, lanes_table, twiddle = (jnp.asarray(t) for t in make_tables())
    planes_a, planes_b = pltpu.VMEM((WIDTH, 4, 3, 8, G), F32), pltpu.VMEM((COLS, 2, 3, 8, G), F32)
    by_cols, by_width = pltpu.VMEM((3, COLS, 16, G), F32), pltpu.VMEM((3, WIDTH, 32, G), F32)
    modes = pltpu.VMEM((3, HALF, G), F32)
    last_a, last_b = pltpu.VMEM((3, WIDTH, 4, 8, G), F32), pltpu.VMEM((3, COLS, 2, 8, G), F32)
    by_depth = (3, DEPTH, 32, CLUSTERS)
    held = (density, interp_weight, proj_weight, line, onward, first, second, lanes_table, twiddle, near_tiles)
    weights = pltpu.VMEM((CLUSTERS // GROUP, G, PANELS), BF16)
    return pl.pallas_call(
        whole_kernel,
        out_shape=shape((3, CLUSTERS * PANELS)),
        in_specs=[VMEM] + [SMEM] * 3 + [ANY] * 10,
        out_specs=VMEM,
        scratch_shapes=[
            *(pltpu.VMEM(array.shape[1:] if array is first else array.shape, array.dtype) for array in held),
            pltpu.VMEM((PACKED, CLUSTERS), F32),
            pltpu.VMEM((SLOTS, 8, PANELS), F32),
            pltpu.VMEM((DEPTH, PACKED, CLUSTERS), F32),
            pltpu.VMEM((DEPTH, G, 3 * CLUSTERS), BF16),
            pltpu.VMEM((DEPTH, 3, 32, CLUSTERS), F32),
            pltpu.VMEM((576, 3 * CLUSTERS), BF16),
            pltpu.VMEM((DEPTH, 3, 4, 8, G), F32),
            *(planes_a, planes_a, planes_b, planes_b),
            *(by_cols, by_cols, by_width, by_width, modes, modes),
            *(by_cols, by_cols, by_width, by_width),
            *(last_a, last_a, last_b, last_b),
            pltpu.VMEM(by_depth, F32),
            pltpu.VMEM(by_depth, F32),
            pltpu.VMEM((SLOTS, 8, PANELS), F32),
            pltpu.VMEM((8, 8, PANELS), F32),
            pltpu.VMEM((CLUSTERS, 3 * PANELS), F32),
            pltpu.VMEM((CLUSTERS, 3 * PANELS), F32),
            weights,
            weights,
            pltpu.VMEM((CLUSTERS // GROUP, 3, 2 * GROUP, G), BF16),
            pltpu.SemaphoreType.DMA((PIECES + 9,)),
            pltpu.SemaphoreType.DMA((DEPTH,)),
            pltpu.SemaphoreType.DMA((DEPTH,)),
            pltpu.SemaphoreType.DMA((2, 2)),
            pltpu.SemaphoreType.DMA((7, 3)),
            pltpu.SemaphoreType.DMA((7, 3)),
            pltpu.SemaphoreType.DMA((2, 8)),
        ],
        compiler_params=pltpu.CompilerParams(
            vmem_limit_bytes=LIMIT, collective_id=0, has_side_effects=True
        ),
    )(stencil_corner, pair_target, pair_landing, pair_count, *held)


def solution(mesh):
    flat = P(None, ("row", "col"))
    slots = P(("row", "col"))
    in_specs = (flat, flat, flat, flat, P(("row", "col"), None, None, None, None), slots, slots, slots)
    return jax.shard_map(
        per_device, mesh=mesh, in_specs=in_specs, out_specs=flat, check_vma=False
    )
```
